256 devices in a mesh: gx: 8 (over y, x_lo), gy: 4 (over x_hi, core), gz: 8 (over z).
Axes of the slice: x: 4 (x_hi: 2, x_lo: 2; x = x_hi * 2 + x_lo), y: 4, z: 8, core: 2. Of those that a mesh axis runs over, the one named last changes fastest.
Arguments:
- positions: float32 [3, 32, 16, 16, 16], P(None, 'gx', 'gy', 'gz'), may hold values from 0 to 5
- occupancy: int32 [32, 16, 16], P('gx', 'gy', 'gz'), may hold values from 1 to 16
- neighbours: int32 [32, 16, 16, 16, 64], P('gx', 'gy', 'gz'), may hold values from 0 to 431
- edge_counts: int32 [32, 16, 16, 16], P('gx', 'gy', 'gz'), may hold values from 1 to 64
- atom_features: bfloat16 [32, 16, 16, 16, 128], P('gx', 'gy', 'gz'), may hold values from -6 to 6
- w_atom: bfloat16 [128, 128], replicated, may hold values from -0.5 to 0.5
- w_radial: bfloat16 [8, 128], replicated, may hold values from -2 to 2
- w_hidden: bfloat16 [128, 128], replicated, may hold values from -0.5 to 0.5
- w_tensor: bfloat16 [128, 32], replicated, may hold values from -0.5 to 0.5
- w_mix: bfloat16 [224, 128], replicated, may hold values from -0.375 to 0.375
- w_out: float32 [128], replicated, may hold values from -0.5 to 0.5
Outputs:
- atom_energy: float32 [32, 16, 16, 16], P('gx', 'gy', 'gz')
- forces: float32 [3, 32, 16, 16, 16], P(None, 'gx', 'gy', 'gz')
The draws below stay inside these ranges and needn't reach their ends.
Inputs may be any that keep to these rules, and one draw needn't show every extreme that they name: `neighbours`: code 16 * 13 + s names the atom itself; other codes name the 26 neighbouring cell bins.
All inputs are finite; a program needn't handle non-finite values.
Results may differ from the reference program's by a relative error of at most 0.0075.
Values may be sent and summed in bfloat16 or wider, within the bound.
A program may use at most 128 MiB of HBM per device.

```python
import math
import jax
import jax.numpy as jnp
from jax import lax

S = 16
K = 64
LAT = 128
TF = 32
NB = 8
FEAT = 128
NX = 32
NY = 16
NZ = 16


def plant(entries, own_key, smallest, high):
    spot = [jax.random.randint(jax.random.fold_in(own_key, axis), (), 0, length) for axis, length in enumerate(entries.shape)]
    longest = entries.shape.index(max(entries.shape))
    neighbour = spot[:longest] + [(spot[longest] + 1) % entries.shape[longest]] + spot[longest + 1:]
    return entries.at[tuple(spot)].set(smallest).at[tuple(neighbour)].set(high)


def steps_of(own_key, shape, pieces, smallest, high):
    def one(position, parts):
        steps = jax.random.uniform(jax.random.fold_in(jax.random.fold_in(own_key, 6), position), (parts,), jnp.float32, smallest / len(pieces), high / len(pieces))
        return jnp.repeat(jnp.exp(steps), shape[position] // parts).reshape((-1,) + (1,) * (len(shape) - position - 1))

    factor_of = one(*pieces[0])
    for cut in pieces[1:]:
        factor_of = factor_of * one(*cut)
    return factor_of


def normal_values(rng, dims, scale, limit, split=(), held_as=jnp.bfloat16):
    level = steps_of(rng, dims, split, -0.22, 0.18) if split else 1.0
    drawn = jax.random.normal(rng, dims, jnp.float32) * scale * level
    return jnp.minimum(jnp.maximum(drawn, -limit), limit).astype(held_as)


def setup_inputs(seed: int = 0) -> dict:
    key_list = jax.random.split(jax.random.key(seed), 12)
    return {
        "positions": jnp.clip(5.0 * jax.random.uniform(key_list[0], (3, NX, NY, NZ, S), jnp.float32) ** steps_of(key_list[0], (3, NX, NY, NZ, S), ((1, 8), (2, 4), (3, 8)), -0.2, 0.2), 0.0, 5.0),
        "occupancy": plant(jax.random.randint(key_list[1], (NX, NY, NZ), 1, S + 1), jax.random.fold_in(key_list[1], 1), 1, S).astype(jnp.int32),
        "neighbours": plant(jax.random.randint(key_list[2], (NX, NY, NZ, S, K), 0, 27 * S), jax.random.fold_in(key_list[2], 1), 0, (27 * S) - 1).astype(jnp.int32),
        "edge_counts": plant(jax.random.randint(key_list[3], (NX, NY, NZ, S), 1, K + 1), jax.random.fold_in(key_list[3], 1), 1, K).astype(jnp.int32),
        "atom_features": normal_values(key_list[4], (NX, NY, NZ, S, FEAT), 1.0, 6.0, ((0, 8), (1, 4), (2, 8))),
        "w_atom": normal_values(key_list[5], (FEAT, LAT), FEAT ** -0.5, 0.5),
        "w_radial": normal_values(key_list[6], (NB, LAT), NB ** -0.5, 2.0),
        "w_hidden": normal_values(key_list[7], (LAT, LAT), LAT ** -0.5, 0.5),
        "w_tensor": normal_values(key_list[8], (LAT, TF), LAT ** -0.5, 0.5),
        "w_mix": normal_values(key_list[9], (LAT + 3 * TF, LAT), (LAT + 3 * TF) ** -0.5, 0.375),
        "w_out": normal_values(key_list[10], (LAT,), LAT ** -0.5, 0.5, (), jnp.float32),
    }


cell_length = 5.0
env_scale = 0.125
root_three = 1.7320508075688772
cutoff_square = 144.0

def harmonics(unit_x, unit_y, unit_z):
    ones = jnp.ones_like(unit_x)
    return jnp.stack([ones, unit_x, unit_y, unit_z, root_three * unit_x * unit_y, root_three * unit_y * unit_z, 0.5 * (3.0 * unit_z * unit_z - 1.0), root_three * unit_x * unit_z, 0.5 * root_three * (unit_x * unit_x - unit_y * unit_y)], axis=-1)

def edge_energy(relative, edge_mask, proj_centre, proj_other, weights):
    w_radial, w_hidden, w_tensor, w_mix, w_out = weights
    rows, fan_count = edge_mask.shape
    dist_square = relative[0] * relative[0] + relative[1] * relative[1] + relative[2] * relative[2] + 0.01
    distance = jnp.sqrt(dist_square)
    unit_x = relative[0] / distance
    unit_y = relative[1] / distance
    unit_z = relative[2] / distance
    envelope = jnp.square(jnp.maximum(1.0 - dist_square / cutoff_square, 0.0))
    weighting = edge_mask * envelope
    nbasis = w_radial.shape[0]
    centres = 0.5 + 2.0 * jnp.arange(nbasis).astype(jnp.float32)
    basis = jnp.exp(-jnp.square((distance[..., None] - centres) * 0.5))
    radial = jnp.dot(basis.reshape(rows * fan_count, nbasis).astype(jnp.bfloat16), w_radial, preferred_element_type=jnp.float32)
    latent = radial.shape[-1]
    pre_act = radial.reshape(rows, fan_count, latent) + proj_centre[:, None, :].astype(jnp.float32) + proj_other.astype(jnp.float32)
    first_hidden = jax.nn.silu(pre_act).astype(jnp.bfloat16).reshape(rows * fan_count, latent)
    second = jax.nn.silu(jnp.dot(first_hidden, w_hidden, preferred_element_type=jnp.float32)).astype(jnp.bfloat16)
    tensor_w = jnp.dot(second, w_tensor, preferred_element_type=jnp.float32).reshape(rows, fan_count, -1)
    sphere = harmonics(unit_x, unit_y, unit_z)
    environ = env_scale * jnp.einsum('bkc,bkm->bcm', tensor_w * weighting[..., None], sphere)
    group_of = jnp.array([0, 1, 1, 1, 2, 2, 2, 2, 2], dtype=jnp.int32)
    groups = (group_of[:, None] == jnp.arange(3, dtype=jnp.int32)[None, :]).astype(jnp.float32)
    invariant = jnp.einsum('bcm,bkm,ml->bkcl', environ, sphere, groups).reshape(rows * fan_count, -1)
    joined = jnp.concatenate([second, invariant.astype(jnp.bfloat16)], axis=1)
    mixed = jax.nn.silu(jnp.dot(joined, w_mix, preferred_element_type=jnp.float32))
    per_edge = lax.optimization_barrier(jnp.sum(mixed * w_out, axis=1)).reshape(rows, fan_count)
    return lax.optimization_barrier(jnp.sum(per_edge * weighting, axis=1))

def local_forces(atom_table, features, occupancy, neighbours, edge_counts, w_atom, weights):
    ext_x, ext_y, ext_z, slots = (atom_table.shape[1], atom_table.shape[2], atom_table.shape[3], atom_table.shape[4])
    cells_x, cells_y, cells_z = (ext_x - 2, ext_y - 2, ext_z - 2)
    fan_count = neighbours.shape[-1]
    shape_four = (cells_x, cells_y, cells_z, slots)
    pos_x = lax.broadcasted_iota(jnp.int32, shape_four, 0) + 1
    pos_y = lax.broadcasted_iota(jnp.int32, shape_four, 1) + 1
    pos_z = lax.broadcasted_iota(jnp.int32, shape_four, 2) + 1
    slot_of = lax.broadcasted_iota(jnp.int32, shape_four, 3)
    centre_flat = ((pos_x * ext_y + pos_y) * ext_z + pos_z) * slots + slot_of
    offset_code = neighbours // slots
    slot_other = neighbours % slots
    step_x = offset_code // 9 - 1
    step_y = offset_code // 3 % 3 - 1
    step_z = offset_code % 3 - 1
    other_flat = (((pos_x[..., None] + step_x) * ext_y + pos_y[..., None] + step_y) * ext_z + pos_z[..., None] + step_z) * slots + slot_other
    centre_count = cells_x * cells_y * cells_z * slots
    flat_table = atom_table.reshape(4, -1)
    other = jnp.take(flat_table, other_flat.reshape(-1), axis=1).reshape(4, centre_count, fan_count)
    centre = jnp.take(flat_table, centre_flat.reshape(-1), axis=1)
    shifts = jnp.stack([step_x, step_y, step_z]).reshape(3, centre_count, fan_count).astype(jnp.float32) * cell_length
    relative = other[:3] + shifts - centre[:3, :, None]
    own_edge = (offset_code == 13) & (slot_other == slot_of[..., None])
    edge_rank = lax.broadcasted_iota(jnp.int32, neighbours.shape, 4)
    live_centre = slot_of < occupancy[..., None]
    keep_edge = (edge_rank < edge_counts[..., None]) & live_centre[..., None] & jnp.logical_not(own_edge)
    edge_mask = (keep_edge.reshape(centre_count, fan_count) & (other[3] > 0.5)).astype(jnp.float32)
    projected = jnp.dot(features.reshape(-1, features.shape[-1]), w_atom, preferred_element_type=jnp.float32).astype(jnp.bfloat16)
    block_size = math.gcd(centre_count, 128)
    blocks = centre_count // block_size

    def one_block(block_data):
        rel_block, mask_block, other_block, centre_block = block_data
        proj_other = jnp.take(projected, other_block.reshape(-1), axis=0).reshape(block_size, fan_count, -1)
        proj_centre = jnp.take(projected, centre_block, axis=0)
        energy, pullback = jax.vjp(lambda shifted_rel: edge_energy(shifted_rel, mask_block, proj_centre, proj_other, weights), rel_block)
        gradient, = pullback(jnp.ones_like(energy))
        return (energy, gradient)
    energy, gradient = lax.map(one_block, (relative.reshape(3, blocks, block_size, fan_count).transpose(1, 0, 2, 3), edge_mask.reshape(blocks, block_size, fan_count), other_flat.reshape(blocks, block_size, fan_count), centre_flat.reshape(blocks, block_size)))
    gradient = gradient.transpose(1, 0, 2, 3).reshape(3, centre_count, fan_count)
    values = jnp.concatenate([-gradient.reshape(3, -1), lax.optimization_barrier(jnp.sum(gradient, axis=2))], axis=1)
    indexer = jnp.concatenate([other_flat.reshape(-1), centre_flat.reshape(-1)])
    force_grid = jax.ops.segment_sum(values.T, indexer, num_segments=flat_table.shape[1])
    force_grid = force_grid.T.reshape(3, ext_x, ext_y, ext_z, slots)
    return (energy.reshape(shape_four), force_grid)

def fold_rim(force_grid, axis_dim, sender):
    length = force_grid.shape[axis_dim]
    lower_rim = lax.slice_in_dim(force_grid, 0, 1, axis=axis_dim)
    upper_rim = lax.slice_in_dim(force_grid, length - 1, length, axis=axis_dim)
    interior = lax.slice_in_dim(force_grid, 1, length - 1, axis=axis_dim)
    from_above = sender(lower_rim, -1)
    from_below = sender(upper_rim, 1)
    indexer = [slice(None)] * force_grid.ndim
    indexer[axis_dim] = slice(length - 3, length - 2)
    interior = interior.at[tuple(indexer)].add(from_above)
    indexer[axis_dim] = slice(0, 1)
    return interior.at[tuple(indexer)].add(from_below)

def keep_slab(piece_slab, direction):
    return piece_slab

def reference(positions, occupancy, neighbours, edge_counts, atom_features, w_atom, w_radial, w_hidden, w_tensor, w_mix, w_out):
    slots = positions.shape[-1]
    alive_slot = (lax.broadcasted_iota(jnp.int32, occupancy.shape + (slots,), 3) < occupancy[..., None]).astype(jnp.float32)
    atom_table = jnp.concatenate([positions, alive_slot[None]], axis=0)
    atom_table = jnp.pad(atom_table, ((0, 0), (1, 1), (1, 1), (1, 1), (0, 0)), mode='wrap')
    features = jnp.pad(atom_features, ((1, 1), (1, 1), (1, 1), (0, 0), (0, 0)), mode='wrap')
    energy, force_grid = local_forces(atom_table, features, occupancy, neighbours, edge_counts, w_atom, (w_radial, w_hidden, w_tensor, w_mix, w_out))
    for axis_dim in (1, 2, 3):
        force_grid = fold_rim(force_grid, axis_dim, keep_slab)
    return (energy, force_grid)
```

```python
import numpy as np
import jax
import jax.numpy as jnp
from jax import lax
from jax.experimental import pallas as pl
from jax.experimental.pallas import tpu as pltpu
from jax.sharding import PartitionSpec as P

F32 = jnp.float32
BF = jnp.bfloat16
root_three = 1.7320508075688772
L = 256
G = 2
CX, CY, CZ = 4, 4, 2
CELLS = 32
MAXCH = CELLS * (1024 // L) + G


def nn(a, b):
    return lax.dot_general(a, b, (((1,), (0,)), ((), ())), preferred_element_type=F32)


def nt(a, b):
    return lax.dot_general(a, b, (((1,), (1,)), ((), ())), preferred_element_type=F32)


def iota(shape, dim, dtype=jnp.int32):
    return lax.broadcasted_iota(jnp.int32, shape, dim).astype(dtype)


def onoff(mask):
    return jnp.where(mask, 1.0, 0.0).astype(F32)


def eye(n, m):
    return onoff(iota((n, m), 0) == iota((n, m), 1)).astype(BF)


def silu_both(x):
    sg = 0.5 * jnp.tanh(0.5 * x) + 0.5
    y = x * sg
    return y, sg + y - y * sg


def edge_kernel(
    occ_s, feats, rows, neigh, counts, w_atom, w_rad, w_hid, w_ten, w_mix, w_out, fold,
    energy_out, force_out,
    list_c, list_r, rank_sc, att_sc, rt_sc, ctr_sc, w_atomT, w_hidT, w_mixT, w_radpad, w_radrow, wout_b, c_sc,
    q_sc, dm_sc, m_sc, dq_sc, f_sc, en_sc, sec_sc, d1_sc, d2_sc, g_sc, ys_sc, geo_sc, eps_sc,
):
    ident = eye(128, 128)
    w_atomT[...] = nt(ident, w_atom[...]).astype(BF)
    w_hidT[...] = nt(ident, w_hid[...]).astype(BF)
    w_mixT[...] = nt(ident, w_mix[0:128, :]).astype(BF)
    w_radrow[...] = jnp.zeros((128, 128), BF)
    w_radrow[48:64, :] = jnp.concatenate([w_rad[...].astype(F32), jnp.zeros((8, 128), F32)], axis=0).astype(BF)
    w_radpad[...] = nt(ident, w_radrow[...])
    wout_b[...] = jnp.sum(
        jnp.where(iota((128, 128), 0) == iota((128, 128), 1), w_out[...], 0.0), axis=1, keepdims=True
    ) * jnp.ones((128, 128), F32)
    tail = w_mix[128:224, :]
    for l in range(3):
        sel = onoff(iota((32, 96), 1) == 3 * iota((32, 96), 0) + l).astype(BF)
        spread = nn(w_ten[...], sel).astype(BF)
        c_sc[l] = (0.125 * nn(spread, tail)).astype(BF)

    counts_t = nt(eye(16, 16), counts[...].astype(F32).astype(BF))
    lane64 = iota((8, 128), 1)
    low = lane64 < 64
    k_of = jnp.where(low, lane64, lane64 - 64)
    s_of = jnp.where(low, iota((8, 128), 0), iota((8, 128), 0) + 8)
    masks = []
    for c in range(CELLS):
        x, y, z = c // (CY * CZ), c // CZ % CY, c % CZ
        nb = jnp.concatenate([neigh[c, 0:8, :], neigh[c, 8:16, :]], axis=1)
        cnt = jnp.where(low, counts_t[0:8, c : c + 1], counts_t[8:16, c : c + 1]).astype(jnp.int32)
        code = lax.shift_right_logical(nb, 4)
        slot = lax.bitwise_and(nb, 15)
        occ_n = jnp.zeros((8, 128), jnp.int32)
        for k in range(27):
            at = ((x + k // 9) * 6 + y + k // 3 % 3) * 4 + z + k % 3
            occ_n = jnp.where(code == k, occ_s[at], occ_n)
        own = occ_s[((x + 1) * 6 + y + 1) * 4 + z + 1]
        live = (k_of < cnt) & (slot < occ_n) & (s_of < own) & (nb != 208 + s_of)
        masks.append(onoff(live))
        sub = iota((16, 128), 0)
        code_f, slot_f, s_f = code.astype(F32), slot.astype(F32), s_of.astype(F32)
        for i in range(8):
            a = jnp.where(
                sub == 0,
                code_f[i : i + 1],
                jnp.where(sub == 1, slot_f[i : i + 1], jnp.where(sub == 2, s_f[i : i + 1], jnp.where(sub == 3, 1.0, 0.0))),
            )
            att_sc[c, :, i * 128 : (i + 1) * 128] = a.astype(BF)
    mask = jnp.concatenate(masks, axis=0)
    mask_b = mask.astype(BF)
    upto = nn(mask_b, onoff(iota((128, 128), 0) <= iota((128, 128), 1)).astype(BF))
    total = nn(mask_b, jnp.ones((128, 128), BF))
    ri, ci = iota((256, 256), 0), iota((256, 256), 1)
    before = onoff((lax.shift_right_logical(ri, 3) == lax.shift_right_logical(ci, 3)) & (ci < ri)).astype(BF)
    base = nn(before, total.astype(BF))
    rank_sc[...] = jnp.where(mask > 0.5, upto - 1.0 + base, -1.0).astype(jnp.int32).reshape(CELLS, 8, 128)
    ends = base + total
    pos = jnp.int32(0)
    for c in range(CELLS):
        n_c = jnp.max(ends[8 * c + 7 : 8 * c + 8, :]).astype(jnp.int32)
        chunks = lax.div(n_c + (L - 1), L)

        def put(k, _, pos=pos, c=c):
            list_c[pos + k] = c
            list_r[pos + k] = k * L
            return 0

        lax.fori_loop(0, chunks, put, 0)
        pos = pos + chunks
    for i in range(G):
        list_c[pos + i] = 0
        list_r[pos + i] = 4096
    groups = lax.div(pos + (G - 1), G)

    lane = iota((32, 128), 1)
    code_i = iota((32, 128), 0)
    ca = code_i // 9
    cb = code_i // 3 - 3 * ca
    cc = code_i - 3 * (code_i // 3)
    coord = lax.shift_right_logical(lane, 4)
    step = jnp.where(coord == 0, ca, jnp.where(coord == 1, cb, jnp.where(coord == 2, cc, 1))) - 1
    shift = 5.0 * step.astype(F32)
    for c in range(CELLS):
        x, y, z = c // (CY * CZ), c // CZ % CY, c % CZ
        parts = []
        for k in range(0, 27, 3):
            at = ((x + k // 9) * 6 + y + k // 3 % 3) * 4 + z
            parts.append(rows[at : at + 3, :])
        parts.append(jnp.zeros((5, 128), F32))
        r27 = jnp.concatenate(parts, axis=0) + shift
        hi = r27.astype(BF)
        rest = r27 - hi.astype(F32)
        mid = rest.astype(BF)
        lo = (rest - mid.astype(F32)).astype(BF)
        cat = jnp.concatenate([hi, mid, lo, jnp.zeros((32, 128), BF)], axis=0)
        rt = nt(eye(64, 128), cat)
        rt_sc[c] = rt.astype(BF)
        centre = rt[:, 13:14] + (rt[:, 45:46] + rt[:, 77:78])
        ctr_sc[c] = centre * jnp.ones((64, L), F32)

    q_sc[...] = jnp.zeros_like(q_sc)
    dm_sc[...] = jnp.zeros_like(dm_sc)
    f_sc[...] = jnp.zeros_like(f_sc)
    en_sc[...] = jnp.zeros_like(en_sc)

    sub16 = iota((16, L), 0, F32)

    def where_of(c):
        x = lax.div(c, CY * CZ)
        rest = c - x * (CY * CZ)
        y = lax.div(rest, CZ)
        return x, y, rest - y * CZ

    def sphere(rx, ry, rz):
        d2 = rx * rx + ry * ry + rz * rz + 0.01
        inv = lax.rsqrt(d2)
        return d2, inv, d2 * inv, rx * inv, ry * inv, rz * inv

    def front(gi, _):
        ids = [gi * G + i for i in range(G)]
        cells = [list_c[i] for i in ids]
        atts, tabs = [], []
        for i, c in zip(ids, cells):
            rk = rank_sc[c]
            target = iota((L, 128), 0) + list_r[i]
            p = jnp.concatenate([onoff(rk[j : j + 1, :] == target).astype(BF) for j in range(8)], axis=1)
            atts.append(nt(att_sc[c], p))
        for c in cells:
            x, y, z = where_of(c)
            parts = [
                feats[pl.ds(((x + k // 3) * 6 + y + k % 3) * 4 + z, 3)].reshape(48, 128) for k in range(9)
            ]
            parts.append(jnp.zeros((80, 128), BF))
            t = nt(w_atomT[...], jnp.concatenate(parts, axis=0))
            tabs.append(
                jnp.concatenate([t[:, 0:384].astype(BF), (t[:, 384:512].astype(BF).astype(F32) + w_radpad[...]).astype(BF)], axis=1)
            )
        pres, rest = [], []
        for i, c, att, tab in zip(ids, cells, atts, tabs):
            code, slot, s, live = att[0:1], att[1:2], att[2:3], att[3:4]
            oh27 = onoff(code == iota((32, L), 0, F32)).astype(BF)
            m_slot = slot == sub16
            m_s = s == sub16
            got = nn(rt_sc[c], jnp.concatenate([oh27, oh27, oh27, jnp.zeros((32, L), BF)], axis=0))
            mine = ctr_sc[c]
            rel = []
            for d in range(3):
                sl = slice(16 * d, 16 * d + 16)
                rel.append(
                    jnp.sum(jnp.where(m_slot, got[sl], 0.0) - jnp.where(m_s, mine[sl], 0.0), axis=0, keepdims=True)
                )
            rx, ry, rz = rel
            d2, inv, dist, nx, ny, nz = sphere(rx, ry, rz)
            u = jnp.maximum(1.0 - d2 * (1.0 / 144.0), 0.0)
            w = live * (u * u)
            arg = (dist - (0.5 + 2.0 * iota((8, L), 0, F32))) * 0.5
            basis = jnp.exp(-(arg * arg))
            idx = code * 16.0 + slot
            oh = onoff(idx == iota((432, L), 0, F32))
            oh = jnp.concatenate(
                [oh[0:208], oh[208:224] + onoff(m_s), oh[224:432], basis, jnp.zeros((72, L), F32)], axis=0
            ).astype(BF)
            pres.append(nn(tab, oh))
            ylist = [
                jnp.ones((1, L), F32), nx, ny, nz, root_three * nx * ny, root_three * ny * nz,
                0.5 * (3.0 * nz * nz - 1.0), root_three * nx * nz, (0.5 * root_three) * (nx * nx - ny * ny),
            ]
            ys = jnp.concatenate([jnp.where(m_s, v, 0.0) for v in ylist], axis=0).astype(BF)
            geo = jnp.concatenate([rx, ry, rz, live, code, slot, s, w], axis=0)
            rest.append((ys, geo, w))
        firsts = [silu_both(v) for v in pres]
        secs = [silu_both(nn(w_hidT[...], f.astype(BF))) for f, _ in firsts]
        qs = []
        for (sec, d), (ys, geo, w) in zip(secs, rest):
            sb = sec.astype(BF)
            qs.append((sb, nt(ys, (sb.astype(F32) * w).astype(BF))))
        for i, c, (f, d1), (sec, d2), (ys, geo, w), (sb, q) in zip(ids, cells, firsts, secs, rest, qs):
            sec_sc[i] = sb
            d1_sc[i] = d1.astype(BF)
            d2_sc[i] = d2.astype(BF)
            ys_sc[i] = ys
            geo_sc[i] = geo
            q_sc[:, c] = q_sc[:, c] + q.reshape(9, 16, 128)
        return 0

    lax.fori_loop(0, groups, front, 0)

    for m in range(9):
        l = 0 if m == 0 else 1 if m < 4 else 2
        m_sc[m] = nn(q_sc[m].reshape(CELLS * 16, 128).astype(BF), c_sc[l]).astype(BF).reshape(CELLS, 16, 128)

    def middle(gi, _):
        ids = [gi * G + i for i in range(G)]
        cells = [list_c[i] for i in ids]
        wout = jnp.concatenate([wout_b[...]] * (L // 128), axis=1)
        mts = [nt(ident, m_sc[:, c].reshape(144, 128)).astype(BF) for c in cells]
        yss = [ys_sc[i] for i in ids]
        ps = [nn(w_mixT[...], sec_sc[i]) + nn(mt, ys) for i, mt, ys in zip(ids, mts, yss)]
        outs = []
        for i, p, ys in zip(ids, ps, yss):
            w = geo_sc[i, 7:8, :]
            mixed, d = silu_both(p)
            eps = jnp.sum(mixed * wout, axis=0, keepdims=True)
            g = (d * wout * w).astype(BF)
            we = eps * w
            hi = we.astype(BF).astype(F32)
            en = nt(jnp.where(iota((16, L), 0) == 0, hi, jnp.where(iota((16, L), 0) == 1, we - hi, 0.0)).astype(BF), ys[0:16])
            outs.append((eps, g, en, nt(ys, g)))
        for i, c, (eps, g, en, dm) in zip(ids, cells, outs):
            g_sc[i] = g
            eps_sc[i] = eps
            dm_sc[:, c] = dm_sc[:, c] + dm.reshape(9, 16, 128)
            en_sc[c] = en_sc[c] + en[0:8]
        return 0

    lax.fori_loop(0, groups, middle, 0)

    for m in range(9):
        l = 0 if m == 0 else 1 if m < 4 else 2
        dq_sc[m] = nt(dm_sc[m].reshape(CELLS * 16, 128).astype(BF), c_sc[l]).astype(BF).reshape(CELLS, 16, 128)

    def back(gi, _):
        ids = [gi * G + i for i in range(G)]
        cells = [list_c[i] for i in ids]
        dqs = [dq_sc[:, c].reshape(144, 128) for c in cells]
        dqts = [nt(ident, v).astype(BF) for v in dqs]
        gs = [g_sc[i] for i in ids]
        secs = [sec_sc[i] for i in ids]
        ts = [nn(v, ys_sc[i]) for i, v in zip(ids, dqts)]
        dpres, dys, dws = [], [], []
        for i, c, g, sb, t, dq in zip(ids, cells, gs, secs, ts, dqs):
            w = geo_sc[i, 7:8, :]
            sf = sb.astype(F32)
            dsec = nn(w_mix[0:128, :], g) + w * t
            dws.append(eps_sc[i] + jnp.sum(sf * t, axis=0, keepdims=True))
            both = jnp.concatenate([g, (sf * w).astype(BF)], axis=0)
            dys.append(nn(jnp.concatenate([m_sc[:, c].reshape(144, 128), dq], axis=1), both))
            dfirst = nn(w_hid[...], (dsec * d2_sc[i].astype(F32)).astype(BF))
            dpres.append((dfirst * d1_sc[i].astype(F32)).astype(BF))
        adds = []
        for i, dpre, dyf, dw in zip(ids, dpres, dys, dws):
            dbasis = nn(w_radrow[48:64, :], dpre)[0:8]
            geo = geo_sc[i]
            rx, ry, rz, live, code, slot, s = [geo[j : j + 1] for j in range(7)]
            d2, inv, dist, nx, ny, nz = sphere(rx, ry, rz)
            m_slot = slot == sub16
            m_s = s == sub16
            dy = [
                jnp.sum(jnp.where(m_s, dyf[16 * m : 16 * m + 16], 0.0), axis=0, keepdims=True) for m in range(1, 9)
            ]
            y1, y2, y3, y4, y5, y6, y7, y8 = dy
            ax = y1 + root_three * (ny * y4 + nz * y7 + nx * y8)
            ay = y2 + root_three * (nx * y4 + nz * y5 - ny * y8)
            az = y3 + root_three * (ny * y5 + nx * y7) + 3.0 * nz * y6
            arg = (dist - (0.5 + 2.0 * iota((8, L), 0, F32))) * 0.5
            basis = jnp.exp(-(arg * arg))
            dd = -jnp.sum(dbasis * basis * arg, axis=0, keepdims=True)
            dd = dd - (ax * nx + ay * ny + az * nz) * inv
            u = jnp.maximum(1.0 - d2 * (1.0 / 144.0), 0.0)
            radial = dd * inv + dw * live * u * (-4.0 / 144.0)
            grads = [a * inv + r * radial for a, r in ((ax, rx), (ay, ry), (az, rz))]
            other = jnp.concatenate([jnp.where(m_slot, -v, 0.0) for v in grads] + [jnp.zeros((16, L), F32)], axis=0)
            mine = jnp.concatenate([jnp.where(m_s, v, 0.0) for v in grads] + [jnp.zeros((16, L), F32)], axis=0)
            where32 = iota((32, L), 0, F32)
            oh = jnp.concatenate([onoff(code == where32), onoff(where32 == 13.0)], axis=1).astype(BF)
            adds.append(nt(oh, jnp.concatenate([other, mine], axis=1).astype(BF)))
        for c, f in zip(cells, adds):
            f_sc[c] = f_sc[c] + f
        return 0

    lax.fori_loop(0, groups, back, 0)

    fa = f_sc[...].reshape(CELLS * 32, 64)
    fh = fa.astype(BF)
    fl = (fa - fh.astype(F32)).astype(BF)
    force_out[...] = jnp.concatenate([nn(fold[...], fh) + nn(fold[...], fl), jnp.zeros((144, 64), F32)], axis=1)
    energy_out[...] = en_sc[:, 0, :] + en_sc[:, 1, :]


def fold_matrix():
    m = np.zeros((144, CELLS * 32), np.float32)
    for c in range(CELLS):
        x, y, z = c // (CY * CZ), c // CZ % CY, c % CZ
        for k in range(27):
            m[((x + k // 9) * 6 + y + k // 3 % 3) * 4 + z + k % 3, c * 32 + k] = 1
    return m


def edge_call(occ_ext, feats, rows, neigh, counts, w_atom, w_rad, w_hid, w_ten, w_mix, w_out):
    V = pltpu.VMEM
    vm = pl.BlockSpec(memory_space=pltpu.VMEM)
    return pl.pallas_call(
        edge_kernel,
        out_shape=(jax.ShapeDtypeStruct((CELLS, 16), F32), jax.ShapeDtypeStruct((144, 128), F32)),
        in_specs=[pl.BlockSpec(memory_space=pltpu.SMEM)] + [vm] * 11,
        out_specs=(vm, vm),
        scratch_shapes=[
            pltpu.SMEM((MAXCH,), jnp.int32),
            pltpu.SMEM((MAXCH,), jnp.int32),
            V((CELLS, 8, 128), jnp.int32),
            V((CELLS, 16, 1024), BF),
            V((CELLS, 64, 128), BF),
            V((CELLS, 64, L), F32),
            V((128, 128), BF),
            V((128, 128), BF),
            V((128, 128), BF),
            V((128, 128), F32),
            V((128, 128), BF),
            V((128, 128), F32),
            V((3, 128, 128), BF),
            V((9, CELLS, 16, 128), F32),
            V((9, CELLS, 16, 128), F32),
            V((9, CELLS, 16, 128), BF),
            V((9, CELLS, 16, 128), BF),
            V((CELLS, 32, 64), F32),
            V((CELLS, 8, 16), F32),
            V((MAXCH, 128, L), BF),
            V((MAXCH, 128, L), BF),
            V((MAXCH, 128, L), BF),
            V((MAXCH, 128, L), BF),
            V((MAXCH, 144, L), BF),
            V((MAXCH, 8, L), F32),
            V((MAXCH, 1, L), F32),
        ],
        compiler_params=pltpu.CompilerParams(vmem_limit_bytes=60 * 1024 * 1024),
        name="edges",
    )(occ_ext, feats, rows, neigh, counts, w_atom, w_rad, w_hid, w_ten, w_mix, w_out, jnp.asarray(fold_matrix(), BF))


def wanted(axis, step):
    return lax.rem(lax.axis_index(axis) + step + lax.axis_size(axis), lax.axis_size(axis))


def meet():
    barrier = pltpu.get_barrier_semaphore()
    for axis in ("gx", "gy", "gz"):
        for step in (-1, 1):
            pl.semaphore_signal(
                barrier, inc=1, device_id={axis: wanted(axis, step)}, device_id_type=pl.DeviceIdType.MESH
            )
    pl.semaphore_wait(barrier, 6)


def sent(src, dst, send, recv, axis, step):
    copy = pltpu.make_async_remote_copy(
        src_ref=src,
        dst_ref=dst,
        send_sem=send,
        recv_sem=recv,
        device_id={axis: wanted(axis, step)},
        device_id_type=pl.DeviceIdType.MESH,
    )
    copy.start()
    return copy


def halo_kernel(pos, occ, feat, feat_ext, rows_ext, send, recv):
    table = jnp.concatenate(
        [pos[0], pos[1], pos[2], occ[...].astype(F32), jnp.zeros((CELLS, 64), F32)], axis=1
    )
    for x in range(CX):
        for y in range(CY):
            for z in range(CZ):
                c = (x * CY + y) * CZ + z
                rows_ext[x + 1, y + 1, z + 1] = table[c : c + 1]
                feat_ext[x + 1, y + 1, z + 1] = feat[c]
    meet()
    inner_y, inner_z = pl.ds(1, CY), pl.ds(1, CZ)
    everything = slice(None)
    places = (
        ("gx", CX, lambda i: (pl.ds(i, 1), inner_y, inner_z)),
        ("gy", CY, lambda i: (everything, pl.ds(i, 1), inner_z)),
        ("gz", CZ, lambda i: (everything, everything, pl.ds(i, 1))),
    )
    for stage, (axis, n, at) in enumerate(places):
        copies = []
        for way, (step, mine, theirs) in enumerate(((-1, 1, n + 1), (1, n, 0))):
            for which, array in enumerate((feat_ext, rows_ext)):
                j = stage * 4 + way * 2 + which
                copies.append(
                    sent(array.at[at(mine)], array.at[at(theirs)], send.at[j], recv.at[j], axis, step)
                )
        for copy in copies:
            copy.wait()


def halo_call(pos, occ, feat):
    vm = pl.BlockSpec(memory_space=pltpu.VMEM)
    return pl.pallas_call(
        halo_kernel,
        out_shape=(
            jax.ShapeDtypeStruct((CX + 2, CY + 2, CZ + 2, 16, 128), BF),
            jax.ShapeDtypeStruct((CX + 2, CY + 2, CZ + 2, 1, 128), F32),
        ),
        in_specs=[vm] * 3,
        out_specs=(vm, vm),
        scratch_shapes=[pltpu.SemaphoreType.DMA((12,)), pltpu.SemaphoreType.DMA((12,))],
        compiler_params=pltpu.CompilerParams(collective_id=0, has_side_effects=True),
        name="halo",
    )(pos, occ, feat)


def fold_kernel(grid, out, acc, got_x, got_y, got_z, send, recv):
    acc[...] = grid[...]
    meet()
    inner_x, inner_y = pl.ds(1, CX), pl.ds(1, CY)
    everything = slice(None)
    places = (
        ("gx", CX, got_x, lambda i: (pl.ds(i, 1), everything, everything)),
        ("gy", CY, got_y, lambda i: (inner_x, pl.ds(i, 1), everything)),
        ("gz", CZ, got_z, lambda i: (inner_x, inner_y, pl.ds(i, 1))),
    )
    for stage, (axis, n, got, at) in enumerate(places):
        copies = []
        for way, (step, rim) in enumerate(((-1, 0), (1, n + 1))):
            j = stage * 2 + way
            copies.append(sent(acc.at[at(rim)], got.at[way], send.at[j], recv.at[j], axis, step))
        for way, edge in enumerate((n, 1)):
            copies[way].wait()
            acc[at(edge)] = acc[at(edge)] + got[way]
    lines = []
    for x in range(CX):
        for y in range(CY):
            for z in range(CZ):
                lines.append(acc[x + 1, y + 1, z + 1])
    lines = jnp.concatenate(lines, axis=0)
    for d in range(3):
        out[d] = lines[:, 16 * d : 16 * d + 16]


def fold_call(grid):
    vm = pl.BlockSpec(memory_space=pltpu.VMEM)
    V = pltpu.VMEM
    return pl.pallas_call(
        fold_kernel,
        out_shape=jax.ShapeDtypeStruct((3, CELLS, 16), F32),
        in_specs=[vm],
        out_specs=vm,
        scratch_shapes=[
            V((CX + 2, CY + 2, CZ + 2, 1, 128), F32),
            V((2, 1, CY + 2, CZ + 2, 1, 128), F32),
            V((2, CX, 1, CZ + 2, 1, 128), F32),
            V((2, CX, CY, 1, 1, 128), F32),
            pltpu.SemaphoreType.DMA((6,)),
            pltpu.SemaphoreType.DMA((6,)),
        ],
        compiler_params=pltpu.CompilerParams(collective_id=1, has_side_effects=True),
        name="fold",
    )(grid)


def on_device(
    positions, occupancy, neighbours, edge_counts, atom_features, w_atom, w_radial, w_hidden, w_tensor, w_mix, w_out
):
    occ = jnp.broadcast_to(occupancy.reshape(CELLS, 1), (CELLS, 16))
    feats, rows = halo_call(positions.reshape(3, CELLS, 16), occ, atom_features.reshape(CELLS, 16, 128))
    rows = rows.reshape(144, 128)
    energy, forces = edge_call(
        rows[:, 48].astype(jnp.int32),
        feats.reshape(144, 16, 128),
        rows,
        neighbours.reshape(CELLS, 16, 64),
        edge_counts.reshape(CELLS, 16),
        w_atom, w_radial, w_hidden, w_tensor, w_mix, w_out.reshape(1, 128),
    )
    forces = fold_call(forces.reshape(CX + 2, CY + 2, CZ + 2, 1, 128))
    return energy.reshape(CX, CY, CZ, 16), forces.reshape(3, CX, CY, CZ, 16)


def solution(mesh):
    cells = P("gx", "gy", "gz", None)
    placed = (
        P(None, "gx", "gy", "gz", None),
        P("gx", "gy", "gz"),
        P("gx", "gy", "gz", None, None),
        cells,
        P("gx", "gy", "gz", None, None),
        P(), P(), P(), P(), P(), P(),
    )
    return jax.shard_map(
        on_device,
        mesh=mesh,
        in_specs=placed,
        out_specs=(cells, P(None, "gx", "gy", "gz", None)),
        check_vma=False,
    )
```

```python
import numpy as np
import jax
import jax.numpy as jnp
from jax import lax
from jax.experimental import pallas as pl
from jax.experimental.pallas import tpu as pltpu
from jax.sharding import PartitionSpec as P

F32 = jnp.float32
BF = jnp.bfloat16
I32 = jnp.int32
root_three = 1.7320508075688772
L = 256
G = 8
CX, CY, CZ = 4, 4, 2
EX, EY, EZ = CX + 2, CY + 2, CZ + 2
CELLS = CX * CY * CZ
GHOSTED = EX * EY * EZ
MAXCH = CELLS * (1024 // L)


def nn(a, b):
    return lax.dot_general(a, b, (((1,), (0,)), ((), ())), preferred_element_type=F32)


def nt(a, b):
    return lax.dot_general(a, b, (((1,), (1,)), ((), ())), preferred_element_type=F32)


def iota(shape, dim, dtype=I32):
    return lax.broadcasted_iota(I32, shape, dim).astype(dtype)


def onoff(mask):
    return jnp.where(mask, 1.0, 0.0).astype(F32)


def eye(n, m):
    return onoff(iota((n, m), 0) == iota((n, m), 1)).astype(BF)


def place_of(c):
    return c // (CY * CZ), c // CZ % CY, c % CZ


def ext_at(x, y, z):
    return (x * EY + y) * EZ + z


def prepare_weights(w_atom, w_rad, w_hid, w_ten_t, w_mix, w_out, mats, radpad, wout_b):
    ident = eye(128, 128)
    half = 0.5
    mats[0] = (half * nt(ident, w_atom[...])).astype(BF)
    mats[1] = (half * nt(ident, w_hid[...])).astype(BF)
    mats[2] = (half * nt(ident, w_mix[0:128, :])).astype(BF)
    rad = jnp.concatenate([jnp.zeros((48, 128), F32), w_rad[...].astype(F32), jnp.zeros((72, 128), F32)], axis=0)
    mats[3] = rad.astype(BF)
    radpad[...] = half * nt(ident, rad.astype(BF))
    wout_b[...] = jnp.sum(
        jnp.where(iota((128, 128), 0) == iota((128, 128), 1), w_out[...], 0.0), axis=1, keepdims=True
    ) * jnp.ones((128, 128), F32)
    tail = w_mix[128:224, :]
    for l in range(3):
        sel = onoff(iota((96, 32), 0) == 3 * iota((96, 32), 1) + l).astype(BF)
        spread = nt(ident, nn(sel, w_ten_t[...]).astype(BF)).astype(BF)
        mats[4 + l] = (0.0625 * nn(spread, tail)).astype(BF)


def prepare_edges(rows, rows2, occ_sp, neigh, counts, rank_out, code_out, rt_out, list_out):
    for x in range(EX):
        for y in range(EY):
            for z in range(EZ):
                at = ext_at(x, y, z)
                rows2[at : at + 1, :] = rows[x, y, z]
    occ_sp[...] = nn(rows2[...].astype(BF), onoff(iota((128, 128), 0) == 48).astype(BF))
    counts_t = nt(eye(16, 16), counts[...].astype(F32).astype(BF))
    lane64 = iota((8, 128), 1)
    low = lane64 < 64
    k_of = jnp.where(low, lane64, lane64 - 64).astype(F32)
    s_of = jnp.where(low, iota((8, 128), 0), iota((8, 128), 0) + 8)
    s_f = s_of.astype(F32)
    masks = []
    for c in range(CELLS):
        x, y, z = place_of(c)
        nb = jnp.concatenate([neigh[c, 0:8, :], neigh[c, 8:16, :]], axis=1)
        code_out[c] = nb
        cnt = jnp.where(low, counts_t[0:8, c : c + 1], counts_t[8:16, c : c + 1])
        code = lax.shift_right_logical(nb, 4)
        slot = lax.bitwise_and(nb, 15).astype(F32)
        occ_n = jnp.zeros((8, 128), F32)
        for k in range(27):
            at = ext_at(x + k // 9, y + k // 3 % 3, z + k % 3)
            occ_n = jnp.where(code == k, occ_sp[at : at + 1, :], occ_n)
        at = ext_at(x + 1, y + 1, z + 1)
        live = (k_of < cnt) & (slot < occ_n) & (s_f < occ_sp[at : at + 1, :]) & (nb != 208 + s_of)
        masks.append(onoff(live))
    mask = jnp.concatenate(masks, axis=0)
    mask_b = mask.astype(BF)
    upto = nn(mask_b, onoff(iota((128, 128), 0) <= iota((128, 128), 1)).astype(BF))
    total = nn(mask_b, jnp.ones((128, 128), BF))
    ri, ci = iota((256, 256), 0), iota((256, 256), 1)
    before = onoff((lax.shift_right_logical(ri, 3) == lax.shift_right_logical(ci, 3)) & (ci < ri)).astype(BF)
    base = nn(before, total.astype(BF))
    rank_out[...] = jnp.where(mask > 0.5, upto - 1.0 + base, -1.0).astype(I32).reshape(CELLS, 8, 128)
    n = (base + total).reshape(CELLS, 8, 128)[:, 7, :].astype(I32)
    chunks = lax.shift_right_logical(n + (L - 1), L.bit_length() - 1).astype(F32)
    ends = nn(onoff(iota((CELLS, CELLS), 1) <= iota((CELLS, CELLS), 0)).astype(BF), chunks.astype(BF))
    t = iota((CELLS, 128), 1, F32)
    done = ends <= t
    cell = jnp.minimum(jnp.sum(onoff(done), axis=0, keepdims=True), CELLS - 1.0)
    start = jnp.max(jnp.where(done, ends, 0.0), axis=0, keepdims=True)
    all_of = ends[CELLS - 1 : CELLS]
    first = jnp.where(t[0:1] < all_of, (t[0:1] - start) * L, 4096.0)
    list_out[...] = jnp.concatenate([cell, first, all_of, jnp.zeros((5, 128), F32)], axis=0).astype(I32)

    lane = iota((32, 128), 1)
    code_i = iota((32, 128), 0)
    ca = code_i // 9
    cb = code_i // 3 - 3 * ca
    cc = code_i - 3 * (code_i // 3)
    coord = lax.shift_right_logical(lane, 4)
    step = jnp.where(coord == 0, ca, jnp.where(coord == 1, cb, jnp.where(coord == 2, cc, 1))) - 1
    shift = 5.0 * step.astype(F32)
    pick = eye(48, 128)
    for c in range(CELLS):
        x, y, z = place_of(c)
        parts = []
        for k in range(0, 27, 3):
            at = ext_at(x + k // 9, y + k // 3 % 3, z)
            parts.append(rows2[at : at + 3, :])
        parts.append(jnp.zeros((5, 128), F32))
        r27 = jnp.concatenate(parts, axis=0) + shift
        hi = r27.astype(BF)
        rest = r27 - hi.astype(F32)
        mid = rest.astype(BF)
        lo = (rest - mid.astype(F32)).astype(BF)
        cat = jnp.concatenate([hi, mid, lo, jnp.zeros((32, 128), BF)], axis=0)
        rt_out[c] = nt(pick, cat).astype(BF)


def silu_both(h):
    t = jnp.tanh(h)
    a = 1.0 + t
    return h * a, a * (1.0 + h * (1.0 - t))


def rows16(v):
    return jnp.broadcast_to(v, (16, v.shape[1])).astype(BF)


def edge_kernel(
    list_s, feats, rank_r, code_r, rt_r, mats, radpad, wout_b, w_mix, w_hid, fold, foldc,
    energy_out, force_out,
    q_sc, dm_sc, m_sc, dq_sc, f_sc, en_sc, sec_sc, d1_sc, d2_sc, g_sc, ys_sc, geo_sc, eps_sc,
):
    groups = lax.div(list_s[2, 0] + (G - 1), G)
    ident = eye(128, 128)
    q_sc[...] = jnp.zeros_like(q_sc)
    dm_sc[...] = jnp.zeros_like(dm_sc)
    f_sc[...] = jnp.zeros_like(f_sc)
    en_sc[...] = jnp.zeros_like(en_sc)
    sub16 = iota((16, L), 0, F32)
    one = jnp.ones((16, L), BF)
    zero = jnp.zeros((16, L), BF)

    def ids_of(gi):
        ids = [gi * G + i for i in range(G)]
        return ids, [list_s[0, i] for i in ids]

    def sphere(rx, ry, rz):
        d2 = rx * rx + ry * ry + rz * rz + 0.01
        inv = lax.rsqrt(d2)
        return d2, inv, d2 * inv, rx * inv, ry * inv, rz * inv

    def front(gi, _):
        ids, cells = ids_of(gi)
        atts, tabs = [], []
        r_of = iota((L, 128), 0, F32).astype(BF)
        s_lane = iota((1, 128), 1)
        sub = iota((16, 128), 0)
        for i, c in zip(ids, cells):
            rk = rank_r[c] - list_s[1, i]
            rk = jnp.where((rk >= 0) & (rk < L), rk, -1).astype(F32)
            nb = code_r[c]
            code_f = lax.shift_right_logical(nb, 4).astype(F32)
            slot_f = lax.bitwise_and(nb, 15).astype(F32)
            ps, att = [], []
            for j in range(8):
                target = jnp.concatenate([jnp.broadcast_to(rk[j : j + 1], (16, 128)).astype(BF)] * (L // 16), axis=0)
                ps.append(jnp.where(r_of == target, jnp.ones((L, 128), BF), jnp.zeros((L, 128), BF)))
                s_row = jnp.where(s_lane < 64, float(j), float(j + 8))
                a = jnp.where(
                    sub == 0, code_f[j : j + 1], jnp.where(sub == 1, slot_f[j : j + 1], jnp.where(sub == 2, s_row, 1.0))
                )
                att.append(a.astype(BF))
            atts.append(nt(jnp.concatenate(att, axis=1), jnp.concatenate(ps, axis=1)))
        for c in cells:
            x = lax.div(c, CY * CZ)
            left = c - x * (CY * CZ)
            y = lax.div(left, CZ)
            z = left - y * CZ
            parts = [
                feats[pl.ds(((x + k // 3) * EY + y + k % 3) * EZ + z, 3)].reshape(48, 128) for k in range(9)
            ]
            parts.append(jnp.zeros((80, 128), BF))
            t = nt(mats[0], jnp.concatenate(parts, axis=0))
            tabs.append(jnp.concatenate([t[:, 0:384], t[:, 384:512] + radpad[...]], axis=1).astype(BF))
        pres, rest = [], []
        for i, c, att, tab in zip(ids, cells, atts, tabs):
            code, slot, s, live = att[0:1], att[1:2], att[2:3], att[3:4]
            oh27 = onoff(code == iota((32, L), 0, F32)).astype(BF)
            m_slot = slot == sub16
            m_s = s == sub16
            rt = rt_r[c]
            got = nn(rt, jnp.concatenate([oh27, oh27, oh27, jnp.zeros((32, L), BF)], axis=0))
            rtf = rt.astype(F32)
            centre = rtf[:, 13:14] + (rtf[:, 45:46] + rtf[:, 77:78])
            rel = []
            for d in range(3):
                sl = slice(16 * d, 16 * d + 16)
                rel.append(
                    jnp.sum(jnp.where(m_slot, got[sl], 0.0) - jnp.where(m_s, centre[sl], 0.0), axis=0, keepdims=True)
                )
            rx, ry, rz = rel
            d2, inv, dist, nx, ny, nz = sphere(rx, ry, rz)
            u = jnp.maximum(1.0 - d2 * (1.0 / 144.0), 0.0)
            w = live * (u * u)
            arg = (dist - (0.5 + 2.0 * iota((8, L), 0, F32))) * 0.5
            basis = jnp.exp(-(arg * arg))
            slot01 = onoff(m_slot).astype(BF)
            s01 = onoff(m_s).astype(BF)
            code16 = rows16(code)
            tiles = [jnp.where(code16 == float(k), slot01, zero) for k in range(27)]
            tiles[13] = tiles[13] + s01
            tiles.append(jnp.concatenate([basis, jnp.zeros((8, L), F32)], axis=0).astype(BF))
            pres.append(nn(tab, jnp.concatenate(tiles + [zero] * 4, axis=0)))
            ylist = [
                nx, ny, nz, root_three * nx * ny, root_three * ny * nz,
                0.5 * (3.0 * nz * nz - 1.0), root_three * nx * nz, (0.5 * root_three) * (nx * nx - ny * ny),
            ]
            ys = jnp.concatenate([s01] + [s01 * rows16(v) for v in ylist], axis=0)
            geo = jnp.concatenate([rx, ry, rz, live, code, slot, s, w], axis=0)
            rest.append((ys, geo, rows16(w)))
        firsts = [silu_both(v) for v in pres]
        secs = [silu_both(nn(mats[1], f.astype(BF))) for f, _ in firsts]
        qs = []
        for (sec, d), (ys, geo, w16) in zip(secs, rest):
            sb = sec.astype(BF)
            qs.append((sb, nt(ys * jnp.concatenate([w16] * 9, axis=0), sb)))
        for i, c, (f, d1), (sec, d2), (ys, geo, w16), (sb, q) in zip(ids, cells, firsts, secs, rest, qs):
            sec_sc[i] = sb
            d1_sc[i] = d1.astype(BF)
            d2_sc[i] = d2.astype(BF)
            ys_sc[i] = ys
            geo_sc[i] = geo
            q_sc[:, c] = q_sc[:, c] + q.reshape(9, 16, 128)
        return 0

    lax.fori_loop(0, groups, front, 0)

    for m in range(9):
        l = 0 if m == 0 else 1 if m < 4 else 2
        m_sc[m] = nn(q_sc[m].reshape(CELLS * 16, 128).astype(BF), mats[4 + l]).astype(BF).reshape(CELLS, 16, 128)

    def middle(gi, _):
        ids, cells = ids_of(gi)
        wout = jnp.concatenate([wout_b[...]] * (L // 128), axis=1)
        wout_h = 0.5 * wout
        mts = [nt(ident, m_sc[:, c].reshape(144, 128)).astype(BF) for c in cells]
        yss = [ys_sc[i] for i in ids]
        ps = [nn(mats[2], sec_sc[i]) + nn(mt, ys) for i, mt, ys in zip(ids, mts, yss)]
        outs = []
        for i, p, ys in zip(ids, ps, yss):
            w = geo_sc[i, 7:8, :]
            mixed, d = silu_both(p)
            eps = jnp.sum(mixed * wout, axis=0, keepdims=True)
            g = (d * wout_h).astype(BF)
            we = eps * w
            hi = we.astype(BF).astype(F32)
            en = nt(jnp.where(iota((16, L), 0) == 0, hi, jnp.where(iota((16, L), 0) == 1, we - hi, 0.0)).astype(BF), ys[0:16])
            outs.append((eps, g, en, nt(ys * jnp.concatenate([rows16(w)] * 9, axis=0), g)))
        for i, c, (eps, g, en, dm) in zip(ids, cells, outs):
            g_sc[i] = g
            eps_sc[i] = eps
            dm_sc[:, c] = dm_sc[:, c] + dm.reshape(9, 16, 128)
            en_sc[c] = en_sc[c] + en[0:8]
        return 0

    lax.fori_loop(0, groups, middle, 0)

    for m in range(9):
        l = 0 if m == 0 else 1 if m < 4 else 2
        dq_sc[m] = nt(dm_sc[m].reshape(CELLS * 16, 128).astype(BF), mats[4 + l]).astype(BF).reshape(CELLS, 16, 128)

    def back(gi, _):
        ids, cells = ids_of(gi)
        dqs = [dq_sc[:, c].reshape(144, 128) for c in cells]
        dqts = [nt(ident, v).astype(BF) for v in dqs]
        secs = [sec_sc[i] for i in ids]
        ts = [nn(v, ys_sc[i]) for i, v in zip(ids, dqts)]
        dpres, dys, dws = [], [], []
        top = jnp.concatenate([w_mix[0:128, :], jnp.zeros((128, 128), BF)], axis=1)
        for i, c, sb, t, dq in zip(ids, cells, secs, ts, dqs):
            t2 = t + t
            low = jnp.concatenate([m_sc[:, c].reshape(144, 128), dq], axis=1)
            both = nn(jnp.concatenate([top, low], axis=0), jnp.concatenate([g_sc[i], sb], axis=0))
            dsec = both[0:128] + t2
            dws.append(eps_sc[i] + jnp.sum(sb.astype(F32) * t2, axis=0, keepdims=True))
            dys.append(both[128:272])
            dfirst = nn(w_hid[...], (dsec * d2_sc[i].astype(F32)).astype(BF))
            dpres.append((dfirst * d1_sc[i].astype(F32)).astype(BF))
        adds = []
        for i, dpre, dyf, dw in zip(ids, dpres, dys, dws):
            dbasis = nn(mats[3, 48:64, :], dpre)[0:8]
            geo = geo_sc[i]
            rx, ry, rz, live, code, slot, s, w = [geo[j : j + 1] for j in range(8)]
            d2, inv, dist, nx, ny, nz = sphere(rx, ry, rz)
            m_slot = slot == sub16
            m_s = s == sub16
            w2 = w + w
            dy = [
                jnp.sum(jnp.where(m_s, dyf[16 * m : 16 * m + 16], 0.0), axis=0, keepdims=True) * w2 for m in range(1, 9)
            ]
            y1, y2, y3, y4, y5, y6, y7, y8 = dy
            ax = y1 + root_three * (ny * y4 + nz * y7 + nx * y8)
            ay = y2 + root_three * (nx * y4 + nz * y5 - ny * y8)
            az = y3 + root_three * (ny * y5 + nx * y7) + 3.0 * nz * y6
            arg = (dist - (0.5 + 2.0 * iota((8, L), 0, F32))) * 0.5
            basis = jnp.exp(-(arg * arg))
            dd = jnp.sum(dbasis * basis * arg, axis=0, keepdims=True) * (-0.25 * w)
            dd = dd - (ax * nx + ay * ny + az * nz) * inv
            u = jnp.maximum(1.0 - d2 * (1.0 / 144.0), 0.0)
            radial = dd * inv + dw * live * u * (-4.0 / 144.0)
            grads = [a * inv + r * radial for a, r in ((ax, rx), (ay, ry), (az, rz))]
            slot01 = onoff(m_slot).astype(BF)
            s01 = onoff(m_s).astype(BF)
            g16 = [rows16(v) for v in grads]
            parts = [slot01 * -v for v in g16] + [zero] + [s01 * v for v in g16] + [zero]
            where32 = iota((32, L), 0, F32)
            oh = onoff((code == where32) | (where32 == 27.0)).astype(BF)
            adds.append(nt(oh, jnp.concatenate(parts, axis=0)))
        for c, f in zip(cells, adds):
            f_sc[c] = f_sc[c] + f
        return 0

    lax.fori_loop(0, groups, back, 0)

    fa = f_sc[...].reshape(CELLS * 32, 128)
    fh = fa.astype(BF)
    fl = (fa - fh.astype(F32)).astype(BF)
    others = nn(fold[...], fh) + nn(fold[...], fl)
    own = nn(foldc[...], fh) + nn(foldc[...], fl)
    force_out[...] = others + jnp.concatenate([own[:, 64:128], jnp.zeros((GHOSTED, 64), F32)], axis=1)
    energy_out[...] = en_sc[:, 0, :] + en_sc[:, 1, :]


def fold_matrices():
    m = np.zeros((2, GHOSTED, CELLS * 32), np.float32)
    for c in range(CELLS):
        x, y, z = place_of(c)
        for k in range(27):
            m[0, ext_at(x + k // 9, y + k // 3 % 3, z + k % 3), c * 32 + k] = 1
        m[1, ext_at(x + 1, y + 1, z + 1), c * 32 + 27] = 1
    return m


PREPARED = (
    jax.ShapeDtypeStruct((CELLS, 8, 128), I32),
    jax.ShapeDtypeStruct((CELLS, 8, 128), I32),
    jax.ShapeDtypeStruct((CELLS, 48, 128), BF),
    jax.ShapeDtypeStruct((8, 128), I32),
    jax.ShapeDtypeStruct((7, 128, 128), BF),
    jax.ShapeDtypeStruct((128, 128), F32),
    jax.ShapeDtypeStruct((128, 128), F32),
)


def edge_stage(feats, prepared, w_mix, w_hid):
    rank, code, rt, todo, mats, radpad, wout_b = prepared
    V = pltpu.VMEM
    vm = pl.BlockSpec(memory_space=pltpu.VMEM)
    folds = fold_matrices()
    return pl.pallas_call(
        edge_kernel,
        out_shape=(jax.ShapeDtypeStruct((CELLS, 16), F32), jax.ShapeDtypeStruct((GHOSTED, 128), F32)),
        in_specs=[pl.BlockSpec(memory_space=pltpu.SMEM)] + [vm] * 11,
        out_specs=(vm, vm),
        scratch_shapes=[
            V((9, CELLS, 16, 128), F32),
            V((9, CELLS, 16, 128), F32),
            V((9, CELLS, 16, 128), BF),
            V((9, CELLS, 16, 128), BF),
            V((CELLS, 32, 128), F32),
            V((CELLS, 8, 16), F32),
            V((MAXCH, 128, L), BF),
            V((MAXCH, 128, L), BF),
            V((MAXCH, 128, L), BF),
            V((MAXCH, 128, L), BF),
            V((MAXCH, 144, L), BF),
            V((MAXCH, 8, L), F32),
            V((MAXCH, 1, L), F32),
        ],
        compiler_params=pltpu.CompilerParams(vmem_limit_bytes=60 * 1024 * 1024),
        name="edges",
    )(todo, feats, rank, code, rt, mats, radpad, wout_b, w_mix, w_hid, jnp.asarray(folds[0], BF), jnp.asarray(folds[1], BF))


MESH = pl.DeviceIdType.MESH
AROUND = tuple((dx, dy) for dx in (-1, 0, 1) for dy in (-1, 0, 1) if (dx, dy) != (0, 0))


def peer(dx, dy, dz):
    there = {}
    for axis, step in (("gx", dx), ("gy", dy), ("gz", dz)):
        size = lax.axis_size(axis)
        there[axis] = lax.rem(lax.axis_index(axis) + (step + size), size)
    return there


def greet():
    barrier = pltpu.get_barrier_semaphore()
    for dx, dy, dz in [(0, 0, -1), (0, 0, 1)] + [(dx, dy, 0) for dx, dy in AROUND]:
        pl.semaphore_signal(barrier, inc=1, device_id=peer(dx, dy, dz), device_id_type=MESH)
    return barrier


def sent(src, dst, send, recv, there):
    copy = pltpu.make_async_remote_copy(
        src_ref=src, dst_ref=dst, send_sem=send, recv_sem=recv, device_id=there, device_id_type=MESH
    )
    copy.start()
    return copy


def border(step, n):
    return pl.ds(1, n) if step == 0 else pl.ds(1 if step < 0 else n, 1)


def ghost(step, n):
    return pl.ds(1, n) if step == 0 else pl.ds(n + 1 if step < 0 else 0, 1)


def halo_kernel(
    occ_s, pos, feat, neigh, counts, w_atom, w_rad, w_hid, w_ten_t, w_mix, w_out,
    feat_ext, rank, code, rt, todo, mats, radpad, wout_b,
    rows, rows2, occ_sp, send, recv,
):
    barrier = greet()
    table = jnp.concatenate([pos[0], pos[1], pos[2], jnp.zeros((CELLS, 80), F32)], axis=1)
    lane = iota((1, 128), 1)
    for c in range(CELLS):
        x, y, z = place_of(c)
        rows[x + 1, y + 1, z + 1] = jnp.where(lane < 48, table[c : c + 1], occ_s[x, z, y].astype(F32))
        feat_ext[x + 1, y + 1, z + 1] = feat[c]
    pl.semaphore_wait(barrier, 10)

    def along_z(array, base):
        copies = []
        for j, step in enumerate((-1, 1)):
            at = (pl.ds(1, CX), pl.ds(1, CY))
            src = array.at[at + (border(step, CZ),)]
            dst = array.at[at + (ghost(step, CZ),)]
            copies.append(sent(src, dst, send.at[base + j], recv.at[base + j], peer(0, 0, step)))
        return copies

    def around(array, base):
        copies = []
        for j, (dx, dy) in enumerate(AROUND):
            src = array.at[border(dx, CX), border(dy, CY)]
            dst = array.at[ghost(dx, CX), ghost(dy, CY)]
            copies.append(sent(src, dst, send.at[base + j], recv.at[base + j], peer(dx, dy, 0)))
        return copies

    rows_z = along_z(rows, 0)
    feat_z = along_z(feat_ext, 2)
    for copy in rows_z:
        copy.wait()
    rows_xy = around(rows, 4)
    for copy in feat_z:
        copy.wait()
    feat_xy = around(feat_ext, 12)
    prepare_weights(w_atom, w_rad, w_hid, w_ten_t, w_mix, w_out, mats, radpad, wout_b)
    for copy in rows_xy:
        copy.wait()
    prepare_edges(rows, rows2, occ_sp, neigh, counts, rank, code, rt, todo)
    for copy in feat_xy:
        copy.wait()


def halo_stage(occ, pos, feat, neigh, counts, w_atom, w_rad, w_hid, w_ten_t, w_mix, w_out):
    vm = pl.BlockSpec(memory_space=pltpu.VMEM)
    V = pltpu.VMEM
    out = pl.pallas_call(
        halo_kernel,
        out_shape=(jax.ShapeDtypeStruct((EX, EY, EZ, 16, 128), BF),) + PREPARED,
        in_specs=[pl.BlockSpec(memory_space=pltpu.SMEM)] + [vm] * 10,
        out_specs=(vm,) * 8,
        scratch_shapes=[
            V((EX, EY, EZ, 1, 128), F32),
            V((GHOSTED, 128), F32),
            V((GHOSTED, 128), F32),
            pltpu.SemaphoreType.DMA((20,)),
            pltpu.SemaphoreType.DMA((20,)),
        ],
        compiler_params=pltpu.CompilerParams(
            collective_id=0, has_side_effects=True, vmem_limit_bytes=32 * 1024 * 1024
        ),
        name="halo",
    )(occ, pos, feat, neigh, counts, w_atom, w_rad, w_hid, w_ten_t, w_mix, w_out)
    return out[0], out[1:]


def fold_kernel(grid, out, acc, got_x, got_y, got_xy, got_z, send, recv):
    barrier = greet()
    acc[...] = grid[...]
    pl.semaphore_wait(barrier, 10)
    copies = []
    for j, (dx, dy) in enumerate(AROUND):
        if dx and dy:
            got = got_xy.at[(dx + 1) + (dy + 1) // 2]
        elif dx:
            got = got_x.at[(dx + 1) // 2]
        else:
            got = got_y.at[(dy + 1) // 2]
        rim = (
            pl.ds(1, CX) if dx == 0 else pl.ds(0 if dx < 0 else CX + 1, 1),
            pl.ds(1, CY) if dy == 0 else pl.ds(0 if dy < 0 else CY + 1, 1),
        )
        copies.append((sent(acc.at[rim], got, send.at[j], recv.at[j], peer(dx, dy, 0)), got, dx, dy))
    for copy, got, dx, dy in copies:
        copy.wait()
        at = (border(-dx, CX), border(-dy, CY))
        acc[at] = acc[at] + got[...]
    inner = (pl.ds(1, CX), pl.ds(1, CY))
    copies = []
    for j, (step, rim) in enumerate(((-1, 0), (1, CZ + 1))):
        copies.append(
            sent(acc.at[inner + (pl.ds(rim, 1),)], got_z.at[j], send.at[8 + j], recv.at[8 + j], peer(0, 0, step))
        )
    for j, step in enumerate((-1, 1)):
        copies[j].wait()
        at = inner + (border(-step, CZ),)
        acc[at] = acc[at] + got_z[j]
    lines = []
    for c in range(CELLS):
        x, y, z = place_of(c)
        lines.append(acc[x + 1, y + 1, z + 1])
    lines = jnp.concatenate(lines, axis=0)
    for d in range(3):
        out[d] = lines[:, 16 * d : 16 * d + 16]


def fold_stage(grid):
    vm = pl.BlockSpec(memory_space=pltpu.VMEM)
    V = pltpu.VMEM
    return pl.pallas_call(
        fold_kernel,
        out_shape=jax.ShapeDtypeStruct((3, CELLS, 16), F32),
        in_specs=[vm],
        out_specs=vm,
        scratch_shapes=[
            V((EX, EY, EZ, 1, 128), F32),
            V((2, 1, CY, EZ, 1, 128), F32),
            V((2, CX, 1, EZ, 1, 128), F32),
            V((4, 1, 1, EZ, 1, 128), F32),
            V((2, CX, CY, 1, 1, 128), F32),
            pltpu.SemaphoreType.DMA((10,)),
            pltpu.SemaphoreType.DMA((10,)),
        ],
        compiler_params=pltpu.CompilerParams(collective_id=1, has_side_effects=True),
        name="fold",
    )(grid)


def on_device(
    positions, occupancy, neighbours, edge_counts, atom_features, w_atom, w_radial, w_hidden, w_tensor, w_mix, w_out
):
    feats, prepared = halo_stage(
        occupancy.transpose(0, 2, 1),
        positions.reshape(3, CELLS, 16),
        atom_features.reshape(CELLS, 16, 128),
        neighbours.reshape(CELLS, 16, 64),
        edge_counts.reshape(CELLS, 16),
        w_atom, w_radial, w_hidden, w_tensor.T, w_mix, w_out.reshape(1, 128),
    )
    energy, forces = edge_stage(feats.reshape(GHOSTED, 16, 128), prepared, w_mix, w_hidden)
    forces = fold_stage(forces.reshape(EX, EY, EZ, 1, 128))
    return energy.reshape(CX, CY, CZ, 16), forces.reshape(3, CX, CY, CZ, 16)


def solution(mesh):
    cells = P("gx", "gy", "gz", None)
    placed = (
        P(None, "gx", "gy", "gz", None),
        P("gx", "gy", "gz"),
        P("gx", "gy", "gz", None, None),
        cells,
        P("gx", "gy", "gz", None, None),
        P(), P(), P(), P(), P(), P(),
    )
    return jax.shard_map(
        on_device,
        mesh=mesh,
        in_specs=placed,
        out_specs=(cells, P(None, "gx", "gy", "gz", None)),
        check_vma=False,
    )
```

```python
import numpy as np
import jax
import jax.numpy as jnp
from jax import lax
from jax.experimental import pallas as pl
from jax.experimental.pallas import tpu as pltpu
from jax.sharding import PartitionSpec as P

F32 = jnp.float32
BF = jnp.bfloat16
I32 = jnp.int32
root_three = 1.7320508075688772
L = 256
G = 8
CX, CY, CZ = 4, 4, 2
EX, EY, EZ = CX + 2, CY + 2, CZ + 2
CELLS = CX * CY * CZ
GHOSTED = EX * EY * EZ
MAXCH = CELLS * (1024 // L)


def nn(a, b):
    return lax.dot_general(a, b, (((1,), (0,)), ((), ())), preferred_element_type=F32)


def nt(a, b):
    return lax.dot_general(a, b, (((1,), (1,)), ((), ())), preferred_element_type=F32)


def tn(a, b):
    return lax.dot_general(a, b, (((0,), (0,)), ((), ())), preferred_element_type=F32)


def iota(shape, dim, dtype=I32):
    return lax.broadcasted_iota(I32, shape, dim).astype(dtype)


def onoff(mask):
    return jnp.where(mask, 1.0, 0.0).astype(F32)


def eye(n, m):
    return onoff(iota((n, m), 0) == iota((n, m), 1)).astype(BF)


def place_of(c):
    return c // (CY * CZ), c // CZ % CY, c % CZ


def ext_at(x, y, z):
    return (x * EY + y) * EZ + z


def prepare_weights(w_atom, w_rad, w_hid, w_ten_t, w_mix, w_out, mats, wout_r, wout_b):
    ident = eye(128, 128)
    half = 0.5
    mats[0] = (half * w_atom[...].astype(F32)).astype(BF)
    mats[1] = (half * nt(ident, w_hid[...])).astype(BF)
    mats[2] = (half * nt(ident, w_mix[0:128, :])).astype(BF)
    rad = jnp.concatenate([jnp.zeros((48, 128), F32), w_rad[...].astype(F32), jnp.zeros((72, 128), F32)], axis=0)
    mats[3] = (half * rad).astype(BF)
    wout_r[...] = w_out[...] * jnp.ones((8, 128), F32)
    wout_b[...] = jnp.sum(
        jnp.where(iota((128, 128), 0) == iota((128, 128), 1), w_out[...], 0.0), axis=1, keepdims=True
    ) * jnp.ones((128, 128), F32)
    tail = w_mix[128:224, :]
    for l in range(3):
        sel = onoff(iota((96, 32), 0) == 3 * iota((96, 32), 1) + l).astype(BF)
        spread = nt(ident, nn(sel, w_ten_t[...]).astype(BF)).astype(BF)
        mats[4 + l] = (0.0625 * nn(spread, tail)).astype(BF)


def prepare_edges(rows, rows2, occ_sp, neigh, counts, rank_out, code_out, rt_out, list_out):
    for x in range(EX):
        for y in range(EY):
            for z in range(EZ):
                at = ext_at(x, y, z)
                rows2[at : at + 1, :] = rows[x, y, z]
    occ_sp[...] = nn(rows2[...].astype(BF), onoff(iota((128, 128), 0) == 48).astype(BF))
    counts_t = nt(eye(16, 16), counts[...].astype(F32).astype(BF))
    lane64 = iota((8, 128), 1)
    low = lane64 < 64
    k_of = jnp.where(low, lane64, lane64 - 64).astype(F32)
    s_of = jnp.where(low, iota((8, 128), 0), iota((8, 128), 0) + 8)
    s_f = s_of.astype(F32)
    masks = []
    for c in range(CELLS):
        x, y, z = place_of(c)
        nb = jnp.concatenate([neigh[c, 0:8, :], neigh[c, 8:16, :]], axis=1)
        code_out[c] = nb
        cnt = jnp.where(low, counts_t[0:8, c : c + 1], counts_t[8:16, c : c + 1])
        code = lax.shift_right_logical(nb, 4)
        slot = lax.bitwise_and(nb, 15).astype(F32)
        occ_n = jnp.zeros((8, 128), F32)
        for k in range(27):
            at = ext_at(x + k // 9, y + k // 3 % 3, z + k % 3)
            occ_n = jnp.where(code == k, occ_sp[at : at + 1, :], occ_n)
        at = ext_at(x + 1, y + 1, z + 1)
        live = (k_of < cnt) & (slot < occ_n) & (s_f < occ_sp[at : at + 1, :]) & (nb != 208 + s_of)
        masks.append(onoff(live))
    mask = jnp.concatenate(masks, axis=0)
    mask_b = mask.astype(BF)
    upto = nn(mask_b, onoff(iota((128, 128), 0) <= iota((128, 128), 1)).astype(BF))
    total = nn(mask_b, jnp.ones((128, 128), BF))
    ri, ci = iota((256, 256), 0), iota((256, 256), 1)
    before = onoff((lax.shift_right_logical(ri, 3) == lax.shift_right_logical(ci, 3)) & (ci < ri)).astype(BF)
    base = nn(before, total.astype(BF))
    rank_out[...] = jnp.where(mask > 0.5, upto - 1.0 + base, -1.0).astype(I32).reshape(CELLS, 8, 128)
    n = (base + total).reshape(CELLS, 8, 128)[:, 7, :].astype(I32)
    chunks = lax.shift_right_logical(n + (L - 1), L.bit_length() - 1).astype(F32)
    ends = nn(onoff(iota((CELLS, CELLS), 1) <= iota((CELLS, CELLS), 0)).astype(BF), chunks.astype(BF))
    t = iota((CELLS, 128), 1, F32)
    done = ends <= t
    cell = jnp.minimum(jnp.sum(onoff(done), axis=0, keepdims=True), CELLS - 1.0)
    start = jnp.max(jnp.where(done, ends, 0.0), axis=0, keepdims=True)
    all_of = ends[CELLS - 1 : CELLS]
    first = jnp.where(t[0:1] < all_of, (t[0:1] - start) * L, 4096.0)
    list_out[...] = jnp.concatenate([cell, first, all_of, jnp.zeros((5, 128), F32)], axis=0).astype(I32)

    lane = iota((32, 128), 1)
    code_i = iota((32, 128), 0)
    ca = code_i // 9
    cb = code_i // 3 - 3 * ca
    cc = code_i - 3 * (code_i // 3)
    coord = lax.shift_right_logical(lane, 4)
    step = jnp.where(coord == 0, ca, jnp.where(coord == 1, cb, jnp.where(coord == 2, cc, 1))) - 1
    shift = 5.0 * step.astype(F32)
    pick = eye(48, 128)
    for c in range(CELLS):
        x, y, z = place_of(c)
        parts = []
        for k in range(0, 27, 3):
            at = ext_at(x + k // 9, y + k // 3 % 3, z)
            parts.append(rows2[at : at + 3, :])
        parts.append(jnp.zeros((5, 128), F32))
        r27 = jnp.concatenate(parts, axis=0) + shift
        hi = r27.astype(BF)
        rest = r27 - hi.astype(F32)
        mid = rest.astype(BF)
        lo = (rest - mid.astype(F32)).astype(BF)
        cat = jnp.concatenate([hi, mid, lo, jnp.zeros((32, 128), BF)], axis=0)
        rt_out[c] = nt(pick, cat).astype(BF)


def silu_both(h):
    t = jnp.tanh(h)
    a = 1.0 + t
    y = h * a
    return y, a + y * (1.0 - t)


def wide16(v):
    return jnp.broadcast_to(v, (16, 128)).astype(BF)


def rows16(v):
    return jnp.broadcast_to(v, (16, v.shape[1])).astype(BF)


def weave(tasks):
    active = list(tasks)
    while active:
        active = [task for task in active if next(task, None) is not None]


RX, RY, RZ, LIVE, CODE, SLOT, WHO, WEIGHT, EPS = range(9)


def edge_kernel(
    list_s, feats, rank_r, code_r, rt_r, mats, wout_r, wout_b, w_mix, w_hid, fold, foldc,
    energy_out, force_out,
    proj_sc, q_sc, dm_sc, m_sc, dq_sc, f_sc, en_sc, sec_sc, d1_sc, d2_sc, g_sc, ys_sc, geo_sc, y_sc, red_sc, gr_sc,
):
    groups = lax.div(list_s[2, 0] + (G - 1), G)
    ident = eye(128, 128)
    q_sc[...] = jnp.zeros_like(q_sc)
    dm_sc[...] = jnp.zeros_like(dm_sc)
    f_sc[...] = jnp.zeros_like(f_sc)
    en_sc[...] = jnp.zeros_like(en_sc)
    sub16 = iota((16, L), 0, F32)
    proj_sc[...] = nn(feats[...].reshape(GHOSTED * 16, 128), mats[0]).astype(BF).reshape(GHOSTED, 16, 128)
    zero = jnp.zeros((16, L), BF)
    centres = 0.5 + 2.0 * iota((8, L), 0, F32)

    def ids_of(gi):
        ids = [gi * G + i for i in range(G)]
        return ids, [list_s[0, i] for i in ids]

    def sphere(gi):
        rx, ry, rz = geo_sc[gi, RX], geo_sc[gi, RY], geo_sc[gi, RZ]
        d2 = rx * rx + ry * ry + rz * rz + 0.01
        inv = lax.rsqrt(d2)
        return rx, ry, rz, d2, inv, d2 * inv, rx * inv, ry * inv, rz * inv

    def front(gi, _):
        ids, cells = ids_of(gi)
        sixteen = iota((16, 128), 0, F32).astype(BF)
        lane_l = iota((16, L), 1)
        unfold = onoff(lax.bitwise_and(lane_l, 15) == iota((16, L), 0)).astype(BF)
        in_high = lax.shift_right_logical(lane_l, 4) == iota((16, L), 0)
        s_lane = iota((1, 128), 1)
        ones = jnp.ones((16, 128), BF)
        zeros = jnp.zeros((16, 128), BF)

        def find(j, i, c):
            rk = rank_r[c] - list_s[1, i]
            inside = (rk >= 0) & (rk < L)
            high = jnp.where(inside, lax.shift_right_logical(rk, 4), -1).astype(F32)
            deep = lax.bitwise_and(rk, 15).astype(F32)
            nb = code_r[c]
            code_f = lax.shift_right_logical(nb, 4).astype(F32)
            slot_f = lax.bitwise_and(nb, 15).astype(F32)
            left, right = [], []
            for k in range(8):
                s_row = jnp.where(s_lane < 64, float(k), float(k + 8))
                at_high = jnp.where(sixteen == wide16(high[k : k + 1]), ones, zeros)
                left.append(
                    jnp.concatenate(
                        [at_high * wide16(v) for v in (code_f[k : k + 1], slot_f[k : k + 1], s_row)] + [at_high], axis=0
                    )
                )
                right.append(jnp.where(sixteen == wide16(deep[k : k + 1]), ones, zeros))
            packed = nt(jnp.concatenate(left, axis=1), jnp.concatenate(right, axis=1))
            yield 1
            spread = nn(packed.astype(BF), unfold)
            yield 1
            code, slot, s, live = [
                jnp.sum(jnp.where(in_high, spread[16 * a : 16 * a + 16], 0.0), axis=0, keepdims=True) for a in range(4)
            ]
            oh27 = onoff(code == iota((32, L), 0, F32)).astype(BF)
            rt = rt_r[c]
            got = nn(rt, jnp.concatenate([oh27, oh27, oh27, jnp.zeros((32, L), BF)], axis=0))
            for q, v in ((LIVE, live), (CODE, code), (SLOT, slot), (WHO, s)):
                geo_sc[gi, q, j : j + 1, :] = v
            yield 1
            m_slot = slot == sub16
            m_s = s == sub16
            rtf = rt.astype(F32)
            centre = rtf[:, 13:14] + (rtf[:, 45:46] + rtf[:, 77:78])
            for d in range(3):
                sl = slice(16 * d, 16 * d + 16)
                geo_sc[gi, d, j : j + 1, :] = jnp.sum(
                    jnp.where(m_slot, got[sl], 0.0) - jnp.where(m_s, centre[sl], 0.0), axis=0, keepdims=True
                )

        weave(find(j, i, c) for j, (i, c) in enumerate(zip(ids, cells)))
        rx, ry, rz, d2, inv, dist, nx, ny, nz = sphere(gi)
        u = jnp.maximum(1.0 - d2 * (1.0 / 144.0), 0.0)
        geo_sc[gi, WEIGHT] = geo_sc[gi, LIVE] * (u * u)
        y_sc[0] = dist
        y_sc[1] = nx
        y_sc[2] = ny
        y_sc[3] = nz
        y_sc[4] = root_three * nx * ny
        y_sc[5] = root_three * ny * nz
        y_sc[6] = 0.5 * (3.0 * nz * nz - 1.0)
        y_sc[7] = root_three * nx * nz
        y_sc[8] = (0.5 * root_three) * (nx * nx - ny * ny)

        def layers(j, i, c):
            x = lax.div(c, CY * CZ)
            rest = c - x * (CY * CZ)
            y = lax.div(rest, CZ)
            z = rest - y * CZ
            parts = [
                proj_sc[pl.ds(((x + k // 3) * EY + y + k % 3) * EZ + z, 3)].reshape(48, 128) for k in range(9)
            ]
            parts.append(mats[3, 48:64, :])
            tab = jnp.concatenate(parts, axis=0)
            code, slot, s = [geo_sc[gi, q, j : j + 1, :] for q in (CODE, SLOT, WHO)]
            arg = (y_sc[0, j : j + 1, :] - centres) * 0.5
            basis = jnp.exp(-(arg * arg))
            slot01 = onoff(slot == sub16).astype(BF)
            s01 = onoff(s == sub16).astype(BF)
            code16 = rows16(code)
            tiles = [jnp.where(code16 == float(k), slot01, zero) for k in range(27)]
            tiles[13] = tiles[13] + s01
            tiles.append(jnp.concatenate([basis, jnp.zeros((8, L), F32)], axis=0).astype(BF))
            pre = tn(tab, jnp.concatenate(tiles, axis=0))
            yield 1
            f, d1 = silu_both(pre)
            d1_sc[i] = d1.astype(BF)
            hidden = nn(mats[1], f.astype(BF))
            yield 1
            ys = jnp.concatenate([s01] + [s01 * rows16(y_sc[m, j : j + 1, :]) for m in range(1, 9)], axis=0)
            ys_sc[i] = ys
            sec, d2 = silu_both(hidden)
            d2_sc[i] = d2.astype(BF)
            sb = sec.astype(BF)
            sec_sc[i] = sb
            w16 = rows16(geo_sc[gi, WEIGHT, j : j + 1, :])
            q = nt(ys * jnp.concatenate([w16] * 9, axis=0), sb)
            yield 1
            q_sc[:, c] = q_sc[:, c] + q.reshape(9, 16, 128)

        weave(layers(j, i, c) for j, (i, c) in enumerate(zip(ids, cells)))
        return 0

    lax.fori_loop(0, groups, front, 0)

    for m in range(9):
        l = 0 if m == 0 else 1 if m < 4 else 2
        m_sc[m] = nn(q_sc[m].reshape(CELLS * 16, 128).astype(BF), mats[4 + l]).astype(BF).reshape(CELLS, 16, 128)

    def middle(gi, _):
        ids, cells = ids_of(gi)
        wout = jnp.concatenate([wout_b[...]] * (L // 128), axis=1)
        wout_h = 0.5 * wout
        row = iota((16, 128), 0)
        w_hi = wout_r[0:1, :].astype(BF).astype(F32)
        w_rows = jnp.where(row == 0, w_hi, jnp.where(row == 1, wout_r[0:1, :] - w_hi, 0.0)).astype(BF)

        def mix(j, i, c):
            mt = nt(ident, m_sc[:, c].reshape(144, 128)).astype(BF)
            yield 1
            ys = ys_sc[i]
            p = nn(mats[2], sec_sc[i]) + nn(mt, ys)
            yield 1
            w = geo_sc[gi, WEIGHT, j : j + 1, :]
            mixed, d = silu_both(p)
            g = (d * wout_h).astype(BF)
            g_sc[i] = g
            energies = nn(w_rows, mixed.astype(BF))
            dm = nt(ys * jnp.concatenate([rows16(w)] * 9, axis=0), g)
            yield 1
            eps = energies[0:1] + energies[1:2]
            geo_sc[gi, EPS, j : j + 1, :] = eps
            we = eps * w
            hi = we.astype(BF).astype(F32)
            en = nt(jnp.where(iota((16, L), 0) == 0, hi, jnp.where(iota((16, L), 0) == 1, we - hi, 0.0)).astype(BF), ys[0:16])
            dm_sc[:, c] = dm_sc[:, c] + dm.reshape(9, 16, 128)
            yield 1
            en_sc[c] = en_sc[c] + en[0:8]

        weave(mix(j, i, c) for j, (i, c) in enumerate(zip(ids, cells)))
        return 0

    lax.fori_loop(0, groups, middle, 0)

    for m in range(9):
        l = 0 if m == 0 else 1 if m < 4 else 2
        dq_sc[m] = nt(dm_sc[m].reshape(CELLS * 16, 128).astype(BF), mats[4 + l]).astype(BF).reshape(CELLS, 16, 128)

    def back(gi, _):
        ids, cells = ids_of(gi)
        top = jnp.concatenate([w_mix[0:128, :], jnp.zeros((128, 128), BF)], axis=1)
        col, row = iota((16, 256), 1), iota((16, 256), 0)
        part = jnp.where(col < 128, 0, lax.shift_right_logical(col - 128, 4) + 1)
        gather = onoff(part == row).astype(BF)
        rx, ry, rz, d2, inv, dist, nx, ny, nz = sphere(gi)
        y_sc[0] = dist

        def undo(j, i, c):
            dq = dq_sc[:, c].reshape(144, 128)
            dqt = nt(ident, dq).astype(BF)
            yield 1
            t = nn(dqt, ys_sc[i])
            sb = sec_sc[i]
            low = jnp.concatenate([m_sc[1:9, c].reshape(128, 128), dq[16:144]], axis=1)
            both = nn(jnp.concatenate([top, low], axis=0), jnp.concatenate([g_sc[i], sb], axis=0))
            yield 1
            t2 = t + t
            dsec = both[0:128] + t2
            dfirst = nn(w_hid[...], dsec.astype(BF) * d2_sc[i])
            s01 = onoff(geo_sc[gi, WHO, j : j + 1, :] == sub16).astype(BF)
            sums = nn(
                gather,
                jnp.concatenate([t2.astype(BF) * sb, both[128:256].astype(BF) * jnp.concatenate([s01] * 8, axis=0)], axis=0),
            )
            yield 1
            for m in range(9):
                red_sc[m, j : j + 1, :] = sums[m : m + 1]
            dbasis = nn(mats[3, 48:64, :], dfirst.astype(BF) * d1_sc[i])[0:8]
            yield 1
            arg = (y_sc[0, j : j + 1, :] - centres) * 0.5
            red_sc[9, j : j + 1, :] = jnp.sum(dbasis * jnp.exp(-(arg * arg)) * arg, axis=0, keepdims=True)

        weave(undo(j, i, c) for j, (i, c) in enumerate(zip(ids, cells)))
        w = geo_sc[gi, WEIGHT]
        w2 = w + w
        dw = geo_sc[gi, EPS] + red_sc[0]
        y1, y2, y3, y4, y5, y6, y7, y8 = [red_sc[m] * w2 for m in range(1, 9)]
        ax = y1 + root_three * (ny * y4 + nz * y7 + nx * y8)
        ay = y2 + root_three * (nx * y4 + nz * y5 - ny * y8)
        az = y3 + root_three * (ny * y5 + nx * y7) + 3.0 * nz * y6
        dd = red_sc[9] * (-0.5 * w) - (ax * nx + ay * ny + az * nz) * inv
        u = jnp.maximum(1.0 - d2 * (1.0 / 144.0), 0.0)
        radial = dd * inv + dw * geo_sc[gi, LIVE] * u * (-4.0 / 144.0)
        gr_sc[0] = ax * inv + rx * radial
        gr_sc[1] = ay * inv + ry * radial
        gr_sc[2] = az * inv + rz * radial
        where32 = iota((32, L), 0, F32)

        def scatter(j, i, c):
            code, slot, s = [geo_sc[gi, q, j : j + 1, :] for q in (CODE, SLOT, WHO)]
            slot01 = onoff(slot == sub16).astype(BF)
            s01 = onoff(s == sub16).astype(BF)
            g16 = [rows16(gr_sc[d, j : j + 1, :]) for d in range(3)]
            parts = [slot01 * -v for v in g16] + [zero] + [s01 * v for v in g16] + [zero]
            oh = onoff((code == where32) | (where32 == 27.0)).astype(BF)
            add = nt(oh, jnp.concatenate(parts, axis=0))
            yield 1
            f_sc[c] = f_sc[c] + add

        weave(scatter(j, i, c) for j, (i, c) in enumerate(zip(ids, cells)))
        return 0

    lax.fori_loop(0, groups, back, 0)

    fa = f_sc[...].reshape(CELLS * 32, 128)
    fh = fa.astype(BF)
    fl = (fa - fh.astype(F32)).astype(BF)
    others = nn(fold[...], fh) + nn(fold[...], fl)
    own = nn(foldc[...], fh) + nn(foldc[...], fl)
    force_out[...] = others + jnp.concatenate([own[:, 64:128], jnp.zeros((GHOSTED, 64), F32)], axis=1)
    energy_out[...] = en_sc[:, 0, :] + en_sc[:, 1, :]


def fold_matrices():
    m = np.zeros((2, GHOSTED, CELLS * 32), np.float32)
    for c in range(CELLS):
        x, y, z = place_of(c)
        for k in range(27):
            m[0, ext_at(x + k // 9, y + k // 3 % 3, z + k % 3), c * 32 + k] = 1
        m[1, ext_at(x + 1, y + 1, z + 1), c * 32 + 27] = 1
    return m


PREPARED = (
    jax.ShapeDtypeStruct((CELLS, 8, 128), I32),
    jax.ShapeDtypeStruct((CELLS, 8, 128), I32),
    jax.ShapeDtypeStruct((CELLS, 48, 128), BF),
    jax.ShapeDtypeStruct((8, 128), I32),
    jax.ShapeDtypeStruct((7, 128, 128), BF),
    jax.ShapeDtypeStruct((8, 128), F32),
    jax.ShapeDtypeStruct((128, 128), F32),
)


def edge_stage(feats, prepared, w_mix, w_hid):
    rank, code, rt, todo, mats, wout_r, wout_b = prepared
    V = pltpu.VMEM
    vm = pl.BlockSpec(memory_space=pltpu.VMEM)
    folds = fold_matrices()
    return pl.pallas_call(
        edge_kernel,
        out_shape=(jax.ShapeDtypeStruct((CELLS, 16), F32), jax.ShapeDtypeStruct((GHOSTED, 128), F32)),
        in_specs=[pl.BlockSpec(memory_space=pltpu.SMEM)] + [vm] * 11,
        out_specs=(vm, vm),
        scratch_shapes=[
            V((GHOSTED, 16, 128), BF),
            V((9, CELLS, 16, 128), F32),
            V((9, CELLS, 16, 128), F32),
            V((9, CELLS, 16, 128), BF),
            V((9, CELLS, 16, 128), BF),
            V((CELLS, 32, 128), F32),
            V((CELLS, 8, 16), F32),
            V((MAXCH, 128, L), BF),
            V((MAXCH, 128, L), BF),
            V((MAXCH, 128, L), BF),
            V((MAXCH, 128, L), BF),
            V((MAXCH, 144, L), BF),
            V((MAXCH // G, 9, G, L), F32),
            V((9, G, L), F32),
            V((10, G, L), F32),
            V((3, G, L), F32),
        ],
        compiler_params=pltpu.CompilerParams(vmem_limit_bytes=60 * 1024 * 1024),
        name="edges",
    )(todo, feats, rank, code, rt, mats, wout_r, wout_b, w_mix, w_hid, jnp.asarray(folds[0], BF), jnp.asarray(folds[1], BF))


MESH = pl.DeviceIdType.MESH
AROUND = tuple((dx, dy) for dx in (-1, 0, 1) for dy in (-1, 0, 1) if (dx, dy) != (0, 0))


def peer(dx, dy, dz):
    there = {}
    for axis, step in (("gx", dx), ("gy", dy), ("gz", dz)):
        size = lax.axis_size(axis)
        there[axis] = lax.rem(lax.axis_index(axis) + (step + size), size)
    return there


def greet():
    barrier = pltpu.get_barrier_semaphore()
    for dx, dy, dz in [(0, 0, -1), (0, 0, 1)] + [(dx, dy, 0) for dx, dy in AROUND]:
        pl.semaphore_signal(barrier, inc=1, device_id=peer(dx, dy, dz), device_id_type=MESH)
    return barrier


def sent(src, dst, send, recv, there):
    copy = pltpu.make_async_remote_copy(
        src_ref=src, dst_ref=dst, send_sem=send, recv_sem=recv, device_id=there, device_id_type=MESH
    )
    copy.start()
    return copy


def border(step, n):
    return pl.ds(1, n) if step == 0 else pl.ds(1 if step < 0 else n, 1)


def ghost(step, n):
    return pl.ds(1, n) if step == 0 else pl.ds(n + 1 if step < 0 else 0, 1)


def halo_kernel(
    occ_s, pos, feat, neigh, counts, w_atom, w_rad, w_hid, w_ten_t, w_mix, w_out,
    feat_ext, rank, code, rt, todo, mats, wout_r, wout_b,
    rows, rows2, occ_sp, send, recv,
):
    barrier = greet()
    table = jnp.concatenate([pos[0], pos[1], pos[2], jnp.zeros((CELLS, 80), F32)], axis=1)
    lane = iota((1, 128), 1)
    for c in range(CELLS):
        x, y, z = place_of(c)
        rows[x + 1, y + 1, z + 1] = jnp.where(lane < 48, table[c : c + 1], occ_s[x, z, y].astype(F32))
        feat_ext[x + 1, y + 1, z + 1] = feat[c]
    pl.semaphore_wait(barrier, 10)

    def along_z(array, base):
        copies = []
        for j, step in enumerate((-1, 1)):
            at = (pl.ds(1, CX), pl.ds(1, CY))
            src = array.at[at + (border(step, CZ),)]
            dst = array.at[at + (ghost(step, CZ),)]
            copies.append(sent(src, dst, send.at[base + j], recv.at[base + j], peer(0, 0, step)))
        return copies

    def around(array, base):
        copies = []
        for j, (dx, dy) in enumerate(AROUND):
            src = array.at[border(dx, CX), border(dy, CY)]
            dst = array.at[ghost(dx, CX), ghost(dy, CY)]
            copies.append(sent(src, dst, send.at[base + j], recv.at[base + j], peer(dx, dy, 0)))
        return copies

    rows_z = along_z(rows, 0)
    feat_z = along_z(feat_ext, 2)
    for copy in rows_z:
        copy.wait()
    rows_xy = around(rows, 4)
    for copy in feat_z:
        copy.wait()
    feat_xy = around(feat_ext, 12)
    prepare_weights(w_atom, w_rad, w_hid, w_ten_t, w_mix, w_out, mats, wout_r, wout_b)
    for copy in rows_xy:
        copy.wait()
    prepare_edges(rows, rows2, occ_sp, neigh, counts, rank, code, rt, todo)
    for copy in feat_xy:
        copy.wait()


def halo_stage(occ, pos, feat, neigh, counts, w_atom, w_rad, w_hid, w_ten_t, w_mix, w_out):
    vm = pl.BlockSpec(memory_space=pltpu.VMEM)
    V = pltpu.VMEM
    out = pl.pallas_call(
        halo_kernel,
        out_shape=(jax.ShapeDtypeStruct((EX, EY, EZ, 16, 128), BF),) + PREPARED,
        in_specs=[pl.BlockSpec(memory_space=pltpu.SMEM)] + [vm] * 10,
        out_specs=(vm,) * 8,
        scratch_shapes=[
            V((EX, EY, EZ, 1, 128), F32),
            V((GHOSTED, 128), F32),
            V((GHOSTED, 128), F32),
            pltpu.SemaphoreType.DMA((20,)),
            pltpu.SemaphoreType.DMA((20,)),
        ],
        compiler_params=pltpu.CompilerParams(
            collective_id=0, has_side_effects=True, vmem_limit_bytes=60 * 1024 * 1024
        ),
        name="halo",
    )(occ, pos, feat, neigh, counts, w_atom, w_rad, w_hid, w_ten_t, w_mix, w_out)
    return out[0], out[1:]


def fold_kernel(grid, out, acc, got_x, got_y, got_xy, got_z, send, recv):
    barrier = greet()
    acc[...] = grid[...]
    pl.semaphore_wait(barrier, 10)
    copies = []
    for j, (dx, dy) in enumerate(AROUND):
        if dx and dy:
            got = got_xy.at[(dx + 1) + (dy + 1) // 2]
        elif dx:
            got = got_x.at[(dx + 1) // 2]
        else:
            got = got_y.at[(dy + 1) // 2]
        rim = (
            pl.ds(1, CX) if dx == 0 else pl.ds(0 if dx < 0 else CX + 1, 1),
            pl.ds(1, CY) if dy == 0 else pl.ds(0 if dy < 0 else CY + 1, 1),
        )
        copies.append((sent(acc.at[rim], got, send.at[j], recv.at[j], peer(dx, dy, 0)), got, dx, dy))
    for copy, got, dx, dy in copies:
        copy.wait()
        at = (border(-dx, CX), border(-dy, CY))
        acc[at] = acc[at] + got[...]
    inner = (pl.ds(1, CX), pl.ds(1, CY))
    copies = []
    for j, (step, rim) in enumerate(((-1, 0), (1, CZ + 1))):
        copies.append(
            sent(acc.at[inner + (pl.ds(rim, 1),)], got_z.at[j], send.at[8 + j], recv.at[8 + j], peer(0, 0, step))
        )
    for j, step in enumerate((-1, 1)):
        copies[j].wait()
        at = inner + (border(-step, CZ),)
        acc[at] = acc[at] + got_z[j]
    lines = []
    for c in range(CELLS):
        x, y, z = place_of(c)
        lines.append(acc[x + 1, y + 1, z + 1])
    lines = jnp.concatenate(lines, axis=0)
    for d in range(3):
        out[d] = lines[:, 16 * d : 16 * d + 16]


def fold_stage(grid):
    vm = pl.BlockSpec(memory_space=pltpu.VMEM)
    V = pltpu.VMEM
    return pl.pallas_call(
        fold_kernel,
        out_shape=jax.ShapeDtypeStruct((3, CELLS, 16), F32),
        in_specs=[vm],
        out_specs=vm,
        scratch_shapes=[
            V((EX, EY, EZ, 1, 128), F32),
            V((2, 1, CY, EZ, 1, 128), F32),
            V((2, CX, 1, EZ, 1, 128), F32),
            V((4, 1, 1, EZ, 1, 128), F32),
            V((2, CX, CY, 1, 1, 128), F32),
            pltpu.SemaphoreType.DMA((10,)),
            pltpu.SemaphoreType.DMA((10,)),
        ],
        compiler_params=pltpu.CompilerParams(collective_id=1, has_side_effects=True, vmem_limit_bytes=60 * 1024 * 1024),
        name="fold",
    )(grid)


def on_device(
    positions, occupancy, neighbours, edge_counts, atom_features, w_atom, w_radial, w_hidden, w_tensor, w_mix, w_out
):
    feats, prepared = halo_stage(
        occupancy.transpose(0, 2, 1),
        positions.reshape(3, CELLS, 16),
        atom_features.reshape(CELLS, 16, 128),
        neighbours.reshape(CELLS, 16, 64),
        edge_counts.reshape(CELLS, 16),
        w_atom, w_radial, w_hidden, w_tensor.T, w_mix, w_out.reshape(1, 128),
    )
    energy, forces = edge_stage(feats.reshape(GHOSTED, 16, 128), prepared, w_mix, w_hidden)
    forces = fold_stage(forces.reshape(EX, EY, EZ, 1, 128))
    return energy.reshape(CX, CY, CZ, 16), forces.reshape(3, CX, CY, CZ, 16)


def solution(mesh):
    cells = P("gx", "gy", "gz", None)
    placed = (
        P(None, "gx", "gy", "gz", None),
        P("gx", "gy", "gz"),
        P("gx", "gy", "gz", None, None),
        cells,
        P("gx", "gy", "gz", None, None),
        P(), P(), P(), P(), P(), P(),
    )
    return jax.shard_map(
        on_device,
        mesh=mesh,
        in_specs=placed,
        out_specs=(cells, P(None, "gx", "gy", "gz", None)),
        check_vma=False,
    )
```

```python
import numpy as np
import jax
import jax.numpy as jnp
from jax import lax
from jax.experimental import pallas as pl
from jax.experimental.pallas import tpu as pltpu
from jax.sharding import PartitionSpec as P

F32 = jnp.float32
BF = jnp.bfloat16
I32 = jnp.int32
root_three = 1.7320508075688772
L = 256
G = 12
CX, CY, CZ = 4, 4, 2
EX, EY, EZ = CX + 2, CY + 2, CZ + 2
CELLS = CX * CY * CZ
GHOSTED = EX * EY * EZ
MAXGR = -(-CELLS * (1024 // L) // G)
MAXCH = MAXGR * G
LISTED = 256


def nn(a, b):
    return lax.dot_general(a, b, (((1,), (0,)), ((), ())), preferred_element_type=F32)


def nt(a, b):
    return lax.dot_general(a, b, (((1,), (1,)), ((), ())), preferred_element_type=F32)


def tn(a, b):
    return lax.dot_general(a, b, (((0,), (0,)), ((), ())), preferred_element_type=F32)


def iota(shape, dim, dtype=I32):
    return lax.broadcasted_iota(I32, shape, dim).astype(dtype)


def onoff(mask):
    return jnp.where(mask, 1.0, 0.0).astype(F32)


def eye(n, m):
    return onoff(iota((n, m), 0) == iota((n, m), 1)).astype(BF)


def place_of(c):
    return c // (CY * CZ), c // CZ % CY, c % CZ


def ext_at(x, y, z):
    return (x * EY + y) * EZ + z


def prepare_weights(w_atom, w_rad, w_hid, w_ten_t, w_mix, w_out, mats, wout_r, wout_b):
    ident = eye(128, 128)
    half = 0.5
    mats[0] = (half * w_atom[...].astype(F32)).astype(BF)
    mats[1] = (half * nt(ident, w_hid[...])).astype(BF)
    mats[2] = (half * nt(ident, w_mix[0:128, :])).astype(BF)
    rad = jnp.concatenate([jnp.zeros((48, 128), F32), w_rad[...].astype(F32), jnp.zeros((72, 128), F32)], axis=0)
    mats[3] = (half * rad).astype(BF)
    wout_r[...] = w_out[...] * jnp.ones((8, 128), F32)
    wout_b[...] = jnp.sum(
        jnp.where(iota((128, 128), 0) == iota((128, 128), 1), w_out[...], 0.0), axis=1, keepdims=True
    ) * jnp.ones((128, 128), F32)
    tail = w_mix[128:224, :]
    for l in range(3):
        sel = onoff(iota((96, 32), 0) == 3 * iota((96, 32), 1) + l).astype(BF)
        spread = nt(ident, nn(sel, w_ten_t[...]).astype(BF)).astype(BF)
        mats[4 + l] = (0.0625 * nn(spread, tail)).astype(BF)


def prepare_edges(rows, rows2, occ_sp, neigh, counts, rank_out, code_out, rt_out, list_out):
    for x in range(EX):
        for y in range(EY):
            for z in range(EZ):
                at = ext_at(x, y, z)
                rows2[at : at + 1, :] = rows[x, y, z]
    occ_sp[...] = nn(rows2[...].astype(BF), onoff(iota((128, 128), 0) == 48).astype(BF))
    counts_t = nt(eye(16, 16), counts[...].astype(F32).astype(BF))
    lane64 = iota((8, 128), 1)
    low = lane64 < 64
    k_of = jnp.where(low, lane64, lane64 - 64).astype(F32)
    s_of = jnp.where(low, iota((8, 128), 0), iota((8, 128), 0) + 8)
    s_f = s_of.astype(F32)
    masks = []
    for c in range(CELLS):
        x, y, z = place_of(c)
        nb = jnp.concatenate([neigh[c, 0:8, :], neigh[c, 8:16, :]], axis=1)
        code_out[c] = nb
        cnt = jnp.where(low, counts_t[0:8, c : c + 1], counts_t[8:16, c : c + 1])
        code = lax.shift_right_logical(nb, 4)
        slot = lax.bitwise_and(nb, 15).astype(F32)
        occ_n = jnp.zeros((8, 128), F32)
        for k in range(27):
            at = ext_at(x + k // 9, y + k // 3 % 3, z + k % 3)
            occ_n = jnp.where(code == k, occ_sp[at : at + 1, :], occ_n)
        at = ext_at(x + 1, y + 1, z + 1)
        live = (k_of < cnt) & (slot < occ_n) & (s_f < occ_sp[at : at + 1, :]) & (nb != 208 + s_of)
        masks.append(onoff(live))
    mask = jnp.concatenate(masks, axis=0)
    mask_b = mask.astype(BF)
    upto = nn(mask_b, onoff(iota((128, 128), 0) <= iota((128, 128), 1)).astype(BF))
    total = nn(mask_b, jnp.ones((128, 128), BF))
    ri, ci = iota((256, 256), 0), iota((256, 256), 1)
    before = onoff((lax.shift_right_logical(ri, 3) == lax.shift_right_logical(ci, 3)) & (ci < ri)).astype(BF)
    base = nn(before, total.astype(BF))
    rank_out[...] = jnp.where(mask > 0.5, upto - 1.0 + base, -1.0).astype(I32).reshape(CELLS, 8, 128)
    n = (base + total).reshape(CELLS, 8, 128)[:, 7, :].astype(I32)
    chunks = lax.shift_right_logical(n + (L - 1), L.bit_length() - 1).astype(F32)
    ends = nn(onoff(iota((CELLS, CELLS), 1) <= iota((CELLS, CELLS), 0)).astype(BF), chunks.astype(BF))
    ends = jnp.concatenate([ends] * (LISTED // 128), axis=1)
    t = iota((CELLS, LISTED), 1, F32)
    done = ends <= t
    cell = jnp.minimum(jnp.sum(onoff(done), axis=0, keepdims=True), CELLS - 1.0)
    start = jnp.max(jnp.where(done, ends, 0.0), axis=0, keepdims=True)
    all_of = ends[CELLS - 1 : CELLS]
    first = jnp.where(t[0:1] < all_of, (t[0:1] - start) * L, 4096.0)
    list_out[...] = jnp.concatenate([cell, first, all_of, jnp.zeros((5, LISTED), F32)], axis=0).astype(I32)

    lane = iota((32, 128), 1)
    code_i = iota((32, 128), 0)
    ca = code_i // 9
    cb = code_i // 3 - 3 * ca
    cc = code_i - 3 * (code_i // 3)
    coord = lax.shift_right_logical(lane, 4)
    step = jnp.where(coord == 0, ca, jnp.where(coord == 1, cb, jnp.where(coord == 2, cc, 1))) - 1
    shift = 5.0 * step.astype(F32)
    pick = eye(48, 128)
    for c in range(CELLS):
        x, y, z = place_of(c)
        parts = []
        for k in range(0, 27, 3):
            at = ext_at(x + k // 9, y + k // 3 % 3, z)
            parts.append(rows2[at : at + 3, :])
        parts.append(jnp.zeros((5, 128), F32))
        r27 = jnp.concatenate(parts, axis=0) + shift
        hi = r27.astype(BF)
        rest = r27 - hi.astype(F32)
        mid = rest.astype(BF)
        lo = (rest - mid.astype(F32)).astype(BF)
        cat = jnp.concatenate([hi, mid, lo, jnp.zeros((32, 128), BF)], axis=0)
        rt_out[c] = nt(pick, cat).astype(BF)


def silu_both(h):
    t = jnp.tanh(h)
    y = (h + h * t).astype(BF)
    t = t.astype(BF)
    return y, (1.0 + t) + y * (1.0 - t)


def wide16(v):
    return jnp.broadcast_to(v, (16, 128)).astype(BF)


def rows16(v):
    return jnp.broadcast_to(v, (16, v.shape[1])).astype(BF)


def weave(tasks):
    active = list(tasks)
    while active:
        active = [task for task in active if next(task, None) is not None]


RX, RY, RZ, LIVE, CODE, SLOT, WHO, WEIGHT, EPS = range(9)


def edge_kernel(
    list_s, feats, rank_r, code_r, rt_r, mats, wout_r, wout_b, w_mix, w_hid, fold_h,
    energy_out, force_out,
    proj_sc, q_sc, m_sc, dq_sc, f_sc, en_sc, sec_sc, d1_sc, d2_sc, g_sc, ys_sc, geo_sc, y_sc, red_sc, gr_sc,
    fold, fold_sem,
):
    fold_copy = pltpu.make_async_copy(fold_h, fold, fold_sem)
    fold_copy.start()
    groups = lax.div(list_s[2, 0] + (G - 1), G)
    ident = eye(128, 128)
    q_sc[...] = jnp.zeros_like(q_sc)
    f_sc[...] = jnp.zeros_like(f_sc)
    en_sc[...] = jnp.zeros_like(en_sc)
    sub16 = iota((16, L), 0, F32)
    proj_sc[...] = nn(feats[...].reshape(GHOSTED * 16, 128), mats[0]).astype(BF).reshape(GHOSTED, 16, 128)
    zero = jnp.zeros((16, L), BF)
    centres = 0.5 + 2.0 * iota((8, L), 0, F32)

    def ids_of(gi):
        ids = [gi * G + i for i in range(G)]
        return ids, [list_s[0, i] for i in ids]

    def sphere(gi):
        rx, ry, rz = geo_sc[gi, RX], geo_sc[gi, RY], geo_sc[gi, RZ]
        d2 = rx * rx + ry * ry + rz * rz + 0.01
        inv = lax.rsqrt(d2)
        return rx, ry, rz, d2, inv, d2 * inv, rx * inv, ry * inv, rz * inv

    def front(gi, _):
        ids, cells = ids_of(gi)
        sixteen = iota((16, 128), 0, F32).astype(BF)
        lane_l = iota((16, L), 1)
        unfold = onoff(lax.bitwise_and(lane_l, 15) == iota((16, L), 0)).astype(BF)
        in_high = lax.shift_right_logical(lane_l, 4) == iota((16, L), 0)
        lane8 = iota((8, 128), 1)
        s_of = jnp.where(lane8 < 64, iota((8, 128), 0), iota((8, 128), 0) + 8)
        ones = jnp.ones((16, 128), BF)
        zeros = jnp.zeros((16, 128), BF)

        def find(j, i, c):
            rk = rank_r[c] - list_s[1, i]
            inside = (rk >= 0) & (rk < L)
            high = jnp.where(inside, lax.shift_right_logical(rk, 4), -1).astype(F32)
            deep = lax.bitwise_and(rk, 15).astype(F32)
            nb = code_r[c]
            code_f = (lax.shift_right_logical(nb, 4) + 1).astype(F32)
            pair_f = (lax.bitwise_and(nb, 15) + 16 * s_of).astype(F32)
            left, right = [], []
            for k in range(8):
                at_high = jnp.where(sixteen == wide16(high[k : k + 1]), ones, zeros)
                left.append(
                    jnp.concatenate([at_high * wide16(code_f[k : k + 1]), at_high * wide16(pair_f[k : k + 1])], axis=0)
                )
                right.append(jnp.where(sixteen == wide16(deep[k : k + 1]), ones, zeros))
            packed = nt(jnp.concatenate(left, axis=1), jnp.concatenate(right, axis=1))
            yield 1
            spread = nn(packed.astype(BF), unfold)
            yield 1
            code1, pair = [
                jnp.sum(jnp.where(in_high, spread[16 * a : 16 * a + 16], 0.0), axis=0, keepdims=True) for a in range(2)
            ]
            live = jnp.minimum(code1, 1.0)
            code = code1 - live
            s = jnp.floor(pair * 0.0625)
            slot = pair - 16.0 * s
            oh27 = onoff(code == iota((32, L), 0, F32)).astype(BF)
            rt = rt_r[c]
            got = nn(rt, jnp.concatenate([oh27, oh27, oh27, jnp.zeros((32, L), BF)], axis=0))
            for q, v in ((LIVE, live), (CODE, code), (SLOT, slot), (WHO, s)):
                geo_sc[gi, q, j : j + 1, :] = v
            yield 1
            m_slot = slot == sub16
            m_s = s == sub16
            rtf = rt.astype(F32)
            centre = rtf[:, 13:14] + (rtf[:, 45:46] + rtf[:, 77:78])
            for d in range(3):
                sl = slice(16 * d, 16 * d + 16)
                geo_sc[gi, d, j : j + 1, :] = jnp.sum(
                    jnp.where(m_slot, got[sl], 0.0) - jnp.where(m_s, centre[sl], 0.0), axis=0, keepdims=True
                )

        weave(find(j, i, c) for j, (i, c) in enumerate(zip(ids, cells)))
        rx, ry, rz, d2, inv, dist, nx, ny, nz = sphere(gi)
        u = jnp.maximum(1.0 - d2 * (1.0 / 144.0), 0.0)
        geo_sc[gi, WEIGHT] = geo_sc[gi, LIVE] * (u * u)
        y_sc[0] = dist
        y_sc[1] = nx
        y_sc[2] = ny
        y_sc[3] = nz
        y_sc[4] = root_three * nx * ny
        y_sc[5] = root_three * ny * nz
        y_sc[6] = 0.5 * (3.0 * nz * nz - 1.0)
        y_sc[7] = root_three * nx * nz
        y_sc[8] = (0.5 * root_three) * (nx * nx - ny * ny)

        def layers(j, i, c):
            x = lax.div(c, CY * CZ)
            rest = c - x * (CY * CZ)
            y = lax.div(rest, CZ)
            z = rest - y * CZ
            parts = [
                proj_sc[pl.ds(((x + k // 3) * EY + y + k % 3) * EZ + z, 3)].reshape(48, 128) for k in range(9)
            ]
            parts.append(mats[3, 48:64, :])
            tab = jnp.concatenate(parts, axis=0)
            code, slot, s = [geo_sc[gi, q, j : j + 1, :] for q in (CODE, SLOT, WHO)]
            arg = (y_sc[0, j : j + 1, :] - centres) * 0.5
            basis = jnp.exp(-(arg * arg))
            slot01 = onoff(slot == sub16).astype(BF)
            s01 = onoff(s == sub16).astype(BF)
            code16 = rows16(code)
            tiles = [jnp.where(code16 == float(k), slot01, zero) for k in range(27)]
            tiles[13] = tiles[13] + s01
            tiles.append(jnp.concatenate([basis, jnp.zeros((8, L), F32)], axis=0).astype(BF))
            pre = tn(tab, jnp.concatenate(tiles, axis=0))
            yield 1
            f, d1 = silu_both(pre)
            d1_sc[i] = d1
            hidden = nn(mats[1], f)
            yield 1
            ys = jnp.concatenate([s01] + [s01 * rows16(y_sc[m, j : j + 1, :]) for m in range(1, 9)], axis=0)
            ys_sc[i] = ys[16:144]
            sb, d2 = silu_both(hidden)
            d2_sc[i] = d2
            sec_sc[i] = sb
            w16 = rows16(geo_sc[gi, WEIGHT, j : j + 1, :])
            q = nt(ys * jnp.concatenate([w16] * 9, axis=0), sb)
            yield 1
            q_sc[:, c] = q_sc[:, c] + q.reshape(9, 16, 128)

        weave(layers(j, i, c) for j, (i, c) in enumerate(zip(ids, cells)))
        return 0

    lax.fori_loop(0, groups, front, 0)

    for m in range(9):
        l = 0 if m == 0 else 1 if m < 4 else 2
        m_sc[m] = nn(q_sc[m].reshape(CELLS * 16, 128).astype(BF), mats[4 + l]).astype(BF).reshape(CELLS, 16, 128)
        q_sc[m] = jnp.zeros((CELLS, 16, 128), F32)

    def middle(gi, _):
        ids, cells = ids_of(gi)
        wout_h = jnp.concatenate([(0.5 * wout_b[...]).astype(BF)] * (L // 128), axis=1)
        row = iota((16, 128), 0)
        w_hi = wout_r[0:1, :].astype(BF).astype(F32)
        w_rows = jnp.where(row == 0, w_hi, jnp.where(row == 1, wout_r[0:1, :] - w_hi, 0.0)).astype(BF)

        def mix(j, i, c):
            s01 = onoff(geo_sc[gi, WHO, j : j + 1, :] == sub16).astype(BF)
            ys = jnp.concatenate([s01, ys_sc[i]], axis=0)
            p = nn(mats[2], sec_sc[i]) + tn(m_sc[:, c].reshape(144, 128), ys)
            yield 1
            w = geo_sc[gi, WEIGHT, j : j + 1, :]
            mixed, d = silu_both(p)
            g = d * wout_h
            g_sc[i] = g
            energies = nn(w_rows, mixed)
            dm = nt(ys * jnp.concatenate([rows16(w)] * 9, axis=0), g)
            yield 1
            eps = energies[0:1] + energies[1:2]
            geo_sc[gi, EPS, j : j + 1, :] = eps
            we = eps * w
            hi = we.astype(BF).astype(F32)
            en = nt(jnp.where(iota((16, L), 0) == 0, hi, jnp.where(iota((16, L), 0) == 1, we - hi, 0.0)).astype(BF), ys[0:16])
            q_sc[:, c] = q_sc[:, c] + dm.reshape(9, 16, 128)
            yield 1
            en_sc[c] = en_sc[c] + en[0:8]

        weave(mix(j, i, c) for j, (i, c) in enumerate(zip(ids, cells)))
        return 0

    lax.fori_loop(0, groups, middle, 0)

    for m in range(9):
        l = 0 if m == 0 else 1 if m < 4 else 2
        dq_sc[m] = nt(q_sc[m].reshape(CELLS * 16, 128).astype(BF), mats[4 + l]).astype(BF).reshape(CELLS, 16, 128)

    def back(gi, _):
        ids, cells = ids_of(gi)
        top = jnp.concatenate([w_mix[0:128, :], jnp.zeros((128, 128), BF)], axis=1)
        col, row = iota((16, 256), 1), iota((16, 256), 0)
        part = jnp.where(col < 128, 0, lax.shift_right_logical(col - 128, 4) + 1)
        gather = onoff(part == row).astype(BF)
        rx, ry, rz, d2, inv, dist, nx, ny, nz = sphere(gi)
        y_sc[0] = dist

        def undo(j, i, c):
            dq = dq_sc[:, c].reshape(144, 128)
            s01 = onoff(geo_sc[gi, WHO, j : j + 1, :] == sub16).astype(BF)
            t = tn(dq, jnp.concatenate([s01, ys_sc[i]], axis=0))
            sb = sec_sc[i]
            low = jnp.concatenate([m_sc[1:9, c].reshape(128, 128), dq[16:144]], axis=1)
            both = nn(jnp.concatenate([top, low], axis=0), jnp.concatenate([g_sc[i], sb], axis=0))
            yield 1
            t2 = t + t
            dsec = both[0:128] + t2
            dfirst = nn(w_hid[...], dsec.astype(BF) * d2_sc[i])
            sums = nn(
                gather,
                jnp.concatenate([t2.astype(BF) * sb, both[128:256].astype(BF) * jnp.concatenate([s01] * 8, axis=0)], axis=0),
            )
            yield 1
            for m in range(9):
                red_sc[m, j : j + 1, :] = sums[m : m + 1]
            dbasis = nn(mats[3, 48:64, :], dfirst.astype(BF) * d1_sc[i])[0:8]
            yield 1
            arg = (y_sc[0, j : j + 1, :] - centres) * 0.5
            red_sc[9, j : j + 1, :] = jnp.sum(dbasis * jnp.exp(-(arg * arg)) * arg, axis=0, keepdims=True)

        weave(undo(j, i, c) for j, (i, c) in enumerate(zip(ids, cells)))
        w = geo_sc[gi, WEIGHT]
        w2 = w + w
        dw = geo_sc[gi, EPS] + red_sc[0]
        y1, y2, y3, y4, y5, y6, y7, y8 = [red_sc[m] * w2 for m in range(1, 9)]
        ax = y1 + root_three * (ny * y4 + nz * y7 + nx * y8)
        ay = y2 + root_three * (nx * y4 + nz * y5 - ny * y8)
        az = y3 + root_three * (ny * y5 + nx * y7) + 3.0 * nz * y6
        dd = red_sc[9] * (-0.5 * w) - (ax * nx + ay * ny + az * nz) * inv
        u = jnp.maximum(1.0 - d2 * (1.0 / 144.0), 0.0)
        radial = dd * inv + dw * geo_sc[gi, LIVE] * u * (-4.0 / 144.0)
        gr_sc[0] = ax * inv + rx * radial
        gr_sc[1] = ay * inv + ry * radial
        gr_sc[2] = az * inv + rz * radial
        where32 = iota((32, L), 0, F32)

        def scatter(j, i, c):
            code, slot, s = [geo_sc[gi, q, j : j + 1, :] for q in (CODE, SLOT, WHO)]
            slot01 = onoff(slot == sub16).astype(BF)
            s01 = onoff(s == sub16).astype(BF)
            g16 = [rows16(gr_sc[d, j : j + 1, :]) for d in range(3)]
            parts = [slot01 * -v for v in g16] + [zero] + [s01 * v for v in g16] + [zero]
            oh = onoff((code == where32) | (where32 == 27.0)).astype(BF)
            add = nt(oh, jnp.concatenate(parts, axis=0))
            yield 1
            f_sc[c] = f_sc[c] + add

        weave(scatter(j, i, c) for j, (i, c) in enumerate(zip(ids, cells)))
        return 0

    lax.fori_loop(0, groups, back, 0)

    fold_copy.wait()
    fa = f_sc[...].reshape(CELLS * 32, 128)
    fh = fa.astype(BF)
    fl = (fa - fh.astype(F32)).astype(BF)
    others = nn(fold[0], fh) + nn(fold[0], fl)
    own = nn(fold[1], fh) + nn(fold[1], fl)
    force_out[...] = others + jnp.concatenate([own[:, 64:128], jnp.zeros((GHOSTED, 64), F32)], axis=1)
    energy_out[...] = en_sc[:, 0, :] + en_sc[:, 1, :]


def fold_matrices():
    m = np.zeros((2, GHOSTED, CELLS * 32), np.float32)
    for c in range(CELLS):
        x, y, z = place_of(c)
        for k in range(27):
            m[0, ext_at(x + k // 9, y + k // 3 % 3, z + k % 3), c * 32 + k] = 1
        m[1, ext_at(x + 1, y + 1, z + 1), c * 32 + 27] = 1
    return m


PREPARED = (
    jax.ShapeDtypeStruct((CELLS, 8, 128), I32),
    jax.ShapeDtypeStruct((CELLS, 8, 128), I32),
    jax.ShapeDtypeStruct((CELLS, 48, 128), BF),
    jax.ShapeDtypeStruct((8, LISTED), I32),
    jax.ShapeDtypeStruct((7, 128, 128), BF),
    jax.ShapeDtypeStruct((8, 128), F32),
    jax.ShapeDtypeStruct((128, 128), F32),
)


def edge_stage(feats, prepared, w_mix, w_hid):
    rank, code, rt, todo, mats, wout_r, wout_b = prepared
    V = pltpu.VMEM
    vm = pl.BlockSpec(memory_space=pltpu.VMEM)
    return pl.pallas_call(
        edge_kernel,
        out_shape=(jax.ShapeDtypeStruct((CELLS, 16), F32), jax.ShapeDtypeStruct((GHOSTED, 128), F32)),
        in_specs=[pl.BlockSpec(memory_space=pltpu.SMEM)] + [vm] * 9 + [pl.BlockSpec(memory_space=pl.ANY)],
        out_specs=(vm, vm),
        scratch_shapes=[
            V((GHOSTED, 16, 128), BF),
            V((9, CELLS, 16, 128), F32),
            V((9, CELLS, 16, 128), BF),
            V((9, CELLS, 16, 128), BF),
            V((CELLS, 32, 128), F32),
            V((CELLS, 8, 16), F32),
            V((MAXCH, 128, L), BF),
            V((MAXCH, 128, L), BF),
            V((MAXCH, 128, L), BF),
            V((MAXCH, 128, L), BF),
            V((MAXCH, 128, L), BF),
            V((MAXGR, 9, G, L), F32),
            V((9, G, L), F32),
            V((10, G, L), F32),
            V((3, G, L), F32),
            V((2, GHOSTED, CELLS * 32), BF),
            pltpu.SemaphoreType.DMA,
        ],
        compiler_params=pltpu.CompilerParams(vmem_limit_bytes=60 * 1024 * 1024),
        name="edges",
    )(todo, feats, rank, code, rt, mats, wout_r, wout_b, w_mix, w_hid, jnp.asarray(fold_matrices(), BF))


MESH = pl.DeviceIdType.MESH
STEPS = (0, -1, 1)
AROUND = tuple((dx, dy, dz) for dx in STEPS for dy in STEPS for dz in STEPS)[1:]


def peer(dx, dy, dz):
    there = {}
    for axis, step in (("gx", dx), ("gy", dy), ("gz", dz)):
        size = lax.axis_size(axis)
        there[axis] = lax.rem(lax.axis_index(axis) + (step + size), size)
    return there


def greet():
    barrier = pltpu.get_barrier_semaphore()
    for dx, dy, dz in AROUND:
        pl.semaphore_signal(barrier, inc=1, device_id=peer(dx, dy, dz), device_id_type=MESH)
    return barrier


def sent(src, dst, send, recv, there):
    copy = pltpu.make_async_remote_copy(
        src_ref=src, dst_ref=dst, send_sem=send, recv_sem=recv, device_id=there, device_id_type=MESH
    )
    copy.start()
    return copy


def border(step, n):
    return pl.ds(1, n) if step == 0 else pl.ds(1 if step < 0 else n, 1)


def ghost(step, n):
    return pl.ds(1, n) if step == 0 else pl.ds(n + 1 if step < 0 else 0, 1)


def halo_kernel(
    occ_s, pos, feat, counts, w_out, neigh_h, w_atom_h, w_rad_h, w_hid_h, w_ten_h, w_mix_h,
    feat_ext, rank_h, code_h, rt_h, todo_h, mats_h, wout_r_h, wout_b_h,
    w_atom, w_rad, w_hid, w_ten_t, w_mix, neigh, rank, code, rt, todo, mats, wout_r, wout_b,
    rows, rows2, occ_sp, send, recv, inward, outward,
):
    barrier = greet()
    fetched = [
        pltpu.make_async_copy(far, near, inward.at[j])
        for j, (far, near) in enumerate(
            zip((w_atom_h, w_rad_h, w_hid_h, w_ten_h, w_mix_h, neigh_h), (w_atom, w_rad, w_hid, w_ten_t, w_mix, neigh))
        )
    ]
    for copy in fetched:
        copy.start()
    table = jnp.concatenate([pos[0], pos[1], pos[2], jnp.zeros((CELLS, 80), F32)], axis=1)
    lane = iota((1, 128), 1)
    for c in range(CELLS):
        x, y, z = place_of(c)
        rows[x + 1, y + 1, z + 1] = jnp.where(lane < 48, table[c : c + 1], occ_s[x, z, y].astype(F32))
        feat_ext[x + 1, y + 1, z + 1] = feat[c]
    pl.semaphore_wait(barrier, len(AROUND))

    def around(array, base):
        copies = []
        for j, (dx, dy, dz) in enumerate(AROUND):
            src = array.at[border(dx, CX), border(dy, CY), border(dz, CZ)]
            dst = array.at[ghost(dx, CX), ghost(dy, CY), ghost(dz, CZ)]
            copies.append(sent(src, dst, send.at[base + j], recv.at[base + j], peer(dx, dy, dz)))
        return copies

    row_copies = around(rows, 0)
    feat_copies = around(feat_ext, len(AROUND))
    for copy in fetched:
        copy.wait()
    prepare_weights(w_atom, w_rad, w_hid, w_ten_t, w_mix, w_out, mats, wout_r, wout_b)
    for copy in row_copies:
        copy.wait()
    prepare_edges(rows, rows2, occ_sp, neigh, counts, rank, code, rt, todo)
    stored = [
        pltpu.make_async_copy(near, far, outward.at[j])
        for j, (near, far) in enumerate(
            zip(
                (rank, code, rt, todo, mats, wout_r, wout_b),
                (rank_h, code_h, rt_h, todo_h, mats_h, wout_r_h, wout_b_h),
            )
        )
    ]
    for copy in stored:
        copy.start()
    for copy in feat_copies:
        copy.wait()
    for copy in stored:
        copy.wait()


def halo_stage(occ, pos, feat, neigh, counts, w_atom, w_rad, w_hid, w_ten_t, w_mix, w_out):
    vm = pl.BlockSpec(memory_space=pltpu.VMEM)
    V = pltpu.VMEM
    far = pl.BlockSpec(memory_space=pl.ANY)
    moved = (w_atom, w_rad, w_hid, w_ten_t, w_mix, neigh)
    out = pl.pallas_call(
        halo_kernel,
        out_shape=(jax.ShapeDtypeStruct((EX, EY, EZ, 16, 128), BF),) + PREPARED,
        in_specs=[pl.BlockSpec(memory_space=pltpu.SMEM)] + [vm] * 4 + [far] * 6,
        out_specs=(vm,) + (far,) * 7,
        scratch_shapes=[V(a.shape, a.dtype) for a in moved]
        + [V(a.shape, a.dtype) for a in PREPARED]
        + [
            V((EX, EY, EZ, 1, 128), F32),
            V((GHOSTED, 128), F32),
            V((GHOSTED, 128), F32),
            pltpu.SemaphoreType.DMA((2 * len(AROUND),)),
            pltpu.SemaphoreType.DMA((2 * len(AROUND),)),
            pltpu.SemaphoreType.DMA((6,)),
            pltpu.SemaphoreType.DMA((7,)),
        ],
        compiler_params=pltpu.CompilerParams(
            collective_id=0, has_side_effects=True, vmem_limit_bytes=60 * 1024 * 1024
        ),
        name="halo",
    )(occ, pos, feat, counts, w_out, neigh, w_atom, w_rad, w_hid, w_ten_t, w_mix)
    return out[0], out[1:]


def fold_kernel(grid, out, acc, got, send, recv):
    barrier = greet()
    acc[...] = grid[...]
    pl.semaphore_wait(barrier, len(AROUND))

    def rim(step, n):
        return pl.ds(1, n) if step == 0 else pl.ds(0 if step < 0 else n + 1, 1)

    def room(step, n):
        return pl.ds(0, n if step == 0 else 1)

    copies = []
    for j, (dx, dy, dz) in enumerate(AROUND):
        src = acc.at[rim(dx, CX), rim(dy, CY), rim(dz, CZ)]
        dst = got.at[j, room(dx, CX), room(dy, CY), room(dz, CZ)]
        copies.append((sent(src, dst, send.at[j], recv.at[j], peer(dx, dy, dz)), dst))
    for (copy, dst), (dx, dy, dz) in zip(copies, AROUND):
        copy.wait()
        at = (border(-dx, CX), border(-dy, CY), border(-dz, CZ))
        acc[at] = acc[at] + dst[...]
    lines = []
    for c in range(CELLS):
        x, y, z = place_of(c)
        lines.append(acc[x + 1, y + 1, z + 1])
    lines = jnp.concatenate(lines, axis=0)
    for d in range(3):
        out[d] = lines[:, 16 * d : 16 * d + 16]


def fold_stage(grid):
    vm = pl.BlockSpec(memory_space=pltpu.VMEM)
    V = pltpu.VMEM
    return pl.pallas_call(
        fold_kernel,
        out_shape=jax.ShapeDtypeStruct((3, CELLS, 16), F32),
        in_specs=[vm],
        out_specs=vm,
        scratch_shapes=[
            V((EX, EY, EZ, 1, 128), F32),
            V((len(AROUND), CX, CY, CZ, 1, 128), F32),
            pltpu.SemaphoreType.DMA((len(AROUND),)),
            pltpu.SemaphoreType.DMA((len(AROUND),)),
        ],
        compiler_params=pltpu.CompilerParams(collective_id=1, has_side_effects=True, vmem_limit_bytes=60 * 1024 * 1024),
        name="fold",
    )(grid)


def on_device(
    positions, occupancy, neighbours, edge_counts, atom_features, w_atom, w_radial, w_hidden, w_tensor, w_mix, w_out
):
    feats, prepared = halo_stage(
        occupancy.transpose(0, 2, 1),
        positions.reshape(3, CELLS, 16),
        atom_features.reshape(CELLS, 16, 128),
        neighbours.reshape(CELLS, 16, 64),
        edge_counts.reshape(CELLS, 16),
        w_atom, w_radial, w_hidden, w_tensor.T, w_mix, w_out.reshape(1, 128),
    )
    energy, forces = edge_stage(feats.reshape(GHOSTED, 16, 128), prepared, w_mix, w_hidden)
    forces = fold_stage(forces.reshape(EX, EY, EZ, 1, 128))
    return energy.reshape(CX, CY, CZ, 16), forces.reshape(3, CX, CY, CZ, 16)


def solution(mesh):
    cells = P("gx", "gy", "gz", None)
    placed = (
        P(None, "gx", "gy", "gz", None),
        P("gx", "gy", "gz"),
        P("gx", "gy", "gz", None, None),
        cells,
        P("gx", "gy", "gz", None, None),
        P(), P(), P(), P(), P(), P(),
    )
    return jax.shard_map(
        on_device,
        mesh=mesh,
        in_specs=placed,
        out_specs=(cells, P(None, "gx", "gy", "gz", None)),
        check_vma=False,
    )
```

```python
import numpy as np
import jax
import jax.numpy as jnp
from jax import lax
from jax.experimental import pallas as pl
from jax.experimental.pallas import tpu as pltpu
from jax.sharding import PartitionSpec as P

F32 = jnp.float32
BF = jnp.bfloat16
I32 = jnp.int32
root_three = 1.7320508075688772
L = 256
G = 12
CX, CY, CZ = 4, 4, 2
EX, EY, EZ = CX + 2, CY + 2, CZ + 2
CELLS = CX * CY * CZ
GHOSTED = EX * EY * EZ
MAXGR = -(-CELLS * (1024 // L) // G)
MAXCH = MAXGR * G
LISTED = 256


def nn(a, b):
    return lax.dot_general(a, b, (((1,), (0,)), ((), ())), preferred_element_type=F32)


def nt(a, b):
    return lax.dot_general(a, b, (((1,), (1,)), ((), ())), preferred_element_type=F32)


def tn(a, b):
    return lax.dot_general(a, b, (((0,), (0,)), ((), ())), preferred_element_type=F32)


def iota(shape, dim, dtype=I32):
    return lax.broadcasted_iota(I32, shape, dim).astype(dtype)


def onoff(mask):
    return jnp.where(mask, 1.0, 0.0).astype(F32)


def eye(n, m):
    return onoff(iota((n, m), 0) == iota((n, m), 1)).astype(BF)


def place_of(c):
    return c // (CY * CZ), c // CZ % CY, c % CZ


def ext_at(x, y, z):
    return (x * EY + y) * EZ + z


def prepare_weights(w_atom, w_rad, w_hid, w_ten_t, w_mix, w_out, mats, wout_r, wout_b):
    ident = eye(128, 128)
    half = 0.5
    mats[0] = (half * w_atom[...].astype(F32)).astype(BF)
    mats[1] = (half * nt(ident, w_hid[...])).astype(BF)
    mats[2] = (half * nt(ident, w_mix[0:128, :])).astype(BF)
    rad = jnp.concatenate([jnp.zeros((48, 128), F32), w_rad[...].astype(F32), jnp.zeros((72, 128), F32)], axis=0)
    mats[3] = (half * rad).astype(BF)
    wout_r[...] = w_out[...] * jnp.ones((8, 128), F32)
    wout_b[...] = jnp.sum(
        jnp.where(iota((128, 128), 0) == iota((128, 128), 1), w_out[...], 0.0), axis=1, keepdims=True
    ) * jnp.ones((128, 128), F32)
    tail = w_mix[128:224, :]
    for l in range(3):
        sel = onoff(iota((96, 32), 0) == 3 * iota((96, 32), 1) + l).astype(BF)
        spread = nt(ident, nn(sel, w_ten_t[...]).astype(BF)).astype(BF)
        mats[4 + l] = (0.0625 * nn(spread, tail)).astype(BF)


def prepare_edges(rows, rows2, occ_sp, neigh, counts, rank_out, code_out, rt_out, list_out):
    for x in range(EX):
        for y in range(EY):
            for z in range(EZ):
                at = ext_at(x, y, z)
                rows2[at : at + 1, :] = rows[x, y, z]
    occ_sp[...] = nn(rows2[...].astype(BF), onoff(iota((128, 128), 0) == 48).astype(BF))
    counts_t = nt(eye(16, 16), counts[...].astype(F32).astype(BF))
    lane64 = iota((8, 128), 1)
    low = lane64 < 64
    k_of = jnp.where(low, lane64, lane64 - 64).astype(F32)
    s_of = jnp.where(low, iota((8, 128), 0), iota((8, 128), 0) + 8)
    s_f = s_of.astype(F32)
    masks = []
    for c in range(CELLS):
        x, y, z = place_of(c)
        nb = jnp.concatenate([neigh[c, 0:8, :], neigh[c, 8:16, :]], axis=1)
        code_out[c] = nb
        cnt = jnp.where(low, counts_t[0:8, c : c + 1], counts_t[8:16, c : c + 1])
        code = lax.shift_right_logical(nb, 4)
        slot = lax.bitwise_and(nb, 15).astype(F32)
        occ_n = jnp.zeros((8, 128), F32)
        for k in range(27):
            at = ext_at(x + k // 9, y + k // 3 % 3, z + k % 3)
            occ_n = jnp.where(code == k, occ_sp[at : at + 1, :], occ_n)
        at = ext_at(x + 1, y + 1, z + 1)
        live = (k_of < cnt) & (slot < occ_n) & (s_f < occ_sp[at : at + 1, :]) & (nb != 208 + s_of)
        masks.append(onoff(live))
    mask = jnp.concatenate(masks, axis=0)
    mask_b = mask.astype(BF)
    upto = nn(mask_b, onoff(iota((128, 128), 0) <= iota((128, 128), 1)).astype(BF))
    total = nn(mask_b, jnp.ones((128, 128), BF))
    ri, ci = iota((256, 256), 0), iota((256, 256), 1)
    before = onoff((lax.shift_right_logical(ri, 3) == lax.shift_right_logical(ci, 3)) & (ci < ri)).astype(BF)
    base = nn(before, total.astype(BF))
    rank_out[...] = jnp.where(mask > 0.5, upto - 1.0 + base, -1.0).astype(I32).reshape(CELLS, 8, 128)
    n = (base + total).reshape(CELLS, 8, 128)[:, 7, :].astype(I32)
    chunks = lax.shift_right_logical(n + (L - 1), L.bit_length() - 1).astype(F32)
    ends = nn(onoff(iota((CELLS, CELLS), 1) <= iota((CELLS, CELLS), 0)).astype(BF), chunks.astype(BF))
    ends = jnp.concatenate([ends] * (LISTED // 128), axis=1)
    t = iota((CELLS, LISTED), 1, F32)
    done = ends <= t
    cell = jnp.minimum(jnp.sum(onoff(done), axis=0, keepdims=True), CELLS - 1.0)
    start = jnp.max(jnp.where(done, ends, 0.0), axis=0, keepdims=True)
    all_of = ends[CELLS - 1 : CELLS]
    first = jnp.where(t[0:1] < all_of, (t[0:1] - start) * L, 4096.0)
    list_out[...] = jnp.concatenate([cell, first, all_of, jnp.zeros((5, LISTED), F32)], axis=0).astype(I32)

    lane = iota((32, 128), 1)
    code_i = iota((32, 128), 0)
    ca = code_i // 9
    cb = code_i // 3 - 3 * ca
    cc = code_i - 3 * (code_i // 3)
    coord = lax.shift_right_logical(lane, 4)
    step = jnp.where(coord == 0, ca, jnp.where(coord == 1, cb, jnp.where(coord == 2, cc, 1))) - 1
    shift = 5.0 * step.astype(F32)
    pick = eye(48, 128)
    for c in range(CELLS):
        x, y, z = place_of(c)
        parts = []
        for k in range(0, 27, 3):
            at = ext_at(x + k // 9, y + k // 3 % 3, z)
            parts.append(rows2[at : at + 3, :])
        parts.append(jnp.zeros((5, 128), F32))
        r27 = jnp.concatenate(parts, axis=0) + shift
        hi = r27.astype(BF)
        rest = r27 - hi.astype(F32)
        mid = rest.astype(BF)
        lo = (rest - mid.astype(F32)).astype(BF)
        cat = jnp.concatenate([hi, mid, lo, jnp.zeros((32, 128), BF)], axis=0)
        rt_out[c] = nt(pick, cat).astype(BF)


def silu_both(h):
    t = jnp.tanh(h)
    y = (h + h * t).astype(BF)
    t = t.astype(BF)
    return y, (1.0 + t) + y * (1.0 - t)


def wide16(v):
    return jnp.broadcast_to(v, (16, 128)).astype(BF)


def rows16(v):
    return jnp.broadcast_to(v, (16, v.shape[1])).astype(BF)


def weave(tasks):
    active = list(tasks)
    while active:
        active = [task for task in active if next(task, None) is not None]


RX, RY, RZ, LIVE, CODE, SLOT, WHO, WEIGHT, EPS = range(9)


def edge_kernel(
    list_s, feats, rank_r, code_r, rt_r, mats, wout_r, wout_b, w_mix, w_hid, fold_h,
    energy_out, force_out,
    proj_sc, q_sc, m_sc, dq_sc, f_sc, en_sc, sec_sc, d1_sc, d2_sc, g_sc, ys_sc, geo_sc, y_sc, red_sc, gr_sc,
    fold, fold_sem,
):
    fold_copy = pltpu.make_async_copy(fold_h, fold, fold_sem)
    fold_copy.start()
    groups = lax.div(list_s[2, 0] + (G - 1), G)
    ident = eye(128, 128)
    q_sc[...] = jnp.zeros_like(q_sc)
    f_sc[...] = jnp.zeros_like(f_sc)
    en_sc[...] = jnp.zeros_like(en_sc)
    sub16 = iota((16, L), 0, F32)
    proj_sc[...] = nn(feats[...].reshape(GHOSTED * 16, 128), mats[0]).astype(BF).reshape(GHOSTED, 16, 128)
    zero = jnp.zeros((16, L), BF)
    centres = 0.5 + 2.0 * iota((8, L), 0, F32)

    def ids_of(gi):
        ids = [gi * G + i for i in range(G)]
        return ids, [list_s[0, i] for i in ids]

    def sphere(gi):
        rx, ry, rz = geo_sc[gi, RX], geo_sc[gi, RY], geo_sc[gi, RZ]
        d2 = rx * rx + ry * ry + rz * rz + 0.01
        inv = lax.rsqrt(d2)
        return rx, ry, rz, d2, inv, d2 * inv, rx * inv, ry * inv, rz * inv

    def front(gi, _):
        ids, cells = ids_of(gi)
        sixteen = iota((16, 128), 0, F32).astype(BF)
        lane_l = iota((16, L), 1)
        unfold = onoff(lax.bitwise_and(lane_l, 15) == iota((16, L), 0)).astype(BF)
        in_high = lax.shift_right_logical(lane_l, 4) == iota((16, L), 0)
        lane8 = iota((8, 128), 1)
        s_of = jnp.where(lane8 < 64, iota((8, 128), 0), iota((8, 128), 0) + 8)
        ones = jnp.ones((16, 128), BF)
        zeros = jnp.zeros((16, 128), BF)

        def find(j, i, c):
            rk = rank_r[c] - list_s[1, i]
            inside = (rk >= 0) & (rk < L)
            high = jnp.where(inside, lax.shift_right_logical(rk, 4), -1).astype(F32)
            deep = lax.bitwise_and(rk, 15).astype(F32)
            nb = code_r[c]
            code_f = (lax.shift_right_logical(nb, 4) + 1).astype(F32)
            pair_f = (lax.bitwise_and(nb, 15) + 16 * s_of).astype(F32)
            left, right = [], []
            for k in range(8):
                at_high = jnp.where(sixteen == wide16(high[k : k + 1]), ones, zeros)
                left.append(
                    jnp.concatenate([at_high * wide16(code_f[k : k + 1]), at_high * wide16(pair_f[k : k + 1])], axis=0)
                )
                right.append(jnp.where(sixteen == wide16(deep[k : k + 1]), ones, zeros))
            packed = nt(jnp.concatenate(left, axis=1), jnp.concatenate(right, axis=1))
            yield 1
            spread = nn(packed.astype(BF), unfold)
            yield 1
            code1, pair = [
                jnp.sum(jnp.where(in_high, spread[16 * a : 16 * a + 16], 0.0), axis=0, keepdims=True) for a in range(2)
            ]
            live = jnp.minimum(code1, 1.0)
            code = code1 - live
            s = jnp.floor(pair * 0.0625)
            slot = pair - 16.0 * s
            oh27 = onoff(code == iota((32, L), 0, F32)).astype(BF)
            rt = rt_r[c]
            got = nn(rt, jnp.concatenate([oh27, oh27, oh27, jnp.zeros((32, L), BF)], axis=0))
            for q, v in ((LIVE, live), (CODE, code), (SLOT, slot), (WHO, s)):
                geo_sc[gi, q, j : j + 1, :] = v
            yield 1
            m_slot = slot == sub16
            m_s = s == sub16
            rtf = rt.astype(F32)
            centre = rtf[:, 13:14] + (rtf[:, 45:46] + rtf[:, 77:78])
            for d in range(3):
                sl = slice(16 * d, 16 * d + 16)
                geo_sc[gi, d, j : j + 1, :] = jnp.sum(
                    jnp.where(m_slot, got[sl], 0.0) - jnp.where(m_s, centre[sl], 0.0), axis=0, keepdims=True
                )

        weave(find(j, i, c) for j, (i, c) in enumerate(zip(ids, cells)))
        rx, ry, rz, d2, inv, dist, nx, ny, nz = sphere(gi)
        u = jnp.maximum(1.0 - d2 * (1.0 / 144.0), 0.0)
        geo_sc[gi, WEIGHT] = geo_sc[gi, LIVE] * (u * u)
        y_sc[0] = dist
        y_sc[1] = nx
        y_sc[2] = ny
        y_sc[3] = nz
        y_sc[4] = root_three * nx * ny
        y_sc[5] = root_three * ny * nz
        y_sc[6] = 0.5 * (3.0 * nz * nz - 1.0)
        y_sc[7] = root_three * nx * nz
        y_sc[8] = (0.5 * root_three) * (nx * nx - ny * ny)

        def layers(j, i, c):
            x = lax.div(c, CY * CZ)
            rest = c - x * (CY * CZ)
            y = lax.div(rest, CZ)
            z = rest - y * CZ
            parts = [
                proj_sc[pl.ds(((x + k // 3) * EY + y + k % 3) * EZ + z, 3)].reshape(48, 128) for k in range(9)
            ]
            parts.append(mats[3, 48:64, :])
            tab = jnp.concatenate(parts, axis=0)
            code, slot, s = [geo_sc[gi, q, j : j + 1, :] for q in (CODE, SLOT, WHO)]
            arg = (y_sc[0, j : j + 1, :] - centres) * 0.5
            basis = jnp.exp(-(arg * arg))
            slot01 = onoff(slot == sub16).astype(BF)
            s01 = onoff(s == sub16).astype(BF)
            code16 = rows16(code)
            tiles = [jnp.where(code16 == float(k), slot01, zero) for k in range(27)]
            tiles[13] = tiles[13] + s01
            tiles.append(jnp.concatenate([basis, jnp.zeros((8, L), F32)], axis=0).astype(BF))
            pre = tn(tab, jnp.concatenate(tiles, axis=0))
            yield 1
            f, d1 = silu_both(pre)
            d1_sc[i] = d1
            hidden = nn(mats[1], f)
            yield 1
            ys = jnp.concatenate([s01] + [s01 * rows16(y_sc[m, j : j + 1, :]) for m in range(1, 9)], axis=0)
            ys_sc[i] = ys[16:144]
            sb, d2 = silu_both(hidden)
            d2_sc[i] = d2
            sec_sc[i] = sb
            w16 = rows16(geo_sc[gi, WEIGHT, j : j + 1, :])
            q = nt(ys * jnp.concatenate([w16] * 9, axis=0), sb)
            yield 1
            q_sc[:, c] = q_sc[:, c] + q.reshape(9, 16, 128)

        weave(layers(j, i, c) for j, (i, c) in enumerate(zip(ids, cells)))
        return 0

    lax.fori_loop(0, groups, front, 0)

    for m in range(9):
        l = 0 if m == 0 else 1 if m < 4 else 2
        m_sc[m] = nn(q_sc[m].reshape(CELLS * 16, 128).astype(BF), mats[4 + l]).astype(BF).reshape(CELLS, 16, 128)
        q_sc[m] = jnp.zeros((CELLS, 16, 128), F32)

    def middle(gi, _):
        ids, cells = ids_of(gi)
        wout_h = jnp.concatenate([(0.5 * wout_b[...]).astype(BF)] * (L // 128), axis=1)
        row = iota((16, 128), 0)
        w_hi = wout_r[0:1, :].astype(BF).astype(F32)
        w_rows = jnp.where(row == 0, w_hi, jnp.where(row == 1, wout_r[0:1, :] - w_hi, 0.0)).astype(BF)

        def mix(j, i, c):
            s01 = onoff(geo_sc[gi, WHO, j : j + 1, :] == sub16).astype(BF)
            ys = jnp.concatenate([s01, ys_sc[i]], axis=0)
            p = nn(mats[2], sec_sc[i]) + tn(m_sc[:, c].reshape(144, 128), ys)
            yield 1
            w = geo_sc[gi, WEIGHT, j : j + 1, :]
            mixed, d = silu_both(p)
            g = d * wout_h
            g_sc[i] = g
            energies = nn(w_rows, mixed)
            dm = nt(ys * jnp.concatenate([rows16(w)] * 9, axis=0), g)
            yield 1
            eps = energies[0:1] + energies[1:2]
            geo_sc[gi, EPS, j : j + 1, :] = eps
            we = eps * w
            hi = we.astype(BF).astype(F32)
            en = nt(jnp.where(iota((16, L), 0) == 0, hi, jnp.where(iota((16, L), 0) == 1, we - hi, 0.0)).astype(BF), ys[0:16])
            q_sc[:, c] = q_sc[:, c] + dm.reshape(9, 16, 128)
            yield 1
            en_sc[c] = en_sc[c] + en[0:8]

        weave(mix(j, i, c) for j, (i, c) in enumerate(zip(ids, cells)))
        return 0

    lax.fori_loop(0, groups, middle, 0)

    for m in range(9):
        l = 0 if m == 0 else 1 if m < 4 else 2
        dq_sc[m] = nt(q_sc[m].reshape(CELLS * 16, 128).astype(BF), mats[4 + l]).astype(BF).reshape(CELLS, 16, 128)

    def back(gi, _):
        ids, cells = ids_of(gi)
        top = jnp.concatenate([w_mix[0:128, :], jnp.zeros((128, 128), BF)], axis=1)
        col, row = iota((16, 256), 1), iota((16, 256), 0)
        part = jnp.where(col < 128, 0, lax.shift_right_logical(col - 128, 4) + 1)
        gather = onoff(part == row).astype(BF)
        rx, ry, rz, d2, inv, dist, nx, ny, nz = sphere(gi)
        y_sc[0] = dist

        def undo(j, i, c):
            dq = dq_sc[:, c].reshape(144, 128)
            s01 = onoff(geo_sc[gi, WHO, j : j + 1, :] == sub16).astype(BF)
            t = tn(dq, jnp.concatenate([s01, ys_sc[i]], axis=0))
            sb = sec_sc[i]
            low = jnp.concatenate([m_sc[1:9, c].reshape(128, 128), dq[16:144]], axis=1)
            both = nn(jnp.concatenate([top, low], axis=0), jnp.concatenate([g_sc[i], sb], axis=0))
            yield 1
            t2 = t + t
            dsec = both[0:128] + t2
            dfirst = nn(w_hid[...], dsec.astype(BF) * d2_sc[i])
            sums = nn(
                gather,
                jnp.concatenate([t2.astype(BF) * sb, both[128:256].astype(BF) * jnp.concatenate([s01] * 8, axis=0)], axis=0),
            )
            yield 1
            for m in range(9):
                red_sc[m, j : j + 1, :] = sums[m : m + 1]
            dbasis = nn(mats[3, 48:64, :], dfirst.astype(BF) * d1_sc[i])[0:8]
            yield 1
            arg = (y_sc[0, j : j + 1, :] - centres) * 0.5
            red_sc[9, j : j + 1, :] = jnp.sum(dbasis * jnp.exp(-(arg * arg)) * arg, axis=0, keepdims=True)

        weave(undo(j, i, c) for j, (i, c) in enumerate(zip(ids, cells)))
        w = geo_sc[gi, WEIGHT]
        w2 = w + w
        dw = geo_sc[gi, EPS] + red_sc[0]
        y1, y2, y3, y4, y5, y6, y7, y8 = [red_sc[m] * w2 for m in range(1, 9)]
        ax = y1 + root_three * (ny * y4 + nz * y7 + nx * y8)
        ay = y2 + root_three * (nx * y4 + nz * y5 - ny * y8)
        az = y3 + root_three * (ny * y5 + nx * y7) + 3.0 * nz * y6
        dd = red_sc[9] * (-0.5 * w) - (ax * nx + ay * ny + az * nz) * inv
        u = jnp.maximum(1.0 - d2 * (1.0 / 144.0), 0.0)
        radial = dd * inv + dw * geo_sc[gi, LIVE] * u * (-4.0 / 144.0)
        gr_sc[0] = ax * inv + rx * radial
        gr_sc[1] = ay * inv + ry * radial
        gr_sc[2] = az * inv + rz * radial
        where32 = iota((32, L), 0, F32)

        def scatter(j, i, c):
            code, slot, s = [geo_sc[gi, q, j : j + 1, :] for q in (CODE, SLOT, WHO)]
            slot01 = onoff(slot == sub16).astype(BF)
            s01 = onoff(s == sub16).astype(BF)
            g16 = [rows16(gr_sc[d, j : j + 1, :]) for d in range(3)]
            parts = [slot01 * -v for v in g16] + [zero] + [s01 * v for v in g16] + [zero]
            oh = onoff((code == where32) | (where32 == 27.0)).astype(BF)
            add = nt(oh, jnp.concatenate(parts, axis=0))
            yield 1
            f_sc[c] = f_sc[c] + add

        weave(scatter(j, i, c) for j, (i, c) in enumerate(zip(ids, cells)))
        return 0

    lax.fori_loop(0, groups, back, 0)

    fold_copy.wait()

    def halves(v):
        hi = v.astype(BF)
        return jnp.concatenate([hi, (v - hi.astype(F32)).astype(BF)], axis=1)

    width = CELLS * 32
    sums = nn(fold[:, 0:width], halves(f_sc[:, :, 0:64].reshape(width, 64)))
    sums = sums + nn(fold[:, width : width + CELLS], halves(f_sc[:, 27, 64:128]))
    force_out[...] = jnp.concatenate([sums[:, 0:64] + sums[:, 64:128], jnp.zeros((GHOSTED, 64), F32)], axis=1)
    energy_out[...] = en_sc[:, 0, :] + en_sc[:, 1, :]


def fold_matrix():
    width = CELLS * 32
    m = np.zeros((GHOSTED, width + 128), np.float32)
    for c in range(CELLS):
        x, y, z = place_of(c)
        for k in range(27):
            m[ext_at(x + k // 9, y + k // 3 % 3, z + k % 3), c * 32 + k] = 1
        m[ext_at(x + 1, y + 1, z + 1), width + c] = 1
    return m


PREPARED = (
    jax.ShapeDtypeStruct((CELLS, 8, 128), I32),
    jax.ShapeDtypeStruct((CELLS, 8, 128), I32),
    jax.ShapeDtypeStruct((CELLS, 48, 128), BF),
    jax.ShapeDtypeStruct((8, LISTED), I32),
    jax.ShapeDtypeStruct((7, 128, 128), BF),
    jax.ShapeDtypeStruct((8, 128), F32),
    jax.ShapeDtypeStruct((128, 128), F32),
)


def edge_stage(feats, prepared, w_mix, w_hid):
    rank, code, rt, todo, mats, wout_r, wout_b = prepared
    V = pltpu.VMEM
    vm = pl.BlockSpec(memory_space=pltpu.VMEM)
    return pl.pallas_call(
        edge_kernel,
        out_shape=(jax.ShapeDtypeStruct((CELLS, 16), F32), jax.ShapeDtypeStruct((GHOSTED, 128), F32)),
        in_specs=[pl.BlockSpec(memory_space=pltpu.SMEM)] + [vm] * 9 + [pl.BlockSpec(memory_space=pl.ANY)],
        out_specs=(vm, vm),
        scratch_shapes=[
            V((GHOSTED, 16, 128), BF),
            V((9, CELLS, 16, 128), F32),
            V((9, CELLS, 16, 128), BF),
            V((9, CELLS, 16, 128), BF),
            V((CELLS, 32, 128), F32),
            V((CELLS, 8, 16), F32),
            V((MAXCH, 128, L), BF),
            V((MAXCH, 128, L), BF),
            V((MAXCH, 128, L), BF),
            V((MAXCH, 128, L), BF),
            V((MAXCH, 128, L), BF),
            V((MAXGR, 9, G, L), F32),
            V((9, G, L), F32),
            V((10, G, L), F32),
            V((3, G, L), F32),
            V((GHOSTED, CELLS * 32 + 128), BF),
            pltpu.SemaphoreType.DMA,
        ],
        compiler_params=pltpu.CompilerParams(vmem_limit_bytes=60 * 1024 * 1024),
        name="edges",
    )(todo, feats, rank, code, rt, mats, wout_r, wout_b, w_mix, w_hid, jnp.asarray(fold_matrix(), BF))


MESH = pl.DeviceIdType.MESH
STEPS = (0, -1, 1)
AROUND = tuple((dx, dy, dz) for dx in STEPS for dy in STEPS for dz in STEPS)[1:]
RING = tuple(v for v in AROUND if v[2] == 0)
BOTH = ((0, 0, -1), (0, 0, 1))


def neighbourhood():
    axes = []
    for axis in ("gx", "gy", "gz"):
        size, me = lax.axis_size(axis), lax.axis_index(axis)
        axes.append({0: me, -1: lax.rem(me + (size - 1), size), 1: lax.rem(me + 1, size)})
    return lambda dx, dy, dz: {"gx": axes[0][dx], "gy": axes[1][dy], "gz": axes[2][dz]}


def greet(peer, others):
    barrier = pltpu.get_barrier_semaphore()
    for dx, dy, dz in others:
        pl.semaphore_signal(barrier, inc=1, device_id=peer(dx, dy, dz), device_id_type=MESH)
    return barrier


def sent(src, dst, send, recv, there):
    copy = pltpu.make_async_remote_copy(
        src_ref=src, dst_ref=dst, send_sem=send, recv_sem=recv, device_id=there, device_id_type=MESH
    )
    copy.start()
    return copy


def border(step, n):
    return pl.ds(1, n) if step == 0 else pl.ds(1 if step < 0 else n, 1)


def ghost(step, n):
    return pl.ds(1, n) if step == 0 else pl.ds(n + 1 if step < 0 else 0, 1)


def halo_kernel(
    occ_s, pos, feat, counts, w_out, neigh_h, w_atom_h, w_rad_h, w_hid_h, w_ten_h, w_mix_h,
    feat_ext, rank_h, code_h, rt_h, todo_h, mats_h, wout_r_h, wout_b_h,
    w_atom, w_rad, w_hid, w_ten_t, w_mix, neigh, rank, code, rt, todo, mats, wout_r, wout_b,
    rows, rows2, occ_sp, send, recv, inward, outward,
):
    peer = neighbourhood()
    barrier = greet(peer, AROUND)
    fetched = [
        pltpu.make_async_copy(far, near, inward.at[j])
        for j, (far, near) in enumerate(
            zip((w_atom_h, w_rad_h, w_hid_h, w_ten_h, w_mix_h, neigh_h), (w_atom, w_rad, w_hid, w_ten_t, w_mix, neigh))
        )
    ]
    for copy in fetched:
        copy.start()
    table = jnp.concatenate([pos[0], pos[1], pos[2], jnp.zeros((CELLS, 80), F32)], axis=1)
    lane = iota((1, 128), 1)
    for c in range(CELLS):
        x, y, z = place_of(c)
        rows[x + 1, y + 1, z + 1] = jnp.where(lane < 48, table[c : c + 1], occ_s[x, z, y].astype(F32))
        feat_ext[x + 1, y + 1, z + 1] = feat[c]
    pl.semaphore_wait(barrier, len(AROUND))

    def around(array, base):
        copies = []
        for j, (dx, dy, dz) in enumerate(AROUND):
            src = array.at[border(dx, CX), border(dy, CY), border(dz, CZ)]
            dst = array.at[ghost(dx, CX), ghost(dy, CY), ghost(dz, CZ)]
            copies.append(sent(src, dst, send.at[base + j], recv.at[base + j], peer(dx, dy, dz)))
        return copies

    row_copies = around(rows, 0)
    feat_copies = around(feat_ext, len(AROUND))
    for copy in fetched:
        copy.wait()
    prepare_weights(w_atom, w_rad, w_hid, w_ten_t, w_mix, w_out, mats, wout_r, wout_b)
    for copy in row_copies:
        copy.wait()
    prepare_edges(rows, rows2, occ_sp, neigh, counts, rank, code, rt, todo)
    stored = [
        pltpu.make_async_copy(near, far, outward.at[j])
        for j, (near, far) in enumerate(
            zip(
                (rank, code, rt, todo, mats, wout_r, wout_b),
                (rank_h, code_h, rt_h, todo_h, mats_h, wout_r_h, wout_b_h),
            )
        )
    ]
    for copy in stored:
        copy.start()
    for copy in feat_copies:
        copy.wait()
    for copy in stored:
        copy.wait()


def halo_stage(occ, pos, feat, neigh, counts, w_atom, w_rad, w_hid, w_ten_t, w_mix, w_out):
    vm = pl.BlockSpec(memory_space=pltpu.VMEM)
    V = pltpu.VMEM
    far = pl.BlockSpec(memory_space=pl.ANY)
    moved = (w_atom, w_rad, w_hid, w_ten_t, w_mix, neigh)
    out = pl.pallas_call(
        halo_kernel,
        out_shape=(jax.ShapeDtypeStruct((EX, EY, EZ, 16, 128), BF),) + PREPARED,
        in_specs=[pl.BlockSpec(memory_space=pltpu.SMEM)] + [vm] * 4 + [far] * 6,
        out_specs=(vm,) + (far,) * 7,
        scratch_shapes=[V(a.shape, a.dtype) for a in moved]
        + [V(a.shape, a.dtype) for a in PREPARED]
        + [
            V((EX, EY, EZ, 1, 128), F32),
            V((GHOSTED, 128), F32),
            V((GHOSTED, 128), F32),
            pltpu.SemaphoreType.DMA((2 * len(AROUND),)),
            pltpu.SemaphoreType.DMA((2 * len(AROUND),)),
            pltpu.SemaphoreType.DMA((6,)),
            pltpu.SemaphoreType.DMA((7,)),
        ],
        compiler_params=pltpu.CompilerParams(
            collective_id=0, has_side_effects=True, vmem_limit_bytes=60 * 1024 * 1024
        ),
        name="halo",
    )(occ, pos, feat, counts, w_out, neigh, w_atom, w_rad, w_hid, w_ten_t, w_mix)
    return out[0], out[1:]


def fold_kernel(grid, out, acc, got_x, got_y, got_xy, got_z, send, recv):
    peer = neighbourhood()
    barrier = greet(peer, RING + BOTH)
    acc[...] = grid[...]
    pl.semaphore_wait(barrier, len(RING + BOTH))
    copies = []
    for j, (dx, dy, _) in enumerate(RING):
        if dx and dy:
            got = got_xy.at[(dx + 1) + (dy + 1) // 2]
        elif dx:
            got = got_x.at[(dx + 1) // 2]
        else:
            got = got_y.at[(dy + 1) // 2]
        rim = (
            pl.ds(1, CX) if dx == 0 else pl.ds(0 if dx < 0 else CX + 1, 1),
            pl.ds(1, CY) if dy == 0 else pl.ds(0 if dy < 0 else CY + 1, 1),
        )
        copies.append((sent(acc.at[rim], got, send.at[j], recv.at[j], peer(dx, dy, 0)), got, dx, dy))
    for copy, got, dx, dy in copies:
        copy.wait()
        at = (border(-dx, CX), border(-dy, CY))
        acc[at] = acc[at] + got[...]
    inner = (pl.ds(1, CX), pl.ds(1, CY))
    copies = []
    for j, (step, rim) in enumerate(((-1, 0), (1, CZ + 1))):
        copies.append(
            sent(acc.at[inner + (pl.ds(rim, 1),)], got_z.at[j], send.at[8 + j], recv.at[8 + j], peer(0, 0, step))
        )
    for j, step in enumerate((-1, 1)):
        copies[j].wait()
        at = inner + (border(-step, CZ),)
        acc[at] = acc[at] + got_z[j]
    lines = []
    for c in range(CELLS):
        x, y, z = place_of(c)
        lines.append(acc[x + 1, y + 1, z + 1])
    lines = jnp.concatenate(lines, axis=0)
    for d in range(3):
        out[d] = lines[:, 16 * d : 16 * d + 16]


def fold_stage(grid):
    vm = pl.BlockSpec(memory_space=pltpu.VMEM)
    V = pltpu.VMEM
    return pl.pallas_call(
        fold_kernel,
        out_shape=jax.ShapeDtypeStruct((3, CELLS, 16), F32),
        in_specs=[vm],
        out_specs=vm,
        scratch_shapes=[
            V((EX, EY, EZ, 1, 128), F32),
            V((2, 1, CY, EZ, 1, 128), F32),
            V((2, CX, 1, EZ, 1, 128), F32),
            V((4, 1, 1, EZ, 1, 128), F32),
            V((2, CX, CY, 1, 1, 128), F32),
            pltpu.SemaphoreType.DMA((10,)),
            pltpu.SemaphoreType.DMA((10,)),
        ],
        compiler_params=pltpu.CompilerParams(collective_id=1, has_side_effects=True, vmem_limit_bytes=60 * 1024 * 1024),
        name="fold",
    )(grid)


def on_device(
    positions, occupancy, neighbours, edge_counts, atom_features, w_atom, w_radial, w_hidden, w_tensor, w_mix, w_out
):
    feats, prepared = halo_stage(
        occupancy.transpose(0, 2, 1),
        positions.reshape(3, CELLS, 16),
        atom_features.reshape(CELLS, 16, 128),
        neighbours.reshape(CELLS, 16, 64),
        edge_counts.reshape(CELLS, 16),
        w_atom, w_radial, w_hidden, w_tensor.T, w_mix, w_out.reshape(1, 128),
    )
    energy, forces = edge_stage(feats.reshape(GHOSTED, 16, 128), prepared, w_mix, w_hidden)
    forces = fold_stage(forces.reshape(EX, EY, EZ, 1, 128))
    return energy.reshape(CX, CY, CZ, 16), forces.reshape(3, CX, CY, CZ, 16)


def solution(mesh):
    cells = P("gx", "gy", "gz", None)
    placed = (
        P(None, "gx", "gy", "gz", None),
        P("gx", "gy", "gz"),
        P("gx", "gy", "gz", None, None),
        cells,
        P("gx", "gy", "gz", None, None),
        P(), P(), P(), P(), P(), P(),
    )
    return jax.shard_map(
        on_device,
        mesh=mesh,
        in_specs=placed,
        out_specs=(cells, P(None, "gx", "gy", "gz", None)),
        check_vma=False,
    )
```

```python
import numpy as np
import jax
import jax.numpy as jnp
from jax import lax
from jax.experimental import pallas as pl
from jax.experimental.pallas import tpu as pltpu
from jax.sharding import PartitionSpec as P

F32 = jnp.float32
BF = jnp.bfloat16
I32 = jnp.int32
root_three = 1.7320508075688772
L = 256
G = 12
TAIL = 4
CX, CY, CZ = 4, 4, 2
EX, EY, EZ = CX + 2, CY + 2, CZ + 2
CELLS = CX * CY * CZ
GHOSTED = EX * EY * EZ
MAXGR = -(-CELLS * (1024 // L) // G)
MAXCH = MAXGR * G
LISTED = 256


def nn(a, b):
    return lax.dot_general(a, b, (((1,), (0,)), ((), ())), preferred_element_type=F32)


def nt(a, b):
    return lax.dot_general(a, b, (((1,), (1,)), ((), ())), preferred_element_type=F32)


def tn(a, b):
    return lax.dot_general(a, b, (((0,), (0,)), ((), ())), preferred_element_type=F32)


def iota(shape, dim, dtype=I32):
    return lax.broadcasted_iota(I32, shape, dim).astype(dtype)


def onoff(mask):
    return jnp.where(mask, 1.0, 0.0).astype(F32)


def eye(n, m):
    return onoff(iota((n, m), 0) == iota((n, m), 1)).astype(BF)


def place_of(c):
    return c // (CY * CZ), c // CZ % CY, c % CZ


def ext_at(x, y, z):
    return (x * EY + y) * EZ + z


def prepare_weights(w_atom, w_rad, w_hid, w_ten_t, w_mix, w_out, mats, wout_r, wout_b):
    ident = eye(128, 128)
    half = 0.5
    mats[0] = (half * w_atom[...].astype(F32)).astype(BF)
    mats[1] = (half * nt(ident, w_hid[...])).astype(BF)
    mats[2] = (half * nt(ident, w_mix[0:128, :])).astype(BF)
    rad = jnp.concatenate([jnp.zeros((48, 128), F32), w_rad[...].astype(F32), jnp.zeros((72, 128), F32)], axis=0)
    mats[3] = (half * rad).astype(BF)
    wout_r[...] = w_out[...] * jnp.ones((8, 128), F32)
    wout_b[...] = jnp.sum(
        jnp.where(iota((128, 128), 0) == iota((128, 128), 1), w_out[...], 0.0), axis=1, keepdims=True
    ) * jnp.ones((128, 128), F32)
    tail = w_mix[128:224, :]
    for l in range(3):
        sel = onoff(iota((96, 32), 0) == 3 * iota((96, 32), 1) + l).astype(BF)
        spread = nt(ident, nn(sel, w_ten_t[...]).astype(BF)).astype(BF)
        mats[4 + l] = (0.0625 * nn(spread, tail)).astype(BF)


def prepare_edges(rows, rows2, occ_sp, neigh, counts, rank_out, code_out, rt_out, list_out):
    for x in range(EX):
        for y in range(EY):
            for z in range(EZ):
                at = ext_at(x, y, z)
                rows2[at : at + 1, :] = rows[x, y, z]
    occ_sp[...] = nn(rows2[...].astype(BF), onoff(iota((128, 128), 0) == 48).astype(BF))
    counts_t = nt(eye(16, 16), counts[...].astype(F32).astype(BF))
    lane64 = iota((8, 128), 1)
    low = lane64 < 64
    k_of = jnp.where(low, lane64, lane64 - 64).astype(F32)
    s_of = jnp.where(low, iota((8, 128), 0), iota((8, 128), 0) + 8)
    s_f = s_of.astype(F32)
    masks = []
    for c in range(CELLS):
        x, y, z = place_of(c)
        nb = jnp.concatenate([neigh[c, 0:8, :], neigh[c, 8:16, :]], axis=1)
        code_out[c] = nb
        cnt = jnp.where(low, counts_t[0:8, c : c + 1], counts_t[8:16, c : c + 1])
        code = lax.shift_right_logical(nb, 4)
        slot = lax.bitwise_and(nb, 15).astype(F32)
        occ_n = jnp.zeros((8, 128), F32)
        for k in range(27):
            at = ext_at(x + k // 9, y + k // 3 % 3, z + k % 3)
            occ_n = jnp.where(code == k, occ_sp[at : at + 1, :], occ_n)
        at = ext_at(x + 1, y + 1, z + 1)
        live = (k_of < cnt) & (slot < occ_n) & (s_f < occ_sp[at : at + 1, :]) & (nb != 208 + s_of)
        masks.append(onoff(live))
    mask = jnp.concatenate(masks, axis=0)
    mask_b = mask.astype(BF)
    upto = nn(mask_b, onoff(iota((128, 128), 0) <= iota((128, 128), 1)).astype(BF))
    total = nn(mask_b, jnp.ones((128, 128), BF))
    ri, ci = iota((256, 256), 0), iota((256, 256), 1)
    before = onoff((lax.shift_right_logical(ri, 3) == lax.shift_right_logical(ci, 3)) & (ci < ri)).astype(BF)
    base = nn(before, total.astype(BF))
    rank_out[...] = jnp.where(mask > 0.5, upto - 1.0 + base, -1.0).astype(I32).reshape(CELLS, 8, 128)
    n = (base + total).reshape(CELLS, 8, 128)[:, 7, :].astype(I32)
    chunks = lax.shift_right_logical(n + (L - 1), L.bit_length() - 1).astype(F32)
    ends = nn(onoff(iota((CELLS, CELLS), 1) <= iota((CELLS, CELLS), 0)).astype(BF), chunks.astype(BF))
    ends = jnp.concatenate([ends] * (LISTED // 128), axis=1)
    t = iota((CELLS, LISTED), 1, F32)
    done = ends <= t
    cell = jnp.minimum(jnp.sum(onoff(done), axis=0, keepdims=True), CELLS - 1.0)
    start = jnp.max(jnp.where(done, ends, 0.0), axis=0, keepdims=True)
    all_of = ends[CELLS - 1 : CELLS]
    first = jnp.where(t[0:1] < all_of, (t[0:1] - start) * L, 4096.0)
    list_out[...] = jnp.concatenate([cell, first, all_of, jnp.zeros((5, LISTED), F32)], axis=0).astype(I32)

    lane = iota((32, 128), 1)
    code_i = iota((32, 128), 0)
    ca = code_i // 9
    cb = code_i // 3 - 3 * ca
    cc = code_i - 3 * (code_i // 3)
    coord = lax.shift_right_logical(lane, 4)
    step = jnp.where(coord == 0, ca, jnp.where(coord == 1, cb, jnp.where(coord == 2, cc, 1))) - 1
    shift = 5.0 * step.astype(F32)
    pick = eye(48, 128)
    for c in range(CELLS):
        x, y, z = place_of(c)
        parts = []
        for k in range(0, 27, 3):
            at = ext_at(x + k // 9, y + k // 3 % 3, z)
            parts.append(rows2[at : at + 3, :])
        parts.append(jnp.zeros((5, 128), F32))
        r27 = jnp.concatenate(parts, axis=0) + shift
        hi = r27.astype(BF)
        rest = r27 - hi.astype(F32)
        mid = rest.astype(BF)
        lo = (rest - mid.astype(F32)).astype(BF)
        cat = jnp.concatenate([hi, mid, lo, jnp.zeros((32, 128), BF)], axis=0)
        rt_out[c] = nt(pick, cat).astype(BF)


def silu_both(h):
    t = jnp.tanh(h)
    y = (h + h * t).astype(BF)
    t = t.astype(BF)
    return y, (1.0 + t) + y * (1.0 - t)


def wide16(v):
    return jnp.broadcast_to(v, (16, 128)).astype(BF)


def rows16(v):
    return jnp.broadcast_to(v, (16, v.shape[1])).astype(BF)


def weave(tasks):
    active = list(tasks)
    while active:
        active = [task for task in active if next(task, None) is not None]


RX, RY, RZ, LIVE, CODE, SLOT, WHO, WEIGHT, EPS = range(9)


def edge_kernel(
    list_s, feats, rank_r, code_r, rt_r, mats, wout_r, wout_b, w_mix, w_hid, fold_h,
    energy_out, force_out,
    proj_sc, q_sc, m_sc, dq_sc, f_sc, en_sc, sec_sc, d1_sc, d2_sc, g_sc, ys_sc, geo_sc, y_sc, red_sc, gr_sc,
    fold, fold_sem,
):
    fold_copy = pltpu.make_async_copy(fold_h, fold, fold_sem)
    fold_copy.start()
    groups = lax.div(list_s[2, 0] + (G - 1 - TAIL), G)
    short = lax.min(lax.max(list_s[2, 0] - groups * G, 0), 1)
    ident = eye(128, 128)
    q_sc[...] = jnp.zeros_like(q_sc)
    f_sc[...] = jnp.zeros_like(f_sc)
    en_sc[...] = jnp.zeros_like(en_sc)
    sub16 = iota((16, L), 0, F32)
    proj_sc[...] = nn(feats[...].reshape(GHOSTED * 16, 128), mats[0]).astype(BF).reshape(GHOSTED, 16, 128)
    zero = jnp.zeros((16, L), BF)
    centres = 0.5 + 2.0 * iota((8, L), 0, F32)

    def ids_of(gi, count):
        ids = [gi * G + i for i in range(count)]
        return ids, [list_s[0, i] for i in ids]

    def run(step):
        def whole(gi, _):
            step(gi, G)
            return 0

        def rest(_, none):
            step(groups, TAIL)
            return 0

        lax.fori_loop(0, groups, whole, 0)
        lax.fori_loop(0, short, rest, 0)

    def sphere(gi):
        rx, ry, rz = geo_sc[gi, RX], geo_sc[gi, RY], geo_sc[gi, RZ]
        d2 = rx * rx + ry * ry + rz * rz + 0.01
        inv = lax.rsqrt(d2)
        return rx, ry, rz, d2, inv, d2 * inv, rx * inv, ry * inv, rz * inv

    def front(gi, count):
        ids, cells = ids_of(gi, count)
        sixteen = iota((16, 128), 0, F32).astype(BF)
        lane_l = iota((16, L), 1)
        unfold = onoff(lax.bitwise_and(lane_l, 15) == iota((16, L), 0)).astype(BF)
        in_high = lax.shift_right_logical(lane_l, 4) == iota((16, L), 0)
        lane8 = iota((8, 128), 1)
        s_of = jnp.where(lane8 < 64, iota((8, 128), 0), iota((8, 128), 0) + 8)
        ones = jnp.ones((16, 128), BF)
        zeros = jnp.zeros((16, 128), BF)

        def find(j, i, c):
            rk = rank_r[c] - list_s[1, i]
            inside = (rk >= 0) & (rk < L)
            high = jnp.where(inside, lax.shift_right_logical(rk, 4), -1).astype(F32)
            deep = lax.bitwise_and(rk, 15).astype(F32)
            nb = code_r[c]
            code_f = (lax.shift_right_logical(nb, 4) + 1).astype(F32)
            pair_f = (lax.bitwise_and(nb, 15) + 16 * s_of).astype(F32)
            left, right = [], []
            for k in range(8):
                at_high = jnp.where(sixteen == wide16(high[k : k + 1]), ones, zeros)
                left.append(
                    jnp.concatenate([at_high * wide16(code_f[k : k + 1]), at_high * wide16(pair_f[k : k + 1])], axis=0)
                )
                right.append(jnp.where(sixteen == wide16(deep[k : k + 1]), ones, zeros))
            packed = nt(jnp.concatenate(left, axis=1), jnp.concatenate(right, axis=1))
            yield 1
            spread = nn(packed.astype(BF), unfold)
            yield 1
            code1, pair = [
                jnp.sum(jnp.where(in_high, spread[16 * a : 16 * a + 16], 0.0), axis=0, keepdims=True) for a in range(2)
            ]
            live = jnp.minimum(code1, 1.0)
            code = code1 - live
            s = jnp.floor(pair * 0.0625)
            slot = pair - 16.0 * s
            oh27 = onoff(code == iota((32, L), 0, F32)).astype(BF)
            rt = rt_r[c]
            got = nn(rt, jnp.concatenate([oh27, oh27, oh27, jnp.zeros((32, L), BF)], axis=0))
            for q, v in ((LIVE, live), (CODE, code), (SLOT, slot), (WHO, s)):
                geo_sc[gi, q, j : j + 1, :] = v
            yield 1
            m_slot = slot == sub16
            m_s = s == sub16
            rtf = rt.astype(F32)
            centre = rtf[:, 13:14] + (rtf[:, 45:46] + rtf[:, 77:78])
            for d in range(3):
                sl = slice(16 * d, 16 * d + 16)
                geo_sc[gi, d, j : j + 1, :] = jnp.sum(
                    jnp.where(m_slot, got[sl], 0.0) - jnp.where(m_s, centre[sl], 0.0), axis=0, keepdims=True
                )

        weave(find(j, i, c) for j, (i, c) in enumerate(zip(ids, cells)))
        rx, ry, rz, d2, inv, dist, nx, ny, nz = sphere(gi)
        u = jnp.maximum(1.0 - d2 * (1.0 / 144.0), 0.0)
        geo_sc[gi, WEIGHT] = geo_sc[gi, LIVE] * (u * u)
        y_sc[0] = dist
        y_sc[1] = nx
        y_sc[2] = ny
        y_sc[3] = nz
        y_sc[4] = root_three * nx * ny
        y_sc[5] = root_three * ny * nz
        y_sc[6] = 0.5 * (3.0 * nz * nz - 1.0)
        y_sc[7] = root_three * nx * nz
        y_sc[8] = (0.5 * root_three) * (nx * nx - ny * ny)

        def layers(j, i, c):
            x = lax.div(c, CY * CZ)
            rest = c - x * (CY * CZ)
            y = lax.div(rest, CZ)
            z = rest - y * CZ
            parts = [
                proj_sc[pl.ds(((x + k // 3) * EY + y + k % 3) * EZ + z, 3)].reshape(48, 128) for k in range(9)
            ]
            parts.append(mats[3, 48:64, :])
            tab = jnp.concatenate(parts, axis=0)
            code, slot, s = [geo_sc[gi, q, j : j + 1, :] for q in (CODE, SLOT, WHO)]
            arg = (y_sc[0, j : j + 1, :] - centres) * 0.5
            basis = jnp.exp(-(arg * arg))
            slot01 = onoff(slot == sub16).astype(BF)
            s01 = onoff(s == sub16).astype(BF)
            code16 = rows16(code)
            tiles = [jnp.where(code16 == float(k), slot01, zero) for k in range(27)]
            tiles[13] = tiles[13] + s01
            tiles.append(jnp.concatenate([basis, jnp.zeros((8, L), F32)], axis=0).astype(BF))
            pre = tn(tab, jnp.concatenate(tiles, axis=0))
            yield 1
            f, d1 = silu_both(pre)
            d1_sc[i] = d1
            hidden = nn(mats[1], f)
            yield 1
            ys = jnp.concatenate([s01] + [s01 * rows16(y_sc[m, j : j + 1, :]) for m in range(1, 9)], axis=0)
            ys_sc[i] = ys[16:144]
            sb, d2 = silu_both(hidden)
            d2_sc[i] = d2
            sec_sc[i] = sb
            w16 = rows16(geo_sc[gi, WEIGHT, j : j + 1, :])
            q = nt(ys * jnp.concatenate([w16] * 9, axis=0), sb)
            yield 1
            q_sc[:, c] = q_sc[:, c] + q.reshape(9, 16, 128)

        weave(layers(j, i, c) for j, (i, c) in enumerate(zip(ids, cells)))

    run(front)

    for m in range(9):
        l = 0 if m == 0 else 1 if m < 4 else 2
        m_sc[m] = nn(q_sc[m].reshape(CELLS * 16, 128).astype(BF), mats[4 + l]).astype(BF).reshape(CELLS, 16, 128)
        q_sc[m] = jnp.zeros((CELLS, 16, 128), F32)

    def middle(gi, count):
        ids, cells = ids_of(gi, count)
        wout_h = jnp.concatenate([(0.5 * wout_b[...]).astype(BF)] * (L // 128), axis=1)
        row = iota((16, 128), 0)
        w_hi = wout_r[0:1, :].astype(BF).astype(F32)
        w_rows = jnp.where(row == 0, w_hi, jnp.where(row == 1, wout_r[0:1, :] - w_hi, 0.0)).astype(BF)

        def mix(j, i, c):
            s01 = onoff(geo_sc[gi, WHO, j : j + 1, :] == sub16).astype(BF)
            ys = jnp.concatenate([s01, ys_sc[i]], axis=0)
            p = nn(mats[2], sec_sc[i]) + tn(m_sc[:, c].reshape(144, 128), ys)
            yield 1
            w = geo_sc[gi, WEIGHT, j : j + 1, :]
            mixed, d = silu_both(p)
            g = d * wout_h
            g_sc[i] = g
            energies = nn(w_rows, mixed)
            dm = nt(ys * jnp.concatenate([rows16(w)] * 9, axis=0), g)
            yield 1
            eps = energies[0:1] + energies[1:2]
            geo_sc[gi, EPS, j : j + 1, :] = eps
            we = eps * w
            hi = we.astype(BF).astype(F32)
            en = nt(jnp.where(iota((16, L), 0) == 0, hi, jnp.where(iota((16, L), 0) == 1, we - hi, 0.0)).astype(BF), ys[0:16])
            q_sc[:, c] = q_sc[:, c] + dm.reshape(9, 16, 128)
            yield 1
            en_sc[c] = en_sc[c] + en[0:8]

        weave(mix(j, i, c) for j, (i, c) in enumerate(zip(ids, cells)))

    run(middle)

    for m in range(9):
        l = 0 if m == 0 else 1 if m < 4 else 2
        dq_sc[m] = nt(q_sc[m].reshape(CELLS * 16, 128).astype(BF), mats[4 + l]).astype(BF).reshape(CELLS, 16, 128)

    def back(gi, count):
        ids, cells = ids_of(gi, count)
        top = jnp.concatenate([w_mix[0:128, :], jnp.zeros((128, 128), BF)], axis=1)
        col, row = iota((16, 256), 1), iota((16, 256), 0)
        part = jnp.where(col < 128, 0, lax.shift_right_logical(col - 128, 4) + 1)
        gather = onoff(part == row).astype(BF)
        rx, ry, rz, d2, inv, dist, nx, ny, nz = sphere(gi)
        y_sc[0] = dist

        def undo(j, i, c):
            dq = dq_sc[:, c].reshape(144, 128)
            s01 = onoff(geo_sc[gi, WHO, j : j + 1, :] == sub16).astype(BF)
            t = tn(dq, jnp.concatenate([s01, ys_sc[i]], axis=0))
            sb = sec_sc[i]
            low = jnp.concatenate([m_sc[1:9, c].reshape(128, 128), dq[16:144]], axis=1)
            both = nn(jnp.concatenate([top, low], axis=0), jnp.concatenate([g_sc[i], sb], axis=0))
            yield 1
            t2 = t + t
            dsec = both[0:128] + t2
            dfirst = nn(w_hid[...], dsec.astype(BF) * d2_sc[i])
            sums = nn(
                gather,
                jnp.concatenate([t2.astype(BF) * sb, both[128:256].astype(BF) * jnp.concatenate([s01] * 8, axis=0)], axis=0),
            )
            yield 1
            for m in range(9):
                red_sc[m, j : j + 1, :] = sums[m : m + 1]
            dbasis = nn(mats[3, 48:64, :], dfirst.astype(BF) * d1_sc[i])[0:8]
            yield 1
            arg = (y_sc[0, j : j + 1, :] - centres) * 0.5
            red_sc[9, j : j + 1, :] = jnp.sum(dbasis * jnp.exp(-(arg * arg)) * arg, axis=0, keepdims=True)

        weave(undo(j, i, c) for j, (i, c) in enumerate(zip(ids, cells)))
        w = geo_sc[gi, WEIGHT]
        w2 = w + w
        dw = geo_sc[gi, EPS] + red_sc[0]
        y1, y2, y3, y4, y5, y6, y7, y8 = [red_sc[m] * w2 for m in range(1, 9)]
        ax = y1 + root_three * (ny * y4 + nz * y7 + nx * y8)
        ay = y2 + root_three * (nx * y4 + nz * y5 - ny * y8)
        az = y3 + root_three * (ny * y5 + nx * y7) + 3.0 * nz * y6
        dd = red_sc[9] * (-0.5 * w) - (ax * nx + ay * ny + az * nz) * inv
        u = jnp.maximum(1.0 - d2 * (1.0 / 144.0), 0.0)
        radial = dd * inv + dw * geo_sc[gi, LIVE] * u * (-4.0 / 144.0)
        gr_sc[0] = ax * inv + rx * radial
        gr_sc[1] = ay * inv + ry * radial
        gr_sc[2] = az * inv + rz * radial
        where32 = iota((32, L), 0, F32)

        def scatter(j, i, c):
            code, slot, s = [geo_sc[gi, q, j : j + 1, :] for q in (CODE, SLOT, WHO)]
            slot01 = onoff(slot == sub16).astype(BF)
            s01 = onoff(s == sub16).astype(BF)
            g16 = [rows16(gr_sc[d, j : j + 1, :]) for d in range(3)]
            parts = [slot01 * -v for v in g16] + [zero] + [s01 * v for v in g16] + [zero]
            oh = onoff((code == where32) | (where32 == 27.0)).astype(BF)
            add = nt(oh, jnp.concatenate(parts, axis=0))
            yield 1
            f_sc[c] = f_sc[c] + add

        weave(scatter(j, i, c) for j, (i, c) in enumerate(zip(ids, cells)))

    run(back)

    fold_copy.wait()

    def halves(v):
        hi = v.astype(BF)
        return jnp.concatenate([hi, (v - hi.astype(F32)).astype(BF)], axis=1)

    width = CELLS * 32
    sums = nn(fold[:, 0:width], halves(f_sc[:, :, 0:64].reshape(width, 64)))
    sums = sums + nn(fold[:, width : width + CELLS], halves(f_sc[:, 27, 64:128]))
    force_out[...] = jnp.concatenate([sums[:, 0:64] + sums[:, 64:128], jnp.zeros((GHOSTED, 64), F32)], axis=1)
    energy_out[...] = en_sc[:, 0, :] + en_sc[:, 1, :]


def fold_matrix():
    width = CELLS * 32
    m = np.zeros((GHOSTED, width + 128), np.float32)
    for c in range(CELLS):
        x, y, z = place_of(c)
        for k in range(27):
            m[ext_at(x + k // 9, y + k // 3 % 3, z + k % 3), c * 32 + k] = 1
        m[ext_at(x + 1, y + 1, z + 1), width + c] = 1
    return m


PREPARED = (
    jax.ShapeDtypeStruct((CELLS, 8, 128), I32),
    jax.ShapeDtypeStruct((CELLS, 8, 128), I32),
    jax.ShapeDtypeStruct((CELLS, 48, 128), BF),
    jax.ShapeDtypeStruct((8, LISTED), I32),
    jax.ShapeDtypeStruct((7, 128, 128), BF),
    jax.ShapeDtypeStruct((8, 128), F32),
    jax.ShapeDtypeStruct((128, 128), F32),
)


def edge_stage(feats, prepared, w_mix, w_hid):
    rank, code, rt, todo, mats, wout_r, wout_b = prepared
    V = pltpu.VMEM
    vm = pl.BlockSpec(memory_space=pltpu.VMEM)
    return pl.pallas_call(
        edge_kernel,
        out_shape=(jax.ShapeDtypeStruct((CELLS, 16), F32), jax.ShapeDtypeStruct((GHOSTED, 128), F32)),
        in_specs=[pl.BlockSpec(memory_space=pltpu.SMEM)] + [vm] * 9 + [pl.BlockSpec(memory_space=pl.ANY)],
        out_specs=(vm, vm),
        scratch_shapes=[
            V((GHOSTED, 16, 128), BF),
            V((9, CELLS, 16, 128), F32),
            V((9, CELLS, 16, 128), BF),
            V((9, CELLS, 16, 128), BF),
            V((CELLS, 32, 128), F32),
            V((CELLS, 8, 16), F32),
            V((MAXCH, 128, L), BF),
            V((MAXCH, 128, L), BF),
            V((MAXCH, 128, L), BF),
            V((MAXCH, 128, L), BF),
            V((MAXCH, 128, L), BF),
            V((MAXGR, 9, G, L), F32),
            V((9, G, L), F32),
            V((10, G, L), F32),
            V((3, G, L), F32),
            V((GHOSTED, CELLS * 32 + 128), BF),
            pltpu.SemaphoreType.DMA,
        ],
        compiler_params=pltpu.CompilerParams(vmem_limit_bytes=60 * 1024 * 1024),
        name="edges",
    )(todo, feats, rank, code, rt, mats, wout_r, wout_b, w_mix, w_hid, jnp.asarray(fold_matrix(), BF))


MESH = pl.DeviceIdType.MESH
STEPS = (0, -1, 1)
AROUND = tuple((dx, dy, dz) for dx in STEPS for dy in STEPS for dz in STEPS)[1:]
RING = tuple(v for v in AROUND if v[2] == 0)
BOTH = ((0, 0, -1), (0, 0, 1))


def neighbourhood():
    axes = []
    for axis in ("gx", "gy", "gz"):
        size, me = lax.axis_size(axis), lax.axis_index(axis)
        axes.append({0: me, -1: lax.rem(me + (size - 1), size), 1: lax.rem(me + 1, size)})
    return lambda dx, dy, dz: {"gx": axes[0][dx], "gy": axes[1][dy], "gz": axes[2][dz]}


def greet(peer, others):
    barrier = pltpu.get_barrier_semaphore()
    for dx, dy, dz in others:
        pl.semaphore_signal(barrier, inc=1, device_id=peer(dx, dy, dz), device_id_type=MESH)
    return barrier


def sent(src, dst, send, recv, there):
    copy = pltpu.make_async_remote_copy(
        src_ref=src, dst_ref=dst, send_sem=send, recv_sem=recv, device_id=there, device_id_type=MESH
    )
    copy.start()
    return copy


def border(step, n):
    return pl.ds(1, n) if step == 0 else pl.ds(1 if step < 0 else n, 1)


def ghost(step, n):
    return pl.ds(1, n) if step == 0 else pl.ds(n + 1 if step < 0 else 0, 1)


def halo_kernel(
    occ_s, pos, feat, counts, w_out, neigh_h, w_atom_h, w_rad_h, w_hid_h, w_ten_h, w_mix_h,
    feat_ext, rank_h, code_h, rt_h, todo_h, mats_h, wout_r_h, wout_b_h,
    w_atom, w_rad, w_hid, w_ten_t, w_mix, neigh, rank, code, rt, todo, mats, wout_r, wout_b,
    rows, rows2, occ_sp, send, recv, inward, outward,
):
    peer = neighbourhood()
    barrier = greet(peer, AROUND)
    fetched = [
        pltpu.make_async_copy(far, near, inward.at[j])
        for j, (far, near) in enumerate(
            zip((w_atom_h, w_rad_h, w_hid_h, w_ten_h, w_mix_h, neigh_h), (w_atom, w_rad, w_hid, w_ten_t, w_mix, neigh))
        )
    ]
    for copy in fetched:
        copy.start()
    table = jnp.concatenate([pos[0], pos[1], pos[2], jnp.zeros((CELLS, 80), F32)], axis=1)
    lane = iota((1, 128), 1)
    for c in range(CELLS):
        x, y, z = place_of(c)
        rows[x + 1, y + 1, z + 1] = jnp.where(lane < 48, table[c : c + 1], occ_s[x, z, y].astype(F32))
        feat_ext[x + 1, y + 1, z + 1] = feat[c]
    pl.semaphore_wait(barrier, len(AROUND))

    def around(array, base):
        copies = []
        for j, (dx, dy, dz) in enumerate(AROUND):
            src = array.at[border(dx, CX), border(dy, CY), border(dz, CZ)]
            dst = array.at[ghost(dx, CX), ghost(dy, CY), ghost(dz, CZ)]
            copies.append(sent(src, dst, send.at[base + j], recv.at[base + j], peer(dx, dy, dz)))
        return copies

    row_copies = around(rows, 0)
    feat_copies = around(feat_ext, len(AROUND))
    for copy in fetched:
        copy.wait()
    prepare_weights(w_atom, w_rad, w_hid, w_ten_t, w_mix, w_out, mats, wout_r, wout_b)
    for copy in row_copies:
        copy.wait()
    prepare_edges(rows, rows2, occ_sp, neigh, counts, rank, code, rt, todo)
    stored = [
        pltpu.make_async_copy(near, far, outward.at[j])
        for j, (near, far) in enumerate(
            zip(
                (rank, code, rt, todo, mats, wout_r, wout_b),
                (rank_h, code_h, rt_h, todo_h, mats_h, wout_r_h, wout_b_h),
            )
        )
    ]
    for copy in stored:
        copy.start()
    for copy in feat_copies:
        copy.wait()
    for copy in stored:
        copy.wait()


def halo_stage(occ, pos, feat, neigh, counts, w_atom, w_rad, w_hid, w_ten_t, w_mix, w_out):
    vm = pl.BlockSpec(memory_space=pltpu.VMEM)
    V = pltpu.VMEM
    far = pl.BlockSpec(memory_space=pl.ANY)
    moved = (w_atom, w_rad, w_hid, w_ten_t, w_mix, neigh)
    out = pl.pallas_call(
        halo_kernel,
        out_shape=(jax.ShapeDtypeStruct((EX, EY, EZ, 16, 128), BF),) + PREPARED,
        in_specs=[pl.BlockSpec(memory_space=pltpu.SMEM)] + [vm] * 4 + [far] * 6,
        out_specs=(vm,) + (far,) * 7,
        scratch_shapes=[V(a.shape, a.dtype) for a in moved]
        + [V(a.shape, a.dtype) for a in PREPARED]
        + [
            V((EX, EY, EZ, 1, 128), F32),
            V((GHOSTED, 128), F32),
            V((GHOSTED, 128), F32),
            pltpu.SemaphoreType.DMA((2 * len(AROUND),)),
            pltpu.SemaphoreType.DMA((2 * len(AROUND),)),
            pltpu.SemaphoreType.DMA((6,)),
            pltpu.SemaphoreType.DMA((7,)),
        ],
        compiler_params=pltpu.CompilerParams(
            collective_id=0, has_side_effects=True, vmem_limit_bytes=60 * 1024 * 1024
        ),
        name="halo",
    )(occ, pos, feat, counts, w_out, neigh, w_atom, w_rad, w_hid, w_ten_t, w_mix)
    return out[0], out[1:]


def fold_kernel(grid, out, acc, got_x, got_y, got_xy, got_z, send, recv):
    peer = neighbourhood()
    barrier = greet(peer, RING + BOTH)
    acc[...] = grid[...]
    pl.semaphore_wait(barrier, len(RING + BOTH))
    copies = []
    for j, (dx, dy, _) in enumerate(RING):
        if dx and dy:
            got = got_xy.at[(dx + 1) + (dy + 1) // 2]
        elif dx:
            got = got_x.at[(dx + 1) // 2]
        else:
            got = got_y.at[(dy + 1) // 2]
        rim = (
            pl.ds(1, CX) if dx == 0 else pl.ds(0 if dx < 0 else CX + 1, 1),
            pl.ds(1, CY) if dy == 0 else pl.ds(0 if dy < 0 else CY + 1, 1),
        )
        copies.append((sent(acc.at[rim], got, send.at[j], recv.at[j], peer(dx, dy, 0)), got, dx, dy))
    for copy, got, dx, dy in copies:
        copy.wait()
        at = (border(-dx, CX), border(-dy, CY))
        acc[at] = acc[at] + got[...]
    inner = (pl.ds(1, CX), pl.ds(1, CY))
    copies = []
    for j, (step, rim) in enumerate(((-1, 0), (1, CZ + 1))):
        copies.append(
            sent(acc.at[inner + (pl.ds(rim, 1),)], got_z.at[j], send.at[8 + j], recv.at[8 + j], peer(0, 0, step))
        )
    for j, step in enumerate((-1, 1)):
        copies[j].wait()
        at = inner + (border(-step, CZ),)
        acc[at] = acc[at] + got_z[j]
    lines = []
    for c in range(CELLS):
        x, y, z = place_of(c)
        lines.append(acc[x + 1, y + 1, z + 1])
    lines = jnp.concatenate(lines, axis=0)
    for d in range(3):
        out[d] = lines[:, 16 * d : 16 * d + 16]


def fold_stage(grid):
    vm = pl.BlockSpec(memory_space=pltpu.VMEM)
    V = pltpu.VMEM
    return pl.pallas_call(
        fold_kernel,
        out_shape=jax.ShapeDtypeStruct((3, CELLS, 16), F32),
        in_specs=[vm],
        out_specs=vm,
        scratch_shapes=[
            V((EX, EY, EZ, 1, 128), F32),
            V((2, 1, CY, EZ, 1, 128), F32),
            V((2, CX, 1, EZ, 1, 128), F32),
            V((4, 1, 1, EZ, 1, 128), F32),
            V((2, CX, CY, 1, 1, 128), F32),
            pltpu.SemaphoreType.DMA((10,)),
            pltpu.SemaphoreType.DMA((10,)),
        ],
        compiler_params=pltpu.CompilerParams(collective_id=1, has_side_effects=True, vmem_limit_bytes=60 * 1024 * 1024),
        name="fold",
    )(grid)


def on_device(
    positions, occupancy, neighbours, edge_counts, atom_features, w_atom, w_radial, w_hidden, w_tensor, w_mix, w_out
):
    feats, prepared = halo_stage(
        occupancy.transpose(0, 2, 1),
        positions.reshape(3, CELLS, 16),
        atom_features.reshape(CELLS, 16, 128),
        neighbours.reshape(CELLS, 16, 64),
        edge_counts.reshape(CELLS, 16),
        w_atom, w_radial, w_hidden, w_tensor.T, w_mix, w_out.reshape(1, 128),
    )
    energy, forces = edge_stage(feats.reshape(GHOSTED, 16, 128), prepared, w_mix, w_hidden)
    forces = fold_stage(forces.reshape(EX, EY, EZ, 1, 128))
    return energy.reshape(CX, CY, CZ, 16), forces.reshape(3, CX, CY, CZ, 16)


def solution(mesh):
    cells = P("gx", "gy", "gz", None)
    placed = (
        P(None, "gx", "gy", "gz", None),
        P("gx", "gy", "gz"),
        P("gx", "gy", "gz", None, None),
        cells,
        P("gx", "gy", "gz", None, None),
        P(), P(), P(), P(), P(), P(),
    )
    return jax.shard_map(
        on_device,
        mesh=mesh,
        in_specs=placed,
        out_specs=(cells, P(None, "gx", "gy", "gz", None)),
        check_vma=False,
    )
```

```python
import numpy as np
import jax
import jax.numpy as jnp
from jax import lax
from jax.experimental import pallas as pl
from jax.experimental.pallas import tpu as pltpu
from jax.sharding import PartitionSpec as P

F32 = jnp.float32
BF = jnp.bfloat16
I32 = jnp.int32
root_three = 1.7320508075688772
L = 256
G = 12
TAIL = 9
CX, CY, CZ = 4, 4, 2
EX, EY, EZ = CX + 2, CY + 2, CZ + 2
CELLS = CX * CY * CZ
GHOSTED = EX * EY * EZ
MAXGR = -(-CELLS * (1024 // L) // G)
MAXCH = MAXGR * G
LISTED = 256


def nn(a, b):
    return lax.dot_general(a, b, (((1,), (0,)), ((), ())), preferred_element_type=F32)


def nt(a, b):
    return lax.dot_general(a, b, (((1,), (1,)), ((), ())), preferred_element_type=F32)


def tn(a, b):
    return lax.dot_general(a, b, (((0,), (0,)), ((), ())), preferred_element_type=F32)


def iota(shape, dim, dtype=I32):
    return lax.broadcasted_iota(I32, shape, dim).astype(dtype)


def onoff(mask):
    return jnp.where(mask, 1.0, 0.0).astype(F32)


def eye(n, m):
    return onoff(iota((n, m), 0) == iota((n, m), 1)).astype(BF)


def place_of(c):
    return c // (CY * CZ), c // CZ % CY, c % CZ


def ext_at(x, y, z):
    return (x * EY + y) * EZ + z


def prepare_weights(w_atom, w_rad, w_hid, w_ten_t, w_mix, w_out, mats, wout_r, wout_b):
    ident = eye(128, 128)
    half = 0.5
    mats[0] = (half * w_atom[...].astype(F32)).astype(BF)
    mats[1] = (half * nt(ident, w_hid[...])).astype(BF)
    mats[2] = (half * nt(ident, w_mix[0:128, :])).astype(BF)
    rad = jnp.concatenate([jnp.zeros((48, 128), F32), w_rad[...].astype(F32), jnp.zeros((72, 128), F32)], axis=0)
    mats[3] = (half * rad).astype(BF)
    wout_r[...] = w_out[...] * jnp.ones((8, 128), F32)
    wout_b[...] = jnp.sum(
        jnp.where(iota((128, 128), 0) == iota((128, 128), 1), w_out[...], 0.0), axis=1, keepdims=True
    ) * jnp.ones((128, 128), F32)
    tail = w_mix[128:224, :]
    for l in range(3):
        sel = onoff(iota((96, 32), 0) == 3 * iota((96, 32), 1) + l).astype(BF)
        spread = nt(ident, nn(sel, w_ten_t[...]).astype(BF)).astype(BF)
        mats[4 + l] = (0.0625 * nn(spread, tail)).astype(BF)


def prepare_edges(rows, rows2, occ_sp, neigh, counts, rank_out, code_out, rt_out, list_out):
    for x in range(EX):
        for y in range(EY):
            for z in range(EZ):
                at = ext_at(x, y, z)
                rows2[at : at + 1, :] = rows[x, y, z]
    occ_sp[...] = nn(rows2[...].astype(BF), onoff(iota((128, 128), 0) == 48).astype(BF))
    counts_t = nt(eye(16, 16), counts[...].astype(F32).astype(BF))
    lane64 = iota((8, 128), 1)
    low = lane64 < 64
    k_of = jnp.where(low, lane64, lane64 - 64).astype(F32)
    s_of = jnp.where(low, iota((8, 128), 0), iota((8, 128), 0) + 8)
    s_f = s_of.astype(F32)
    masks = []
    for c in range(CELLS):
        x, y, z = place_of(c)
        nb = jnp.concatenate([neigh[c, 0:8, :], neigh[c, 8:16, :]], axis=1)
        code_out[c] = nb
        cnt = jnp.where(low, counts_t[0:8, c : c + 1], counts_t[8:16, c : c + 1])
        code = lax.shift_right_logical(nb, 4)
        slot = lax.bitwise_and(nb, 15).astype(F32)
        occ_n = jnp.zeros((8, 128), F32)
        for k in range(27):
            at = ext_at(x + k // 9, y + k // 3 % 3, z + k % 3)
            occ_n = jnp.where(code == k, occ_sp[at : at + 1, :], occ_n)
        at = ext_at(x + 1, y + 1, z + 1)
        live = (k_of < cnt) & (slot < occ_n) & (s_f < occ_sp[at : at + 1, :]) & (nb != 208 + s_of)
        masks.append(onoff(live))
    mask = jnp.concatenate(masks, axis=0)
    mask_b = mask.astype(BF)
    upto = nn(mask_b, onoff(iota((128, 128), 0) <= iota((128, 128), 1)).astype(BF))
    total = nn(mask_b, jnp.ones((128, 128), BF))
    ri, ci = iota((256, 256), 0), iota((256, 256), 1)
    before = onoff((lax.shift_right_logical(ri, 3) == lax.shift_right_logical(ci, 3)) & (ci < ri)).astype(BF)
    base = nn(before, total.astype(BF))
    rank_out[...] = jnp.where(mask > 0.5, upto - 1.0 + base, -1.0).astype(I32).reshape(CELLS, 8, 128)
    n = (base + total).reshape(CELLS, 8, 128)[:, 7, :].astype(I32)
    chunks = lax.shift_right_logical(n + (L - 1), L.bit_length() - 1).astype(F32)
    ends = nn(onoff(iota((CELLS, CELLS), 1) <= iota((CELLS, CELLS), 0)).astype(BF), chunks.astype(BF))
    ends = jnp.concatenate([ends] * (LISTED // 128), axis=1)
    t = iota((CELLS, LISTED), 1, F32)
    done = ends <= t
    cell = jnp.minimum(jnp.sum(onoff(done), axis=0, keepdims=True), CELLS - 1.0)
    start = jnp.max(jnp.where(done, ends, 0.0), axis=0, keepdims=True)
    all_of = ends[CELLS - 1 : CELLS]
    first = jnp.where(t[0:1] < all_of, (t[0:1] - start) * L, 4096.0)
    list_out[...] = jnp.concatenate([cell, first, all_of, jnp.zeros((5, LISTED), F32)], axis=0).astype(I32)

    lane = iota((32, 128), 1)
    code_i = iota((32, 128), 0)
    ca = code_i // 9
    cb = code_i // 3 - 3 * ca
    cc = code_i - 3 * (code_i // 3)
    coord = lax.shift_right_logical(lane, 4)
    step = jnp.where(coord == 0, ca, jnp.where(coord == 1, cb, jnp.where(coord == 2, cc, 1))) - 1
    shift = 5.0 * step.astype(F32)
    pick = eye(48, 128)
    for c in range(CELLS):
        x, y, z = place_of(c)
        parts = []
        for k in range(0, 27, 3):
            at = ext_at(x + k // 9, y + k // 3 % 3, z)
            parts.append(rows2[at : at + 3, :])
        parts.append(jnp.zeros((5, 128), F32))
        r27 = jnp.concatenate(parts, axis=0) + shift
        hi = r27.astype(BF)
        rest = r27 - hi.astype(F32)
        mid = rest.astype(BF)
        lo = (rest - mid.astype(F32)).astype(BF)
        cat = jnp.concatenate([hi, mid, lo, jnp.zeros((32, 128), BF)], axis=0)
        rt_out[c] = nt(pick, cat).astype(BF)


def silu_both(h):
    t = jnp.tanh(h)
    y = (h + h * t).astype(BF)
    t = t.astype(BF)
    return y, (1.0 + t) + y * (1.0 - t)


def wide16(v):
    return jnp.broadcast_to(v, (16, 128)).astype(BF)


def rows16(v):
    return jnp.broadcast_to(v, (16, v.shape[1])).astype(BF)


def weave(tasks):
    active = list(tasks)
    while active:
        active = [task for task in active if next(task, None) is not None]


RX, RY, RZ, LIVE, CODE, SLOT, WHO, WEIGHT, EPS = range(9)


def edge_kernel(
    list_s, feats, rank_r, code_r, rt_r, mats, wout_r, wout_b, w_mix, w_hid, fold_h,
    energy_out, force_out,
    proj_sc, q_sc, m_sc, dq_sc, f_sc, en_sc, sec_sc, d1_sc, d2_sc, g_sc, ys_sc, geo_sc, y_sc, red_sc, gr_sc,
    fold, fold_sem,
):
    fold_copy = pltpu.make_async_copy(fold_h, fold, fold_sem)
    fold_copy.start()
    groups = lax.div(list_s[2, 0] + (G - 1 - TAIL), G)
    short = lax.min(lax.max(list_s[2, 0] - groups * G, 0), 1)
    ident = eye(128, 128)
    q_sc[...] = jnp.zeros_like(q_sc)
    f_sc[...] = jnp.zeros_like(f_sc)
    en_sc[...] = jnp.zeros_like(en_sc)
    sub16 = iota((16, L), 0, F32)
    proj_sc[...] = nn(feats[...].reshape(GHOSTED * 16, 128), mats[0]).astype(BF).reshape(GHOSTED, 16, 128)
    zero = jnp.zeros((16, L), BF)
    centres = 0.5 + 2.0 * iota((8, L), 0, F32)

    def ids_of(gi, count):
        ids = [gi * G + i for i in range(count)]
        return ids, [list_s[0, i] for i in ids]

    def run(step):
        def whole(gi, _):
            step(gi, G)
            return 0

        def rest(_, none):
            step(groups, TAIL)
            return 0

        lax.fori_loop(0, groups, whole, 0)
        lax.fori_loop(0, short, rest, 0)

    def sphere(gi):
        rx, ry, rz = geo_sc[gi, RX], geo_sc[gi, RY], geo_sc[gi, RZ]
        d2 = rx * rx + ry * ry + rz * rz + 0.01
        inv = lax.rsqrt(d2)
        return rx, ry, rz, d2, inv, d2 * inv, rx * inv, ry * inv, rz * inv

    def front(gi, count):
        ids, cells = ids_of(gi, count)
        sixteen = iota((16, 128), 0, F32).astype(BF)
        lane_l = iota((16, L), 1)
        unfold = onoff(lax.bitwise_and(lane_l, 15) == iota((16, L), 0)).astype(BF)
        in_high = lax.shift_right_logical(lane_l, 4) == iota((16, L), 0)
        lane8 = iota((8, 128), 1)
        s_of = jnp.where(lane8 < 64, iota((8, 128), 0), iota((8, 128), 0) + 8)
        ones = jnp.ones((16, 128), BF)
        zeros = jnp.zeros((16, 128), BF)

        def find(j, i, c):
            rk = rank_r[c] - list_s[1, i]
            inside = (rk >= 0) & (rk < L)
            high = jnp.where(inside, lax.shift_right_logical(rk, 4), -1).astype(F32)
            deep = lax.bitwise_and(rk, 15).astype(F32)
            nb = code_r[c]
            code_f = (lax.shift_right_logical(nb, 4) + 1).astype(F32)
            pair_f = (lax.bitwise_and(nb, 15) + 16 * s_of).astype(F32)
            left, right = [], []
            for k in range(8):
                at_high = jnp.where(sixteen == wide16(high[k : k + 1]), ones, zeros)
                left.append(
                    jnp.concatenate([at_high * wide16(code_f[k : k + 1]), at_high * wide16(pair_f[k : k + 1])], axis=0)
                )
                right.append(jnp.where(sixteen == wide16(deep[k : k + 1]), ones, zeros))
            packed = nt(jnp.concatenate(left, axis=1), jnp.concatenate(right, axis=1))
            yield 1
            spread = nn(packed.astype(BF), unfold)
            yield 1
            code1, pair = [
                jnp.sum(jnp.where(in_high, spread[16 * a : 16 * a + 16], 0.0), axis=0, keepdims=True) for a in range(2)
            ]
            live = jnp.minimum(code1, 1.0)
            code = code1 - live
            s = jnp.floor(pair * 0.0625)
            slot = pair - 16.0 * s
            oh27 = onoff(code == iota((32, L), 0, F32)).astype(BF)
            rt = rt_r[c]
            got = nn(rt, jnp.concatenate([oh27, oh27, oh27, jnp.zeros((32, L), BF)], axis=0))
            for q, v in ((LIVE, live), (CODE, code), (SLOT, slot), (WHO, s)):
                geo_sc[gi, q, j : j + 1, :] = v
            yield 1
            m_slot = slot == sub16
            m_s = s == sub16
            rtf = rt.astype(F32)
            centre = rtf[:, 13:14] + (rtf[:, 45:46] + rtf[:, 77:78])
            for d in range(3):
                sl = slice(16 * d, 16 * d + 16)
                geo_sc[gi, d, j : j + 1, :] = jnp.sum(
                    jnp.where(m_slot, got[sl], 0.0) - jnp.where(m_s, centre[sl], 0.0), axis=0, keepdims=True
                )

        weave(find(j, i, c) for j, (i, c) in enumerate(zip(ids, cells)))
        rx, ry, rz, d2, inv, dist, nx, ny, nz = sphere(gi)
        u = jnp.maximum(1.0 - d2 * (1.0 / 144.0), 0.0)
        geo_sc[gi, WEIGHT] = geo_sc[gi, LIVE] * (u * u)
        y_sc[0] = dist
        y_sc[1] = nx
        y_sc[2] = ny
        y_sc[3] = nz
        y_sc[4] = root_three * nx * ny
        y_sc[5] = root_three * ny * nz
        y_sc[6] = 0.5 * (3.0 * nz * nz - 1.0)
        y_sc[7] = root_three * nx * nz
        y_sc[8] = (0.5 * root_three) * (nx * nx - ny * ny)

        def layers(j, i, c):
            x = lax.div(c, CY * CZ)
            rest = c - x * (CY * CZ)
            y = lax.div(rest, CZ)
            z = rest - y * CZ
            parts = [
                proj_sc[pl.ds(((x + k // 3) * EY + y + k % 3) * EZ + z, 3)].reshape(48, 128) for k in range(9)
            ]
            parts.append(mats[3, 48:64, :])
            tab = jnp.concatenate(parts, axis=0)
            code, slot, s = [geo_sc[gi, q, j : j + 1, :] for q in (CODE, SLOT, WHO)]
            arg = (y_sc[0, j : j + 1, :] - centres) * 0.5
            basis = jnp.exp(-(arg * arg))
            slot01 = onoff(slot == sub16).astype(BF)
            s01 = onoff(s == sub16).astype(BF)
            code16 = rows16(code)
            tiles = [jnp.where(code16 == float(k), slot01, zero) for k in range(27)]
            tiles[13] = tiles[13] + s01
            tiles.append(jnp.concatenate([basis, jnp.zeros((8, L), F32)], axis=0).astype(BF))
            pre = tn(tab, jnp.concatenate(tiles, axis=0))
            yield 1
            f, d1 = silu_both(pre)
            d1_sc[i] = d1
            hidden = nn(mats[1], f)
            yield 1
            ys = jnp.concatenate([s01] + [s01 * rows16(y_sc[m, j : j + 1, :]) for m in range(1, 9)], axis=0)
            ys_sc[i] = ys[16:144]
            sb, d2 = silu_both(hidden)
            d2_sc[i] = d2
            sec_sc[i] = sb
            w16 = rows16(geo_sc[gi, WEIGHT, j : j + 1, :])
            q = nt(ys * jnp.concatenate([w16] * 9, axis=0), sb)
            yield 1
            q_sc[:, c] = q_sc[:, c] + q.reshape(9, 16, 128)

        weave(layers(j, i, c) for j, (i, c) in enumerate(zip(ids, cells)))

    run(front)

    for m in range(9):
        l = 0 if m == 0 else 1 if m < 4 else 2
        m_sc[m] = nn(q_sc[m].reshape(CELLS * 16, 128).astype(BF), mats[4 + l]).astype(BF).reshape(CELLS, 16, 128)
        q_sc[m] = jnp.zeros((CELLS, 16, 128), F32)

    def middle(gi, count):
        ids, cells = ids_of(gi, count)
        wout_h = jnp.concatenate([(0.5 * wout_b[...]).astype(BF)] * (L // 128), axis=1)
        row = iota((16, 128), 0)
        w_hi = wout_r[0:1, :].astype(BF).astype(F32)
        w_rows = jnp.where(row == 0, w_hi, jnp.where(row == 1, wout_r[0:1, :] - w_hi, 0.0)).astype(BF)

        def mix(j, i, c):
            s01 = onoff(geo_sc[gi, WHO, j : j + 1, :] == sub16).astype(BF)
            ys = jnp.concatenate([s01, ys_sc[i]], axis=0)
            p = nn(mats[2], sec_sc[i]) + tn(m_sc[:, c].reshape(144, 128), ys)
            yield 1
            w = geo_sc[gi, WEIGHT, j : j + 1, :]
            mixed, d = silu_both(p)
            g = d * wout_h
            g_sc[i] = g
            energies = nn(w_rows, mixed)
            dm = nt(ys * jnp.concatenate([rows16(w)] * 9, axis=0), g)
            yield 1
            eps = energies[0:1] + energies[1:2]
            geo_sc[gi, EPS, j : j + 1, :] = eps
            we = eps * w
            hi = we.astype(BF).astype(F32)
            en = nt(jnp.where(iota((16, L), 0) == 0, hi, jnp.where(iota((16, L), 0) == 1, we - hi, 0.0)).astype(BF), ys[0:16])
            q_sc[:, c] = q_sc[:, c] + dm.reshape(9, 16, 128)
            yield 1
            en_sc[c] = en_sc[c] + en[0:8]

        weave(mix(j, i, c) for j, (i, c) in enumerate(zip(ids, cells)))

    run(middle)

    for m in range(9):
        l = 0 if m == 0 else 1 if m < 4 else 2
        dq_sc[m] = nt(q_sc[m].reshape(CELLS * 16, 128).astype(BF), mats[4 + l]).astype(BF).reshape(CELLS, 16, 128)

    def back(gi, count):
        ids, cells = ids_of(gi, count)
        top = jnp.concatenate([w_mix[0:128, :], jnp.zeros((128, 128), BF)], axis=1)
        col, row = iota((16, 256), 1), iota((16, 256), 0)
        part = jnp.where(col < 128, 0, lax.shift_right_logical(col - 128, 4) + 1)
        gather = onoff(part == row).astype(BF)
        rx, ry, rz, d2, inv, dist, nx, ny, nz = sphere(gi)
        y_sc[0] = dist

        def undo(j, i, c):
            dq = dq_sc[:, c].reshape(144, 128)
            s01 = onoff(geo_sc[gi, WHO, j : j + 1, :] == sub16).astype(BF)
            t = tn(dq, jnp.concatenate([s01, ys_sc[i]], axis=0))
            sb = sec_sc[i]
            low = jnp.concatenate([m_sc[1:9, c].reshape(128, 128), dq[16:144]], axis=1)
            both = nn(jnp.concatenate([top, low], axis=0), jnp.concatenate([g_sc[i], sb], axis=0))
            yield 1
            t2 = t + t
            dsec = both[0:128] + t2
            dfirst = nn(w_hid[...], dsec.astype(BF) * d2_sc[i])
            sums = nn(
                gather,
                jnp.concatenate([t2.astype(BF) * sb, both[128:256].astype(BF) * jnp.concatenate([s01] * 8, axis=0)], axis=0),
            )
            yield 1
            for m in range(9):
                red_sc[m, j : j + 1, :] = sums[m : m + 1]
            dbasis = nn(mats[3, 48:64, :], dfirst.astype(BF) * d1_sc[i])[0:8]
            yield 1
            arg = (y_sc[0, j : j + 1, :] - centres) * 0.5
            red_sc[9, j : j + 1, :] = jnp.sum(dbasis * jnp.exp(-(arg * arg)) * arg, axis=0, keepdims=True)

        weave(undo(j, i, c) for j, (i, c) in enumerate(zip(ids, cells)))
        w = geo_sc[gi, WEIGHT]
        w2 = w + w
        dw = geo_sc[gi, EPS] + red_sc[0]
        y1, y2, y3, y4, y5, y6, y7, y8 = [red_sc[m] * w2 for m in range(1, 9)]
        ax = y1 + root_three * (ny * y4 + nz * y7 + nx * y8)
        ay = y2 + root_three * (nx * y4 + nz * y5 - ny * y8)
        az = y3 + root_three * (ny * y5 + nx * y7) + 3.0 * nz * y6
        dd = red_sc[9] * (-0.5 * w) - (ax * nx + ay * ny + az * nz) * inv
        u = jnp.maximum(1.0 - d2 * (1.0 / 144.0), 0.0)
        radial = dd * inv + dw * geo_sc[gi, LIVE] * u * (-4.0 / 144.0)
        gr_sc[0] = ax * inv + rx * radial
        gr_sc[1] = ay * inv + ry * radial
        gr_sc[2] = az * inv + rz * radial
        where32 = iota((32, L), 0, F32)

        def scatter(j, i, c):
            code, slot, s = [geo_sc[gi, q, j : j + 1, :] for q in (CODE, SLOT, WHO)]
            slot01 = onoff(slot == sub16).astype(BF)
            s01 = onoff(s == sub16).astype(BF)
            g16 = [rows16(gr_sc[d, j : j + 1, :]) for d in range(3)]
            parts = [slot01 * -v for v in g16] + [zero] + [s01 * v for v in g16] + [zero]
            oh = onoff((code == where32) | (where32 == 27.0)).astype(BF)
            add = nt(oh, jnp.concatenate(parts, axis=0))
            yield 1
            f_sc[c] = f_sc[c] + add

        weave(scatter(j, i, c) for j, (i, c) in enumerate(zip(ids, cells)))

    run(back)

    fold_copy.wait()

    def halves(v):
        hi = v.astype(BF)
        return jnp.concatenate([hi, (v - hi.astype(F32)).astype(BF)], axis=1)

    width = CELLS * 32
    sums = nn(fold[:, 0:width], halves(f_sc[:, :, 0:64].reshape(width, 64)))
    sums = sums + nn(fold[:, width : width + CELLS], halves(f_sc[:, 27, 64:128]))
    force_out[...] = jnp.concatenate([sums[:, 0:64] + sums[:, 64:128], jnp.zeros((GHOSTED, 64), F32)], axis=1)
    energy_out[...] = en_sc[:, 0, :] + en_sc[:, 1, :]


def fold_matrix():
    width = CELLS * 32
    m = np.zeros((GHOSTED, width + 128), np.float32)
    for c in range(CELLS):
        x, y, z = place_of(c)
        for k in range(27):
            m[ext_at(x + k // 9, y + k // 3 % 3, z + k % 3), c * 32 + k] = 1
        m[ext_at(x + 1, y + 1, z + 1), width + c] = 1
    return m


PREPARED = (
    jax.ShapeDtypeStruct((CELLS, 8, 128), I32),
    jax.ShapeDtypeStruct((CELLS, 8, 128), I32),
    jax.ShapeDtypeStruct((CELLS, 48, 128), BF),
    jax.ShapeDtypeStruct((8, LISTED), I32),
    jax.ShapeDtypeStruct((7, 128, 128), BF),
    jax.ShapeDtypeStruct((8, 128), F32),
    jax.ShapeDtypeStruct((128, 128), F32),
)


def edge_stage(feats, prepared, w_mix, w_hid):
    rank, code, rt, todo, mats, wout_r, wout_b = prepared
    V = pltpu.VMEM
    vm = pl.BlockSpec(memory_space=pltpu.VMEM)
    return pl.pallas_call(
        edge_kernel,
        out_shape=(jax.ShapeDtypeStruct((CELLS, 16), F32), jax.ShapeDtypeStruct((GHOSTED, 128), F32)),
        in_specs=[pl.BlockSpec(memory_space=pltpu.SMEM)] + [vm] * 9 + [pl.BlockSpec(memory_space=pl.ANY)],
        out_specs=(vm, vm),
        scratch_shapes=[
            V((GHOSTED, 16, 128), BF),
            V((9, CELLS, 16, 128), F32),
            V((9, CELLS, 16, 128), BF),
            V((9, CELLS, 16, 128), BF),
            V((CELLS, 32, 128), F32),
            V((CELLS, 8, 16), F32),
            V((MAXCH, 128, L), BF),
            V((MAXCH, 128, L), BF),
            V((MAXCH, 128, L), BF),
            V((MAXCH, 128, L), BF),
            V((MAXCH, 128, L), BF),
            V((MAXGR, 9, G, L), F32),
            V((9, G, L), F32),
            V((10, G, L), F32),
            V((3, G, L), F32),
            V((GHOSTED, CELLS * 32 + 128), BF),
            pltpu.SemaphoreType.DMA,
        ],
        compiler_params=pltpu.CompilerParams(vmem_limit_bytes=60 * 1024 * 1024),
        name="edges",
    )(todo, feats, rank, code, rt, mats, wout_r, wout_b, w_mix, w_hid, jnp.asarray(fold_matrix(), BF))


MESH = pl.DeviceIdType.MESH
STEPS = (0, -1, 1)
AROUND = tuple((dx, dy, dz) for dx in STEPS for dy in STEPS for dz in STEPS)[1:]
RING = tuple(v for v in AROUND if v[2] == 0)
BOTH = ((0, 0, -1), (0, 0, 1))


def neighbourhood():
    axes = []
    for axis in ("gx", "gy", "gz"):
        size, me = lax.axis_size(axis), lax.axis_index(axis)
        axes.append({0: me, -1: lax.rem(me + (size - 1), size), 1: lax.rem(me + 1, size)})
    return lambda dx, dy, dz: {"gx": axes[0][dx], "gy": axes[1][dy], "gz": axes[2][dz]}


def greet(peer, others):
    barrier = pltpu.get_barrier_semaphore()
    for dx, dy, dz in others:
        pl.semaphore_signal(barrier, inc=1, device_id=peer(dx, dy, dz), device_id_type=MESH)
    return barrier


def sent(src, dst, send, recv, there):
    copy = pltpu.make_async_remote_copy(
        src_ref=src, dst_ref=dst, send_sem=send, recv_sem=recv, device_id=there, device_id_type=MESH
    )
    copy.start()
    return copy


def border(step, n):
    return pl.ds(1, n) if step == 0 else pl.ds(1 if step < 0 else n, 1)


def ghost(step, n):
    return pl.ds(1, n) if step == 0 else pl.ds(n + 1 if step < 0 else 0, 1)


def halo_kernel(
    occ_s, pos, feat, counts, w_out, neigh_h, w_atom_h, w_rad_h, w_hid_h, w_ten_h, w_mix_h,
    feat_ext, rank_h, code_h, rt_h, todo_h, mats_h, wout_r_h, wout_b_h,
    w_atom, w_rad, w_hid, w_ten_t, w_mix, neigh, rank, code, rt, todo, mats, wout_r, wout_b,
    rows, rows2, occ_sp, send, recv, inward, outward,
):
    peer = neighbourhood()
    barrier = greet(peer, AROUND)
    fetched = [
        pltpu.make_async_copy(far, near, inward.at[j])
        for j, (far, near) in enumerate(
            zip((w_atom_h, w_rad_h, w_hid_h, w_ten_h, w_mix_h, neigh_h), (w_atom, w_rad, w_hid, w_ten_t, w_mix, neigh))
        )
    ]
    for copy in fetched:
        copy.start()
    table = jnp.concatenate([pos[0], pos[1], pos[2], jnp.zeros((CELLS, 80), F32)], axis=1)
    lane = iota((1, 128), 1)
    for c in range(CELLS):
        x, y, z = place_of(c)
        rows[x + 1, y + 1, z + 1] = jnp.where(lane < 48, table[c : c + 1], occ_s[x, z, y].astype(F32))
        feat_ext[x + 1, y + 1, z + 1] = feat[c]
    pl.semaphore_wait(barrier, len(AROUND))

    def around(array, base):
        copies = []
        for j, (dx, dy, dz) in enumerate(AROUND):
            src = array.at[border(dx, CX), border(dy, CY), border(dz, CZ)]
            dst = array.at[ghost(dx, CX), ghost(dy, CY), ghost(dz, CZ)]
            copies.append(sent(src, dst, send.at[base + j], recv.at[base + j], peer(dx, dy, dz)))
        return copies

    row_copies = around(rows, 0)
    feat_copies = around(feat_ext, len(AROUND))
    for copy in fetched:
        copy.wait()
    prepare_weights(w_atom, w_rad, w_hid, w_ten_t, w_mix, w_out, mats, wout_r, wout_b)
    for copy in row_copies:
        copy.wait()
    prepare_edges(rows, rows2, occ_sp, neigh, counts, rank, code, rt, todo)
    stored = [
        pltpu.make_async_copy(near, far, outward.at[j])
        for j, (near, far) in enumerate(
            zip(
                (rank, code, rt, todo, mats, wout_r, wout_b),
                (rank_h, code_h, rt_h, todo_h, mats_h, wout_r_h, wout_b_h),
            )
        )
    ]
    for copy in stored:
        copy.start()
    for copy in feat_copies:
        copy.wait()
    for copy in stored:
        copy.wait()


def halo_stage(occ, pos, feat, neigh, counts, w_atom, w_rad, w_hid, w_ten_t, w_mix, w_out):
    vm = pl.BlockSpec(memory_space=pltpu.VMEM)
    V = pltpu.VMEM
    far = pl.BlockSpec(memory_space=pl.ANY)
    moved = (w_atom, w_rad, w_hid, w_ten_t, w_mix, neigh)
    out = pl.pallas_call(
        halo_kernel,
        out_shape=(jax.ShapeDtypeStruct((EX, EY, EZ, 16, 128), BF),) + PREPARED,
        in_specs=[pl.BlockSpec(memory_space=pltpu.SMEM)] + [vm] * 4 + [far] * 6,
        out_specs=(vm,) + (far,) * 7,
        scratch_shapes=[V(a.shape, a.dtype) for a in moved]
        + [V(a.shape, a.dtype) for a in PREPARED]
        + [
            V((EX, EY, EZ, 1, 128), F32),
            V((GHOSTED, 128), F32),
            V((GHOSTED, 128), F32),
            pltpu.SemaphoreType.DMA((2 * len(AROUND),)),
            pltpu.SemaphoreType.DMA((2 * len(AROUND),)),
            pltpu.SemaphoreType.DMA((6,)),
            pltpu.SemaphoreType.DMA((7,)),
        ],
        compiler_params=pltpu.CompilerParams(
            collective_id=0, has_side_effects=True, vmem_limit_bytes=60 * 1024 * 1024
        ),
        name="halo",
    )(occ, pos, feat, counts, w_out, neigh, w_atom, w_rad, w_hid, w_ten_t, w_mix)
    return out[0], out[1:]


def fold_kernel(grid, out, acc, got_x, got_y, got_xy, got_z, send, recv):
    peer = neighbourhood()
    barrier = greet(peer, RING + BOTH)
    acc[...] = grid[...]
    pl.semaphore_wait(barrier, len(RING + BOTH))
    copies = []
    for j, (dx, dy, _) in enumerate(RING):
        if dx and dy:
            got = got_xy.at[(dx + 1) + (dy + 1) // 2]
        elif dx:
            got = got_x.at[(dx + 1) // 2]
        else:
            got = got_y.at[(dy + 1) // 2]
        rim = (
            pl.ds(1, CX) if dx == 0 else pl.ds(0 if dx < 0 else CX + 1, 1),
            pl.ds(1, CY) if dy == 0 else pl.ds(0 if dy < 0 else CY + 1, 1),
        )
        copies.append((sent(acc.at[rim], got, send.at[j], recv.at[j], peer(dx, dy, 0)), got, dx, dy))
    for copy, got, dx, dy in copies:
        copy.wait()
        at = (border(-dx, CX), border(-dy, CY))
        acc[at] = acc[at] + got[...]
    inner = (pl.ds(1, CX), pl.ds(1, CY))
    copies = []
    for j, (step, rim) in enumerate(((-1, 0), (1, CZ + 1))):
        copies.append(
            sent(acc.at[inner + (pl.ds(rim, 1),)], got_z.at[j], send.at[8 + j], recv.at[8 + j], peer(0, 0, step))
        )
    for j, step in enumerate((-1, 1)):
        copies[j].wait()
        at = inner + (border(-step, CZ),)
        acc[at] = acc[at] + got_z[j]
    lines = []
    for c in range(CELLS):
        x, y, z = place_of(c)
        lines.append(acc[x + 1, y + 1, z + 1])
    lines = jnp.concatenate(lines, axis=0)
    for d in range(3):
        out[d] = lines[:, 16 * d : 16 * d + 16]


def fold_stage(grid):
    vm = pl.BlockSpec(memory_space=pltpu.VMEM)
    V = pltpu.VMEM
    return pl.pallas_call(
        fold_kernel,
        out_shape=jax.ShapeDtypeStruct((3, CELLS, 16), F32),
        in_specs=[vm],
        out_specs=vm,
        scratch_shapes=[
            V((EX, EY, EZ, 1, 128), F32),
            V((2, 1, CY, EZ, 1, 128), F32),
            V((2, CX, 1, EZ, 1, 128), F32),
            V((4, 1, 1, EZ, 1, 128), F32),
            V((2, CX, CY, 1, 1, 128), F32),
            pltpu.SemaphoreType.DMA((10,)),
            pltpu.SemaphoreType.DMA((10,)),
        ],
        compiler_params=pltpu.CompilerParams(collective_id=1, has_side_effects=True, vmem_limit_bytes=60 * 1024 * 1024),
        name="fold",
    )(grid)


def on_device(
    positions, occupancy, neighbours, edge_counts, atom_features, w_atom, w_radial, w_hidden, w_tensor, w_mix, w_out
):
    feats, prepared = halo_stage(
        occupancy.transpose(0, 2, 1),
        positions.reshape(3, CELLS, 16),
        atom_features.reshape(CELLS, 16, 128),
        neighbours.reshape(CELLS, 16, 64),
        edge_counts.reshape(CELLS, 16),
        w_atom, w_radial, w_hidden, w_tensor.T, w_mix, w_out.reshape(1, 128),
    )
    energy, forces = edge_stage(feats.reshape(GHOSTED, 16, 128), prepared, w_mix, w_hidden)
    forces = fold_stage(forces.reshape(EX, EY, EZ, 1, 128))
    return energy.reshape(CX, CY, CZ, 16), forces.reshape(3, CX, CY, CZ, 16)


def solution(mesh):
    cells = P("gx", "gy", "gz", None)
    placed = (
        P(None, "gx", "gy", "gz", None),
        P("gx", "gy", "gz"),
        P("gx", "gy", "gz", None, None),
        cells,
        P("gx", "gy", "gz", None, None),
        P(), P(), P(), P(), P(), P(),
    )
    return jax.shard_map(
        on_device,
        mesh=mesh,
        in_specs=placed,
        out_specs=(cells, P(None, "gx", "gy", "gz", None)),
        check_vma=False,
    )
```
